32 devices in a mesh: dp: 4 (over z), expert: 2 (over y), ctx: 4 (over x, core).
Axes of the slice: x: 2, y: 2, z: 4, core: 2. Of those that a mesh axis runs over, the one named last changes fastest.
Arguments:
- tokens: bfloat16 [8192, 1536], P(('dp', 'expert', 'ctx')), may hold values from -6 to 6
- cotangent: bfloat16 [8192, 1536], P(('dp', 'expert', 'ctx')), may hold values from -6 to 6
- routes: int32 [8192, 8], P(('dp', 'expert', 'ctx')), may hold values from 0 to 39, all different within a row; in each aligned block of 256 rows (0 to 255, 256 to 511, ...) at most 64 rows name the same one
- positions: int32 [8192], P(('dp', 'expert', 'ctx')), may hold values from 0 to 2046, as said below
- gain_attend: bfloat16 [1536], P(('dp', 'expert', 'ctx')), may hold values from 0.5 to 1.5
- gain_attend_mean: float32 [1536], P(('dp', 'expert', 'ctx'))
- gain_attend_square: float32 [1536], P(('dp', 'expert', 'ctx'))
- project_in: bfloat16 [1536, 2560], P(('dp', 'expert', 'ctx')), may hold values from -0.625 to 0.625
- project_in_mean: float32 [1536, 2560], P(('dp', 'expert', 'ctx'))
- project_in_square: float32 [1536, 2560], P(('dp', 'expert', 'ctx'))
- project_out: bfloat16 [1536, 1536], P(('dp', 'expert', 'ctx')), may hold values from -0.5 to 0.5
- project_out_mean: float32 [1536, 1536], P(('dp', 'expert', 'ctx'))
- project_out_square: float32 [1536, 1536], P(('dp', 'expert', 'ctx'))
- gain_expert: bfloat16 [1536], P(('dp', 'expert', 'ctx')), may hold values from 0.5 to 1.5
- gain_expert_mean: float32 [1536], P(('dp', 'expert', 'ctx'))
- gain_expert_square: float32 [1536], P(('dp', 'expert', 'ctx'))
- router_weight: bfloat16 [1536, 40], P(('dp', 'expert', 'ctx')), may hold values from -0.078125 to 0.078125
- router_weight_mean: float32 [1536, 40], P(('dp', 'expert', 'ctx'))
- router_weight_square: float32 [1536, 40], P(('dp', 'expert', 'ctx'))
- expert_in: bfloat16 [40, 1536, 1024], P('expert', ('dp', 'ctx')), may hold values from -0.15625 to 0.15625
- expert_in_mean: float32 [40, 1536, 1024], P('expert', ('dp', 'ctx'))
- expert_in_square: float32 [40, 1536, 1024], P('expert', ('dp', 'ctx'))
- expert_out: bfloat16 [40, 512, 1536], P('expert', ('dp', 'ctx')), may hold values from -1.5 to 1.5
- expert_out_mean: float32 [40, 512, 1536], P('expert', ('dp', 'ctx'))
- expert_out_square: float32 [40, 512, 1536], P('expert', ('dp', 'ctx'))
Outputs:
- block_output: bfloat16 [8192, 1536], P(('dp', 'expert', 'ctx'))
- input_grad: float32 [8192, 1536], P(('dp', 'expert', 'ctx'))
- gain_attend_grad: float32 [1536], P(('dp', 'expert', 'ctx'))
- gain_attend_mean_out: float32 [1536], P(('dp', 'expert', 'ctx'))
- gain_attend_square_out: float32 [1536], P(('dp', 'expert', 'ctx'))
- gain_attend_new: float32 [1536], P(('dp', 'expert', 'ctx'))
- project_in_grad: float32 [1536, 2560], P(('dp', 'expert', 'ctx'))
- project_in_mean_out: float32 [1536, 2560], P(('dp', 'expert', 'ctx'))
- project_in_square_out: float32 [1536, 2560], P(('dp', 'expert', 'ctx'))
- project_in_new: float32 [1536, 2560], P(('dp', 'expert', 'ctx'))
- project_out_grad: float32 [1536, 1536], P(('dp', 'expert', 'ctx'))
- project_out_mean_out: float32 [1536, 1536], P(('dp', 'expert', 'ctx'))
- project_out_square_out: float32 [1536, 1536], P(('dp', 'expert', 'ctx'))
- project_out_new: float32 [1536, 1536], P(('dp', 'expert', 'ctx'))
- gain_expert_grad: float32 [1536], P(('dp', 'expert', 'ctx'))
- gain_expert_mean_out: float32 [1536], P(('dp', 'expert', 'ctx'))
- gain_expert_square_out: float32 [1536], P(('dp', 'expert', 'ctx'))
- gain_expert_new: float32 [1536], P(('dp', 'expert', 'ctx'))
- router_weight_grad: float32 [1536, 40], P(('dp', 'expert', 'ctx'))
- router_weight_mean_out: float32 [1536, 40], P(('dp', 'expert', 'ctx'))
- router_weight_square_out: float32 [1536, 40], P(('dp', 'expert', 'ctx'))
- router_weight_new: float32 [1536, 40], P(('dp', 'expert', 'ctx'))
- expert_in_grad: float32 [40, 1536, 1024], P('expert', ('dp', 'ctx'))
- expert_in_mean_out: float32 [40, 1536, 1024], P('expert', ('dp', 'ctx'))
- expert_in_square_out: float32 [40, 1536, 1024], P('expert', ('dp', 'ctx'))
- expert_in_new: float32 [40, 1536, 1024], P('expert', ('dp', 'ctx'))
- expert_out_grad: float32 [40, 512, 1536], P('expert', ('dp', 'ctx'))
- expert_out_mean_out: float32 [40, 512, 1536], P('expert', ('dp', 'ctx'))
- expert_out_square_out: float32 [40, 512, 1536], P('expert', ('dp', 'ctx'))
- expert_out_new: float32 [40, 512, 1536], P('expert', ('dp', 'ctx'))
The draws below stay inside these ranges and needn't reach their ends.
Inputs may be any that keep to these rules, and one draw needn't show every extreme that they name: `routes`: each row names 8 different experts; in each device's 256 rows no expert is named by more than 64 rows. Within each sequence positions start at 0 and rise by 1 or 2 from one token to the next.
All inputs are finite; a program needn't handle non-finite values.
Results may differ from the reference program's by a relative error of at most 0.019.
Values may be sent and summed in bfloat16 or wider, within the bound.
A program may use at most 384 MiB of HBM per device.

```python
import math
import jax
import jax.numpy as jnp
import numpy as np
from jax import lax

D = 1536
H = 24
KV = 8
HD = 64
FFE = 512
EXPERTS = 40
TOP = 8
TOK_DEV = 256
STEP = 8
CAP = 64
SEQ_LEN = 1024
TOKENS = 8192
QKV = 2560


def draw_positions(key, part):
    steps = jax.random.randint(key, (TOKENS // SEQ_LEN, SEQ_LEN), 1, 3)
    steps = steps.at[0].set(2)
    rising = jnp.cumsum(steps, axis=1) - steps[:, :1]
    return rising.reshape(TOKENS).astype(jnp.int32)


def grad_sizes():
    routed = math.sqrt(TOKENS * TOP / EXPERTS)
    spread = math.sqrt(TOKENS)
    gated = 0.22 / TOP
    produced = 0.5 * math.sqrt(FFE) / math.sqrt(FFE // 32)
    grad_gate_up = 0.5 * gated * math.sqrt(D) / math.sqrt(FFE // 32)
    return {'gain_attend': 0.4 * math.sqrt(QKV) * math.sqrt(16.0 / D) * spread, 'project_in': 0.4 * spread, 'project_out': 0.11 * spread, 'gain_expert': math.sqrt(TOP) * grad_gate_up * math.sqrt(2.0 * FFE / D) * spread, 'router_weight': 0.22 * math.sqrt(D) * produced / TOP * routed, 'expert_in': grad_gate_up * routed, 'expert_out': 0.5 * gated * routed}


def first_moment(key, shape, name):
    size = grad_sizes()[name]
    noise = jax.random.normal(jax.random.fold_in(key, 11), shape, jnp.float32)
    return 0.11 * size * noise


def second_moment(key, shape, name):
    size = grad_sizes()[name]
    factor = jnp.exp(jax.random.uniform(jax.random.fold_in(key, 23), shape, jnp.float32, -math.log(2.0), math.log(2.0)))
    return 0.105 * size * size * factor


def draw_gain_attend_mean(key, part):
    return first_moment(key, (D,), 'gain_attend')


def draw_gain_attend_square(key, part):
    return second_moment(key, (D,), 'gain_attend')


def draw_project_in_mean(key, part):
    return first_moment(key, (D, QKV), 'project_in')


def draw_project_in_square(key, part):
    return second_moment(key, (D, QKV), 'project_in')


def draw_project_out_mean(key, part):
    return first_moment(key, (H * HD, D), 'project_out')


def draw_project_out_square(key, part):
    return second_moment(key, (H * HD, D), 'project_out')


def draw_gain_expert_mean(key, part):
    return first_moment(key, (D,), 'gain_expert')


def draw_gain_expert_square(key, part):
    return second_moment(key, (D,), 'gain_expert')


def draw_router_weight_mean(key, part):
    return first_moment(key, (D, EXPERTS), 'router_weight')


def draw_router_weight_square(key, part):
    return second_moment(key, (D, EXPERTS), 'router_weight')


def draw_expert_in_mean(key, part):
    return first_moment(key, (EXPERTS, D, 2 * FFE), 'expert_in')


def draw_expert_in_square(key, part):
    return second_moment(key, (EXPERTS, D, 2 * FFE), 'expert_in')


def draw_expert_out_mean(key, part):
    return first_moment(key, (EXPERTS, FFE, D), 'expert_out')


def draw_expert_out_square(key, part):
    return second_moment(key, (EXPERTS, FFE, D), 'expert_out')


def block_levels(own_key, shape, pieces, smallest, high):
    def one(dim, parts):
        steps = jax.random.uniform(jax.random.fold_in(jax.random.fold_in(own_key, 6), dim), (parts,), jnp.float32, smallest / len(pieces), high / len(pieces))
        return jnp.repeat(jnp.exp(steps), shape[dim] // parts).reshape((-1,) + (1,) * (len(shape) - dim - 1))

    level = one(*pieces[0])
    for cut in pieces[1:]:
        level = level * one(*cut)
    return level


def routed_block(own_key, own, number, rows, number_of, top, most, slope):
    order = jax.random.permutation(own_key, number_of)
    crowded, ordinary = shares(number_of, rows * top, most, slope, True), shares(number_of, rows * top, most, slope, False)
    places = jnp.arange(number_of)

    def named(lengths, offset_by):
        used = int((lengths > 0).sum())
        fixed = max(1, used // 4)
        shifted = fixed + (places - fixed + offset_by * (used - fixed)) % max(1, number_of - fixed)
        return jnp.zeros((number_of,), jnp.int32).at[order[jnp.where(places < fixed, places, shifted)]].set(jnp.asarray(lengths, jnp.int32))

    lengths = jnp.where(number % 4 == 0, named(crowded, number // 4), named(ordinary, number - number // 4 - 1))
    mixed = jax.random.permutation(jax.random.fold_in(own, 3), number_of)
    source_of, receiver = mixed[0:number_of // 2 * 2:2], mixed[1:number_of // 2 * 2:2]
    margin = jnp.minimum(lengths[source_of] - 1, most - lengths[receiver]) // 2
    margin = jnp.where((source_of == order[0]) | (receiver == order[0]) | (lengths[receiver] == 0), 0, jnp.maximum(margin, 0))
    shifted = jax.random.randint(jax.random.fold_in(own, 4), (number_of // 2,), 0, 1 << 20) % (margin + 1)
    lengths = lengths.at[source_of].add(-shifted).at[receiver].add(shifted)
    labels = jnp.searchsorted(jnp.cumsum(lengths), jnp.arange(rows * top), side="right").astype(jnp.int32)
    listing = labels.reshape(top, rows).T
    listing = listing[jax.random.permutation(jax.random.fold_in(own, 1), rows)]
    offset_by = jax.random.randint(jax.random.fold_in(own, 2), (rows, 1), 0, top)
    return jnp.take_along_axis(listing, (jnp.arange(top)[None, :] + offset_by) % top, axis=1)


def shares(number_of, total, reach, lean, full):
    loads = [(1 << 20) // math.isqrt(grade ** lean) + 1 for grade in range(1, number_of + 1)]
    largest = reach if full else min(reach, max(-(-total // number_of), total * loads[0] // sum(loads)))
    least = 1 if total - largest >= number_of - 1 else 0
    counts, spare = [largest] + [least] * (number_of - 1), total - largest - least * (number_of - 1)
    while spare > 0:
        candidates = [i for i in range(1, number_of) if counts[i] < largest] or [i for i in range(1, number_of) if counts[i] < reach]
        mass, left = sum([loads[i] for i in candidates]), spare
        for i in candidates:
            extra = min(reach - counts[i], max(1, left * loads[i] // mass), spare)
            counts[i] = counts[i] + extra
            spare = spare - extra
    return np.array(counts)


def centred(rng, dims, scale, bound, shards=(), kind=jnp.bfloat16):
    level = block_levels(rng, dims, shards, -0.22, 0.18) if shards else 1.0
    entries = jax.random.normal(rng, dims, jnp.float32) * scale * level
    return jnp.minimum(jnp.maximum(entries, -bound), bound).astype(kind)


def setup_inputs(seed: int = 0) -> dict:
    arg_keys = jax.random.split(jax.random.key(seed), 26)
    tokens = centred(arg_keys[0], (TOKENS, D), 1.0, 6.0, ((0, 32),))
    cotangent = centred(arg_keys[1], (TOKENS, D), 1.0, 6.0, ((0, 32),))
    routes_keys = jax.random.split(jax.random.fold_in(arg_keys[2], 1), TOKENS // TOK_DEV)
    routes_turns = jax.random.permutation(jax.random.fold_in(arg_keys[2], 3), TOKENS // TOK_DEV)
    routes = jax.vmap(lambda own, number: routed_block(jax.random.fold_in(arg_keys[2], 2), own, number, TOK_DEV, EXPERTS, TOP, CAP, 1))(routes_keys, routes_turns).reshape((TOKENS, TOP))
    positions = draw_positions(jax.random.fold_in(arg_keys[25], 71), 0)
    gain_attend = jnp.clip(1.0 + 0.1 * jax.random.normal(arg_keys[4], (D,), jnp.float32), 0.5, 1.5).astype(jnp.bfloat16)
    gain_attend_mean = draw_gain_attend_mean(jax.random.fold_in(arg_keys[25], 71), 0)
    gain_attend_square = draw_gain_attend_square(jax.random.fold_in(arg_keys[25], 71), 0)
    project_in = centred(arg_keys[7], (D, QKV), (D // 16) ** -0.5, 0.625, ((0, 32),))
    project_in_mean = draw_project_in_mean(jax.random.fold_in(arg_keys[25], 71), 0)
    project_in_square = draw_project_in_square(jax.random.fold_in(arg_keys[25], 71), 0)
    project_out = centred(arg_keys[10], (H * HD, D), (D // 12) ** -0.5, 0.5, ((0, 32),))
    project_out_mean = draw_project_out_mean(jax.random.fold_in(arg_keys[25], 71), 0)
    project_out_square = draw_project_out_square(jax.random.fold_in(arg_keys[25], 71), 0)
    gain_expert = jnp.clip(1.0 + 0.1 * jax.random.normal(arg_keys[13], (D,), jnp.float32), 0.5, 1.5).astype(jnp.bfloat16)
    gain_expert_mean = draw_gain_expert_mean(jax.random.fold_in(arg_keys[25], 71), 0)
    gain_expert_square = draw_gain_expert_square(jax.random.fold_in(arg_keys[25], 71), 0)
    router_weight = centred(arg_keys[16], (D, EXPERTS), (4 * D) ** -0.5, 0.078125, ((0, 32),))
    router_weight_mean = draw_router_weight_mean(jax.random.fold_in(arg_keys[25], 71), 0)
    router_weight_square = draw_router_weight_square(jax.random.fold_in(arg_keys[25], 71), 0)
    expert_in = centred(arg_keys[19], (EXPERTS, D, 2 * FFE), D ** -0.5, 0.15625, ((0, 2), (1, 16)))
    expert_in_mean = draw_expert_in_mean(jax.random.fold_in(arg_keys[25], 71), 0)
    expert_in_square = draw_expert_in_square(jax.random.fold_in(arg_keys[25], 71), 0)
    expert_out = centred(arg_keys[22], (EXPERTS, FFE, D), (FFE // 32) ** -0.5, 1.5, ((0, 2), (1, 16)))
    expert_out_mean = draw_expert_out_mean(jax.random.fold_in(arg_keys[25], 71), 0)
    expert_out_square = draw_expert_out_square(jax.random.fold_in(arg_keys[25], 71), 0)
    return dict(tokens=tokens, cotangent=cotangent, routes=routes, positions=positions, gain_attend=gain_attend, gain_attend_mean=gain_attend_mean, gain_attend_square=gain_attend_square, project_in=project_in, project_in_mean=project_in_mean, project_in_square=project_in_square, project_out=project_out, project_out_mean=project_out_mean, project_out_square=project_out_square, gain_expert=gain_expert, gain_expert_mean=gain_expert_mean, gain_expert_square=gain_expert_square, router_weight=router_weight, router_weight_mean=router_weight_mean, router_weight_square=router_weight_square, expert_in=expert_in, expert_in_mean=expert_in_mean, expert_in_square=expert_in_square, expert_out=expert_out, expert_out_mean=expert_out_mean, expert_out_square=expert_out_square)


EPS_NORM = 1e-06
ATTN_SCALE = 0.015625
RESIDUAL_SCALE = 0.22
BETA_ONE = 0.9
BETA_TWO = 0.95
ADAM_EPS = 1e-08
DECAY_RATE = 0.1
ROPE_BASE = 10000.0

@jax.custom_vjp
def low(v):
    return lax.optimization_barrier(v.astype(jnp.bfloat16)).astype(jnp.float32)

@jax.custom_vjp
def low_back(v):
    return v

def low_keep(v):
    return (low(v), None)

def low_pass(kept, grad):
    return (grad,)

def back_keep(v):
    return (v, None)

def back_low(kept, grad):
    return (low(grad),)
low.defvjp(low_keep, low_pass)
low_back.defvjp(back_keep, back_low)

def product(left, right):
    return jnp.dot(left, right, precision=lax.Precision.HIGHEST, preferred_element_type=jnp.float32)

def normalize(rows):
    factor = lax.rsqrt(lax.optimization_barrier(jnp.mean(rows * rows, axis=-1, keepdims=True)) + EPS_NORM)
    return rows * factor

def rope_tables(positions):
    half = HD // 2
    freqs = ROPE_BASE ** (-jnp.arange(half, dtype=jnp.float32) * 2.0 / HD)
    angles = positions.astype(jnp.float32)[:, None] * freqs[None, :]
    cosine = jnp.cos(angles)
    sine = jnp.sin(angles)
    return (jnp.concatenate([cosine, cosine], 1), jnp.concatenate([sine, sine], 1))

def rotate(values, cosine, sine):
    half = values.shape[-1] // 2
    turned = jnp.concatenate([-values[..., half:], values[..., :half]], -1)
    return values * cosine[:, None, :] + turned * sine[:, None, :]

def forward(weight_list, hidden_in, seq_positions, seq_routes):
    gain_attend, project_in, project_out, gain_expert, router_weight, expert_in, expert_out = weight_list
    length = hidden_in.shape[0]
    query_width = H * HD
    key_width = KV * HD
    attend_in = low(normalize(hidden_in) * gain_attend)
    mixed = low_back(product(attend_in, project_in))
    cosine, sine = rope_tables(seq_positions)
    query = low(rotate(mixed[:, :query_width].reshape(length, H, HD), cosine, sine))
    keys = low(rotate(mixed[:, query_width:query_width + key_width].reshape(length, KV, HD), cosine, sine))
    values = low(mixed[:, query_width + key_width:].reshape(length, KV, HD))
    keys_heads = jnp.repeat(keys, H // KV, axis=1)
    values_heads = jnp.repeat(values, H // KV, axis=1)
    block = min(512, length)
    count = length // block
    key_index = jnp.arange(length, dtype=jnp.int32)

    def attend_block(index):
        start = (index * block).astype(jnp.int32)
        rows = lax.dynamic_slice_in_dim(query, start, block, 0)
        scores = jnp.einsum('qhd,khd->hqk', rows, keys_heads, precision=lax.Precision.HIGHEST) * ATTN_SCALE
        scores = low_back(scores)
        query_index = start + jnp.arange(block, dtype=jnp.int32)
        allowed = key_index[None, :] <= query_index[:, None]
        scores = jnp.where(allowed[None], scores, -1e+30)
        peak = lax.optimization_barrier(jnp.max(scores, axis=-1, keepdims=True))
        raised = jnp.exp(scores - peak)
        probs = raised / lax.optimization_barrier(jnp.sum(raised, axis=-1, keepdims=True))
        return jnp.einsum('hqk,khd->qhd', low(probs), values_heads, precision=lax.Precision.HIGHEST)
    outputs = lax.map(jax.checkpoint(attend_block), jnp.arange(count, dtype=jnp.int32))
    attended = low(low_back(outputs.reshape(length, query_width)))
    branch = low_back(product(attended, project_out))
    after = hidden_in + RESIDUAL_SCALE * branch
    expert_input = low(normalize(after) * gain_expert)
    logits = low_back(product(expert_input, router_weight))
    picked = jnp.take_along_axis(logits, seq_routes, axis=1)
    top_logit = lax.optimization_barrier(jnp.max(picked, axis=-1, keepdims=True))
    raised_gates = jnp.exp(picked - top_logit)
    gates = raised_gates / lax.optimization_barrier(jnp.sum(raised_gates, axis=-1, keepdims=True))
    chosen = seq_routes[:, :, None] == jnp.arange(EXPERTS, dtype=jnp.int32)[None, None, :]
    mixing = lax.optimization_barrier(jnp.sum(jnp.where(chosen, gates[:, :, None], 0.0), axis=1))

    def expert_step(total, operands):
        weight_in, weight_out, share = operands
        rows = low_back(expert_input)
        gate_up = low_back(product(rows, weight_in))
        gate_half = gate_up[:, :FFE]
        middle = low(gate_half * jax.nn.sigmoid(gate_half) * gate_up[:, FFE:])
        produced = low(low_back(product(middle, weight_out)))
        return (total + share[:, None] * produced, None)
    moe, unused = lax.scan(jax.checkpoint(expert_step), jnp.zeros_like(hidden_in), (expert_in, expert_out, mixing.T))
    return after + RESIDUAL_SCALE * moe

def add_trees(left, right):
    return jax.tree.map(jnp.add, left, right)

def learn_rates():
    return (0.3, 3.0 / (D // 16) ** 0.5, 3.0 / (D // 12) ** 0.5, 0.3, 3.0 / (4 * D) ** 0.5, 3.0 / D ** 0.5, 3.0 / (FFE // 32) ** 0.5)

def adam_step(weight, first, second, grad, decay, rate):
    new_first = BETA_ONE * first + (1.0 - BETA_ONE) * grad
    new_second = BETA_TWO * second + (1.0 - BETA_TWO) * grad * grad
    corrected = new_first / (1.0 - BETA_ONE ** STEP) / (jnp.sqrt(new_second / (1.0 - BETA_TWO ** STEP)) + ADAM_EPS)
    old = weight.astype(jnp.float32)
    return (grad, new_first, new_second, old - rate * (corrected + decay * old))

def reference(tokens, cotangent, routes, positions, gain_attend, gain_attend_mean, gain_attend_square, project_in, project_in_mean, project_in_square, project_out, project_out_mean, project_out_square, gain_expert, gain_expert_mean, gain_expert_square, router_weight, router_weight_mean, router_weight_square, expert_in, expert_in_mean, expert_in_square, expert_out, expert_out_mean, expert_out_square):
    raw = (gain_attend, project_in, project_out, gain_expert, router_weight, expert_in, expert_out)
    weight_list = tuple((item.astype(jnp.float32) for item in raw))
    count = TOKENS // SEQ_LEN
    inputs = (tokens.astype(jnp.float32).reshape(count, SEQ_LEN, D), cotangent.astype(jnp.float32).reshape(count, SEQ_LEN, D), positions.reshape(count, SEQ_LEN), routes.reshape(count, SEQ_LEN, TOP))

    def one_sequence(totals, operands):
        hidden_in, grad_out, seq_positions, seq_routes = operands

        def apply(weights_now, rows):
            return forward(weights_now, rows, seq_positions, seq_routes)
        result, pullback = jax.vjp(apply, weight_list, hidden_in)
        grad_weights, grad_rows = pullback(grad_out)
        return (add_trees(totals, grad_weights), (result.astype(jnp.bfloat16), grad_rows))
    zeros = jax.tree.map(jnp.zeros_like, weight_list)
    grads, (outputs, grads_in) = lax.scan(one_sequence, zeros, inputs)
    firsts = (gain_attend_mean, project_in_mean, project_out_mean, gain_expert_mean, router_weight_mean, expert_in_mean, expert_out_mean)
    seconds = (gain_attend_square, project_in_square, project_out_square, gain_expert_square, router_weight_square, expert_in_square, expert_out_square)
    decays = (0.0, DECAY_RATE, DECAY_RATE, 0.0, DECAY_RATE, DECAY_RATE, DECAY_RATE)
    rates = learn_rates()
    results = [outputs.reshape(TOKENS, D), grads_in.reshape(TOKENS, D)]
    for index in range(7):
        results.extend(adam_step(raw[index], firsts[index], seconds[index], grads[index], decays[index], rates[index]))
    return tuple(results)
```

```python
import jax
import jax.numpy as jnp
from jax import lax
from jax.experimental import pallas as pl
from jax.experimental.pallas import tpu as pltpu
from jax.sharding import PartitionSpec as P

D = 1536
H = 24
KV = 8
HD = 64
FFE = 512
EXPERTS = 40
TOP = 8
STEP = 8
CAP = 64


EPS_NORM = 1e-06
ATTN_SCALE = 0.015625
RESIDUAL_SCALE = 0.22
BETA_ONE = 0.9
BETA_TWO = 0.95
ADAM_EPS = 1e-08
DECAY_RATE = 0.1
ROPE_BASE = 10000.0


def normalize(rows):
    factor = lax.rsqrt(jnp.mean(rows * rows, axis=-1, keepdims=True) + EPS_NORM)
    return (rows * factor, factor)


def norm_back(grad_normed, normed, factor):
    return factor * (grad_normed - normed * jnp.mean(grad_normed * normed, axis=-1, keepdims=True))


def learn_rates():
    return (
        0.3,
        3.0 / (D // 16) ** 0.5,
        3.0 / (D // 12) ** 0.5,
        0.3,
        3.0 / (4 * D) ** 0.5,
        3.0 / D**0.5,
        3.0 / (FFE // 32) ** 0.5,
    )


def adam_step(weight, first, second, grad, decay, rate):
    new_first = BETA_ONE * first + (1.0 - BETA_ONE) * grad
    new_second = BETA_TWO * second + (1.0 - BETA_TWO) * grad * grad
    corrected = (
        new_first
        / (1.0 - BETA_ONE**STEP)
        / (jnp.sqrt(new_second / (1.0 - BETA_TWO**STEP)) + ADAM_EPS)
    )
    old = weight.astype(jnp.float32)
    return (grad, new_first, new_second, old - rate * (corrected + decay * old))


def lane_tables(table):
    half = HD // 2
    source = lax.broadcasted_iota(jnp.int32, (128, 128), 0)
    target = lax.broadcasted_iota(jnp.int32, (128, 128), 1)
    same = (source % half) == (target % half)
    group = source // half
    first = (target % HD) < half
    cosine = jnp.where(same & (group < 2), 1.0, 0.0).astype(jnp.bfloat16)
    ahead = jnp.where(same & (group >= 2) & first, -1.0, 0.0).astype(jnp.bfloat16)
    behind = jnp.where(same & (group >= 2) & jnp.logical_not(first), 1.0, 0.0).astype(jnp.bfloat16)
    return tuple(
        jnp.dot(table, item, preferred_element_type=jnp.float32)
        for item in (cosine, ahead, behind)
    )


def turn_lanes(block, tables, sign):
    cosine, ahead, behind = tables
    half = HD // 2
    turned = pltpu.roll(block, 128 - half, 1) * ahead + pltpu.roll(block, half, 1) * behind
    return block * cosine + sign * turned


def scores_of(keys, query, start, length):
    scores = (
        lax.dot_general(
            keys, query, (((1,), (1,)), ((), ())), preferred_element_type=jnp.float32
        )
        * ATTN_SCALE
    )
    rows = lax.broadcasted_iota(jnp.int32, scores.shape, 0)
    columns = lax.broadcasted_iota(jnp.int32, scores.shape, 1) + start
    return jnp.where(rows <= columns, scores, -1e30)


def project_rows(rows_ref, weight, normed_ref, query_ref, keys_ref, values_ref, flipped):
    blocks, block = rows_ref.shape[:2]
    heads, groups = query_ref.shape[0], keys_ref.shape[0]
    wide = heads * HD
    for index in range(blocks):
        span = pl.ds(index * block, block)
        rows = rows_ref[index, :, :D].astype(jnp.float32)
        factor = lax.rsqrt(jnp.mean(rows * rows, axis=-1, keepdims=True) + EPS_NORM)
        normed = (rows * factor).astype(jnp.bfloat16)
        normed_ref[span, :] = normed
        tables = lane_tables(rows_ref[index, :, D : D + 128])
        mixed = jnp.dot(normed, weight, preferred_element_type=jnp.float32)
        for column in range(0, wide + 2 * groups * HD, 128):
            part = mixed[:, column : column + 128]
            if column < wide + groups * HD:
                part = turn_lanes(part, tables, 1.0)
            else:
                flipped[column - wide - groups * HD : column - wide - groups * HD + 128, span] = (
                    part.T.astype(jnp.bfloat16)
                )
            part = part.astype(jnp.bfloat16)
            for half in range(2):
                head = column // HD + half
                piece = part[:, half * HD : (half + 1) * HD]
                if head < heads:
                    query_ref[head, span, :] = piece
                elif head < heads + groups:
                    keys_ref[head - heads, span, :] = piece
                else:
                    values_ref[head - heads - groups, span, :] = piece


def attend_rows(index, block, query_ref, keys_ref, out_ref, flipped):
    heads, groups = query_ref.shape[0], keys_ref.shape[0]
    length = (index + 1) * block
    span = pl.ds(index * block, block)
    outputs = []
    for head in range(heads):
        group = head // (heads // groups)
        scores = scores_of(
            keys_ref[group, :length, :], query_ref[head, span, :], index * block, length
        )
        peak = jnp.max(scores, axis=0, keepdims=True)
        raised = jnp.exp(scores - peak)
        total = jnp.sum(raised, axis=0, keepdims=True)
        probs = (raised * (1.0 / total)).astype(jnp.bfloat16)
        outputs.append(
            jnp.dot(
                flipped[group * HD : (group + 1) * HD, :length],
                probs,
                preferred_element_type=jnp.float32,
            )
        )
    out_ref[index] = jnp.concatenate(outputs, 0).T.astype(jnp.bfloat16)


def attend_kernel(rows_ref, weight_ref, normed_ref, query_ref, keys_ref, values_ref, out_ref, flipped):
    project_rows(rows_ref, weight_ref[...], normed_ref, query_ref, keys_ref, values_ref, flipped)
    for index in range(rows_ref.shape[0]):
        attend_rows(index, rows_ref.shape[1], query_ref, keys_ref, out_ref, flipped)


def attend_shapes(rows, heads, groups):
    blocks, block = rows[:2]
    length = blocks * block
    return (
        jax.ShapeDtypeStruct((length, D), jnp.bfloat16),
        jax.ShapeDtypeStruct((heads, length, HD), jnp.bfloat16),
        jax.ShapeDtypeStruct((groups, length, HD), jnp.bfloat16),
        jax.ShapeDtypeStruct((groups, length, HD), jnp.bfloat16),
        jax.ShapeDtypeStruct((blocks, block, heads * HD), jnp.bfloat16),
    )


def attend_back_kernel(rows_ref, query_ref, keys_ref, values_ref, grad_ref, out_ref, flipped, grad_keys, grad_values):
    block = 256
    blocks = rows_ref.shape[0] // block
    heads, groups = query_ref.shape[0], keys_ref.shape[0]
    repeat = heads // groups
    wide = heads * HD
    for group in range(groups):
        flipped[group * HD : (group + 1) * HD, :] = (
            keys_ref[group].astype(jnp.float32).T.astype(jnp.bfloat16)
        )
    grad_keys[...] = jnp.zeros_like(grad_keys)
    grad_values[...] = jnp.zeros_like(grad_values)
    for index in range(blocks):
        length = (index + 1) * block
        span = pl.ds(index * block, block)
        outputs = []
        for head in range(heads):
            group = head // repeat
            query = query_ref[head, span, :]
            grad = grad_ref[span, head * HD : (head + 1) * HD]
            scores = scores_of(keys_ref[group, :length, :], query, index * block, length)
            peak = jnp.max(scores, axis=0, keepdims=True)
            raised = jnp.exp(scores - peak)
            total = jnp.sum(raised, axis=0, keepdims=True)
            probs = raised * (1.0 / total)
            grad_probs = lax.dot_general(
                values_ref[group, :length, :],
                grad,
                (((1,), (1,)), ((), ())),
                preferred_element_type=jnp.float32,
            )
            middle = jnp.sum(probs * grad_probs, axis=0, keepdims=True)
            grad_scores = (probs * (grad_probs - middle)).astype(jnp.bfloat16)
            grad_keys[group, :length, :] += jnp.dot(
                grad_scores, query, preferred_element_type=jnp.float32
            )
            grad_values[group, :length, :] += jnp.dot(
                probs.astype(jnp.bfloat16), grad, preferred_element_type=jnp.float32
            )
            outputs.append(
                jnp.dot(
                    flipped[group * HD : (group + 1) * HD, :length],
                    grad_scores,
                    preferred_element_type=jnp.float32,
                )
            )
        tables = lane_tables(rows_ref[span, :])
        stacked = jnp.concatenate(outputs, 0).T * ATTN_SCALE
        for column in range(0, wide, 128):
            out_ref[span, column : column + 128] = turn_lanes(
                stacked[:, column : column + 128], tables, -1.0
            ).astype(jnp.bfloat16)
    for index in range(blocks):
        span = pl.ds(index * block, block)
        tables = lane_tables(rows_ref[span, :])
        keys = jnp.concatenate([grad_keys[group, span, :] for group in range(groups)], 1)
        values = jnp.concatenate([grad_values[group, span, :] for group in range(groups)], 1)
        keys = turn_lanes(keys * ATTN_SCALE, tables, -1.0)
        out_ref[span, wide : wide + groups * HD] = keys.astype(jnp.bfloat16)
        out_ref[span, wide + groups * HD :] = values.astype(jnp.bfloat16)


def attend_forward(rows, weight, heads, groups):
    return pl.pallas_call(
        attend_kernel,
        out_shape=attend_shapes(rows.shape, heads, groups),
        scratch_shapes=[pltpu.VMEM((groups * HD, rows.shape[0] * rows.shape[1]), jnp.bfloat16)],
        compiler_params=pltpu.CompilerParams(vmem_limit_bytes=48 * 1024 * 1024),
        cost_estimate=pl.CostEstimate(flops=1, bytes_accessed=1, transcendentals=0),
    )(rows, weight)


def attend_backward(table, query, keys, values, grad):
    heads, length = query.shape[:2]
    groups = keys.shape[0]
    return pl.pallas_call(
        attend_back_kernel,
        out_shape=jax.ShapeDtypeStruct((length, (heads + 2 * groups) * HD), jnp.bfloat16),
        scratch_shapes=[
            pltpu.VMEM((groups * HD, length), jnp.bfloat16),
            pltpu.VMEM((groups, length, HD), jnp.float32),
            pltpu.VMEM((groups, length, HD), jnp.float32),
        ],
        compiler_params=pltpu.CompilerParams(vmem_limit_bytes=48 * 1024 * 1024),
        cost_estimate=pl.CostEstimate(flops=1, bytes_accessed=1, transcendentals=0),
    )(table, query, keys, values, grad)


def dispatch_kernel(first_ref, rows_ref, grads_ref, out_rows, out_grads, out_pick):
    count = out_rows.shape[0]
    tokens = rows_ref.shape[1]
    padded = -(-count // 16) * 16
    tail = rows_ref[0, :, D:]
    lane = lax.broadcasted_iota(jnp.int32, (padded, 128), 1)
    row = lax.broadcasted_iota(jnp.int32, (padded, 128), 0)
    wanted = (lane == 2 * EXPERTS + first_ref[0] + row) & (row < count)
    marks = lax.dot_general(
        wanted.astype(jnp.bfloat16),
        tail,
        (((1,), (1,)), ((), ())),
        preferred_element_type=jnp.float32,
    )
    earlier = lax.broadcasted_iota(jnp.int32, (tokens, tokens), 0) < lax.broadcasted_iota(
        jnp.int32, (tokens, tokens), 1
    )
    rank = jnp.dot(
        marks.astype(jnp.bfloat16),
        earlier.astype(jnp.bfloat16),
        preferred_element_type=jnp.float32,
    )
    slot = lax.broadcasted_iota(jnp.int32, (CAP, tokens), 0).astype(jnp.float32)
    pick = jnp.concatenate(
        [
            jnp.where(
                rank[item : item + 1, :] == slot, marks[item : item + 1, :], 0.0
            ).astype(jnp.bfloat16)
            for item in range(count)
        ],
        0,
    )
    out_pick[0] = pick
    moved = jnp.dot(pick, rows_ref[0], preferred_element_type=jnp.float32).astype(jnp.bfloat16)
    moved_grads = jnp.dot(pick, grads_ref[0], preferred_element_type=jnp.float32).astype(
        jnp.bfloat16
    )
    for item in range(count):
        out_rows[item] = moved[item * CAP : (item + 1) * CAP]
        out_grads[item] = moved_grads[item * CAP : (item + 1) * CAP]


def dispatch(first, rows, grads, count):
    sources, tokens, wide = rows.shape
    return pl.pallas_call(
        dispatch_kernel,
        grid_spec=pltpu.PrefetchScalarGridSpec(
            num_scalar_prefetch=1,
            grid=(sources,),
            in_specs=[
                pl.BlockSpec((1, tokens, wide), lambda s, f: (s, 0, 0)),
                pl.BlockSpec((1, tokens, D), lambda s, f: (s, 0, 0)),
            ],
            out_specs=(
                pl.BlockSpec((count, CAP, wide), lambda s, f: (0, s, 0)),
                pl.BlockSpec((count, CAP, D), lambda s, f: (0, s, 0)),
                pl.BlockSpec((1, count * CAP, tokens), lambda s, f: (s, 0, 0)),
            ),
        ),
        out_shape=(
            jax.ShapeDtypeStruct((count, sources * CAP, wide), jnp.bfloat16),
            jax.ShapeDtypeStruct((count, sources * CAP, D), jnp.bfloat16),
            jax.ShapeDtypeStruct((sources, count * CAP, tokens), jnp.bfloat16),
        ),
        compiler_params=pltpu.CompilerParams(vmem_limit_bytes=40 * 1024 * 1024),
        cost_estimate=pl.CostEstimate(flops=1, bytes_accessed=1, transcendentals=0),
    )(first, rows, grads)


def combine_kernel(pick_ref, rows_ref, out_ref):
    rows = jnp.concatenate([rows_ref[item] for item in range(rows_ref.shape[0])], 0)
    out_ref[0] = lax.dot_general(
        pick_ref[0], rows, (((0,), (0,)), ((), ())), preferred_element_type=jnp.float32
    ).astype(jnp.bfloat16)


def combine(pick, rows):
    sources, slots, tokens = pick.shape
    count, _, wide = rows.shape
    return pl.pallas_call(
        combine_kernel,
        grid=(sources,),
        in_specs=[
            pl.BlockSpec((1, slots, tokens), lambda s: (s, 0, 0)),
            pl.BlockSpec((count, CAP, wide), lambda s: (0, s, 0)),
        ],
        out_specs=pl.BlockSpec((1, tokens, wide), lambda s: (s, 0, 0)),
        out_shape=jax.ShapeDtypeStruct((sources, tokens, wide), jnp.bfloat16),
        compiler_params=pltpu.CompilerParams(vmem_limit_bytes=40 * 1024 * 1024),
        cost_estimate=pl.CostEstimate(flops=1, bytes_accessed=1, transcendentals=0),
    )(pick, rows)


def expert_kernel(first_ref, order_ref, rows_ref, grads_ref, *refs):
    produced_ref, grad_rows_ref, grad_hidden_ref, gated_ref, whole_in, whole_out = refs[-6:]
    pieces = refs[:-6]
    expert = first_ref[0] + pl.program_id(0)

    @pl.when(pl.program_id(1) == 0)
    def assemble():
        if len(pieces) == 2:
            whole_in[...] = pieces[0][0]
            whole_out[...] = pieces[1][0]
            return
        (folded,) = pieces
        deep = folded.shape[2]
        wide = whole_in.shape[1]
        folds = (folded.shape[3] - D) // wide
        for index in range(folded.shape[0]):
            block = order_ref[index]
            for fold in range(folds):
                start = pl.multiple_of((block * folds + fold) * deep, deep)
                whole_in[pl.ds(start, deep), :] = folded[
                    index, 0, :, fold * wide : (fold + 1) * wide
                ]
            start = pl.multiple_of(block * deep, deep)
            whole_out[pl.ds(start, deep), :] = folded[index, 0, :, folds * wide :]

    tail = rows_ref[0, :, D:].astype(jnp.float32)
    lane = lax.broadcasted_iota(jnp.int32, tail.shape, 1)
    own = (lane == expert) | (lane == EXPERTS + expert)
    gate = jnp.sum(jnp.where(own, tail, 0.0), axis=-1, keepdims=True)
    hidden = whole_out.shape[0]
    gate_up = jnp.dot(rows_ref[0, :, :D], whole_in[...], preferred_element_type=jnp.float32)
    gate_half = gate_up[:, :hidden]
    up_half = gate_up[:, hidden:]
    sigma = 1.0 / (1.0 + jnp.exp(-gate_half))
    activated = gate_half * sigma
    middle = activated * up_half
    gated = (gate * middle).astype(jnp.bfloat16)
    gated_ref[0] = gated
    produced_ref[0] = jnp.dot(gated, whole_out[...], preferred_element_type=jnp.float32).astype(
        jnp.bfloat16
    )
    grad_middle = RESIDUAL_SCALE * lax.dot_general(
        grads_ref[0],
        whole_out[...],
        (((1,), (1,)), ((), ())),
        preferred_element_type=jnp.float32,
    )
    grad_gate = jnp.sum(middle * grad_middle, axis=-1, keepdims=True)
    grad_middle = gate * grad_middle
    slope = sigma * (1.0 + gate_half * (1.0 - sigma))
    grad_hidden = jnp.concatenate(
        [grad_middle * up_half * slope, grad_middle * activated], -1
    ).astype(jnp.bfloat16)
    grad_hidden_ref[0] = grad_hidden
    grad_rows_ref[0, :, :D] = lax.dot_general(
        grad_hidden,
        whole_in[...],
        (((1,), (1,)), ((), ())),
        preferred_element_type=jnp.float32,
    ).astype(jnp.bfloat16)
    high = grad_gate.astype(jnp.bfloat16).astype(jnp.float32)
    spread = jnp.where(
        lane == expert, high, jnp.where(lane == EXPERTS + expert, grad_gate - high, 0.0)
    )
    grad_rows_ref[0, :, D:] = spread.astype(jnp.bfloat16)


def run_experts(first, order, rows, grads, pieces, hidden):
    count, slots, wide = rows.shape
    chunk = min(512, slots)
    by_chunk = lambda e, c, *_: (e, c, 0)
    if len(pieces) == 1:
        folded = pieces[0].shape
        piece_specs = [pl.BlockSpec((folded[0], 1) + folded[2:], lambda e, c, *_: (0, e, 0, 0))]
    else:
        piece_specs = [
            pl.BlockSpec((1,) + piece.shape[1:], lambda e, c, *_: (e, 0, 0)) for piece in pieces
        ]
    return pl.pallas_call(
        expert_kernel,
        grid_spec=pltpu.PrefetchScalarGridSpec(
            num_scalar_prefetch=2,
            grid=(count, slots // chunk),
            in_specs=[
                pl.BlockSpec((1, chunk, wide), by_chunk),
                pl.BlockSpec((1, chunk, D), by_chunk),
            ]
            + piece_specs,
            out_specs=(
                pl.BlockSpec((1, chunk, D), by_chunk),
                pl.BlockSpec((1, chunk, wide), by_chunk),
                pl.BlockSpec((1, chunk, 2 * hidden), by_chunk),
                pl.BlockSpec((1, chunk, hidden), by_chunk),
            ),
            scratch_shapes=[
                pltpu.VMEM((D, 2 * hidden), jnp.bfloat16),
                pltpu.VMEM((hidden, D), jnp.bfloat16),
            ],
        ),
        out_shape=(
            jax.ShapeDtypeStruct((count, slots, D), jnp.bfloat16),
            jax.ShapeDtypeStruct((count, slots, wide), jnp.bfloat16),
            jax.ShapeDtypeStruct((count, slots, 2 * hidden), jnp.bfloat16),
            jax.ShapeDtypeStruct((count, slots, hidden), jnp.bfloat16),
        ),
        compiler_params=pltpu.CompilerParams(vmem_limit_bytes=56 * 1024 * 1024),
        cost_estimate=pl.CostEstimate(flops=1, bytes_accessed=1, transcendentals=0),
    )(first, order, rows, grads, *pieces)


def weight_grad_kernel(order_ref, rows_ref, grads_ref, hidden_ref, gated_ref, *refs):
    outs, total_in, total_out = refs[:-2], refs[-2], refs[-1]
    chunk = pl.program_id(1)
    part_in = lax.dot_general(
        rows_ref[0, :, :D],
        hidden_ref[0],
        (((0,), (0,)), ((), ())),
        preferred_element_type=jnp.float32,
    )
    part_out = RESIDUAL_SCALE * lax.dot_general(
        gated_ref[0],
        grads_ref[0],
        (((0,), (0,)), ((), ())),
        preferred_element_type=jnp.float32,
    )

    @pl.when(chunk == 0)
    def store():
        total_in[...] = part_in
        total_out[...] = part_out

    @pl.when(chunk > 0)
    def add():
        total_in[...] += part_in
        total_out[...] += part_out

    @pl.when(chunk == pl.num_programs(1) - 1)
    def finish():
        if len(outs) == 2:
            outs[0][0] = total_in[...].astype(jnp.bfloat16)
            outs[1][0] = total_out[...].astype(jnp.bfloat16)
            return
        wide = total_in.shape[1]
        turns = outs[0].shape[0]
        deep = outs[0].shape[2]
        folds = (outs[0].shape[3] - D) // wide
        for number, out in enumerate(outs):
            for turn in range(turns):
                block = order_ref[number * turns + turn]
                for fold in range(folds):
                    start = pl.multiple_of((block * folds + fold) * deep, deep)
                    out[turn, 0, :, fold * wide : (fold + 1) * wide] = total_in[
                        pl.ds(start, deep), :
                    ].astype(jnp.bfloat16)
                start = pl.multiple_of(block * deep, deep)
                out[turn, 0, :, folds * wide :] = total_out[pl.ds(start, deep), :].astype(
                    jnp.bfloat16
                )


def weight_grads(order, rows, grads, grad_hidden, gated, shapes):
    count, slots, wide = rows.shape
    hidden = gated.shape[2]
    chunk = min(512, slots)
    by_chunk = lambda e, c, *_: (e, c, 0)
    if len(shapes) == 2:
        out_specs = tuple(pl.BlockSpec((1,) + s[1:], lambda e, c, *_: (e, 0, 0)) for s in shapes)
    else:
        out_specs = tuple(
            pl.BlockSpec((s[0], 1) + s[2:], lambda e, c, *_: (0, e, 0, 0)) for s in shapes
        )
    return pl.pallas_call(
        weight_grad_kernel,
        grid_spec=pltpu.PrefetchScalarGridSpec(
            num_scalar_prefetch=1,
            grid=(count, slots // chunk),
            in_specs=[
                pl.BlockSpec((1, chunk, wide), by_chunk),
                pl.BlockSpec((1, chunk, D), by_chunk),
                pl.BlockSpec((1, chunk, 2 * hidden), by_chunk),
                pl.BlockSpec((1, chunk, hidden), by_chunk),
            ],
            out_specs=out_specs,
            scratch_shapes=[
                pltpu.VMEM((D, 2 * hidden), jnp.float32),
                pltpu.VMEM((hidden, D), jnp.float32),
            ],
        ),
        out_shape=tuple(jax.ShapeDtypeStruct(s, jnp.bfloat16) for s in shapes),
        compiler_params=pltpu.CompilerParams(vmem_limit_bytes=56 * 1024 * 1024),
        cost_estimate=pl.CostEstimate(flops=1, bytes_accessed=1, transcendentals=0),
    )(order, rows, grads, grad_hidden, gated)


def swap(rows, axis, flip):
    size = lax.axis_size(axis)
    return lax.ppermute(rows, axis, [(i, i ^ flip) for i in range(size)])


def near(place, axis, flip):
    if lax.axis_size(axis) == 2:
        return 1 - place
    if flip == 1:
        return place + 1 - 2 * lax.rem(place, 2)
    if flip == 2:
        return lax.rem(place + 2, 4)
    return 3 - place


def greet(partners):
    barrier = pltpu.get_barrier_semaphore()
    for axis, flip in partners:
        pl.semaphore_signal(
            barrier,
            inc=1,
            device_id={axis: near(lax.axis_index(axis), axis, flip)},
            device_id_type=pl.DeviceIdType.MESH,
        )
    pl.semaphore_wait(barrier, len(partners))


class Link:
    def __init__(self, sends, receives):
        self.sends, self.receives, self.used, self.started = sends, receives, 0, []

    def push(self, source, target, axis, flip):
        copy = pltpu.make_async_remote_copy(
            src_ref=source,
            dst_ref=target,
            send_sem=self.sends.at[self.used],
            recv_sem=self.receives.at[self.used],
            device_id={axis: near(lax.axis_index(axis), axis, flip)},
            device_id_type=pl.DeviceIdType.MESH,
        )
        copy.start()
        self.used += 1
        self.started.append(copy)
        return copy

    def finish(self):
        for copy in self.started:
            copy.wait_send()


class Line:
    def __init__(self, rows_ref, out_ref, sends, receives):
        z, y = lax.axis_index("dp"), lax.axis_index("expert")
        self.inner = z * (3 - z) > 0
        self.outer = z * (3 - z) < 1

        def slot(flip):
            return 2 * (near(z, "dp", flip) if flip else z) + y

        def hand(sent, received, source, target, flip, axis="dp"):
            return pltpu.make_async_remote_copy(
                src_ref=source,
                dst_ref=target,
                send_sem=sends.at[sent],
                recv_sem=receives.at[received],
                device_id={axis: near(lax.axis_index(axis), axis, flip)},
                device_id_type=pl.DeviceIdType.MESH,
            )

        def block(flip):
            return out_ref.at[slot(flip)]

        self.to_first = hand(0, 1, rows_ref, block(0), 1)
        self.across_own = hand(1, 3, rows_ref, block(0), 3)
        self.across_first = hand(2, 2, block(1), block(1), 3)
        self.pass_third = hand(3, 2, block(3), block(3), 1)
        self.pass_second = hand(8, 3, block(2), block(2), 1)
        self.over = [
            hand(4 + flip, 4 + flip, block(flip) if flip else rows_ref, block(flip), 1, "expert")
            for flip in range(4)
        ]
        self.got = [None] + [hand(0, flip, block(flip), block(flip), 1) for flip in range(1, 4)]
        self.got_over = [
            hand(0, 4 + flip, block(flip), out_ref.at[slot(flip) + 1 - 2 * y], 1, "expert")
            for flip in range(4)
        ]

    def start(self):
        self.to_first.start()

        @pl.when(self.inner)
        def inner():
            self.across_own.start()

        self.over[0].start()

    def first(self):
        self.got[1].wait_recv()

        @pl.when(self.inner)
        def inner():
            self.across_first.start()

        self.over[1].start()

    def second(self):
        @pl.when(self.inner)
        def inner():
            self.got[3].wait_recv()
            self.pass_third.start()
            self.over[3].start()

        @pl.when(self.outer)
        def outer():
            self.got[2].wait_recv()
            self.over[2].start()

    def third(self):
        @pl.when(self.inner)
        def inner():
            self.got[2].wait_recv()
            self.pass_second.start()
            self.over[2].start()

        @pl.when(self.outer)
        def outer():
            self.got[3].wait_recv()
            self.over[3].start()

    def finish(self):
        self.to_first.wait_send()

        @pl.when(self.inner)
        def inner():
            for copy in (self.across_own, self.across_first, self.pass_third, self.pass_second):
                copy.wait_send()

        for copy in self.over:
            copy.wait_send()
        for copy in self.got_over:
            copy.wait_recv()


def gather_kernel(rows_ref, out_ref, sends, receives, local):
    greet([("dp", 1), ("dp", 3), ("expert", 1)])
    own = 2 * lax.axis_index("dp") + lax.axis_index("expert")
    keep = pltpu.make_async_copy(rows_ref, out_ref.at[own], local)
    keep.start()
    line = Line(rows_ref, out_ref, sends, receives)
    line.start()
    line.first()
    line.second()
    line.third()
    line.finish()
    keep.wait()


def gather_owners(rows, number):
    return pl.pallas_call(
        gather_kernel,
        out_shape=jax.ShapeDtypeStruct((8,) + rows.shape, rows.dtype),
        in_specs=[pl.BlockSpec(memory_space=pl.ANY)],
        out_specs=pl.BlockSpec(memory_space=pl.ANY),
        scratch_shapes=[
            pltpu.SemaphoreType.DMA((9,)),
            pltpu.SemaphoreType.DMA((8,)),
            pltpu.SemaphoreType.DMA,
        ],
        compiler_params=pltpu.CompilerParams(collective_id=number, has_side_effects=True),
    )(rows)


def scatter_kernel(blocks_ref, out_ref, over, sums, parts, sends, receives):
    greet([("dp", 1), ("dp", 3), ("expert", 1)])
    z, y = lax.axis_index("dp"), lax.axis_index("expert")
    inner = z * (3 - z) > 0

    def slot(flip, plane):
        return 2 * (near(z, "dp", flip) if flip else z) + plane

    def hand(number, source, target, flip, axis="dp"):
        return pltpu.make_async_remote_copy(
            src_ref=source,
            dst_ref=target,
            send_sem=sends.at[number],
            recv_sem=receives.at[number],
            device_id={axis: near(lax.axis_index(axis), axis, flip)},
            device_id_type=pl.DeviceIdType.MESH,
        )

    across = [
        hand(flip, blocks_ref.at[slot(flip, 1 - y)], over.at[flip], 1, "expert") for flip in range(4)
    ]
    to_line = [hand(4 + k, sums.at[3 - k], parts.at[k], 1) for k in range(3)]
    to_middle = [hand(7 + k, sums.at[2 + k], parts.at[3 + k], 3) for k in range(2)]
    to_end = hand(9, sums.at[1], parts.at[5], 1)

    def fold(flip):
        across[flip].wait_recv()
        return blocks_ref[slot(flip, y)].astype(jnp.float32) + over[flip].astype(jnp.float32)

    def part(number):
        return parts[number].astype(jnp.float32)

    @pl.when(inner)
    def middle():
        for flip in (2, 3, 1, 0):
            across[flip].start()
        second = fold(2)
        to_line[0].wait_recv()
        sums[2] = (second + part(0)).astype(jnp.bfloat16)
        to_middle[0].start()
        third = fold(3)
        to_line[1].wait_recv()
        sums[3] = (third + part(1)).astype(jnp.bfloat16)
        to_middle[1].start()
        first = fold(1)
        to_middle[0].wait_recv()
        sums[1] = (first + part(3)).astype(jnp.bfloat16)
        to_end.start()
        own = fold(0)
        to_line[2].wait_recv()
        to_middle[1].wait_recv()
        out_ref[...] = own + part(2) + part(4)
        to_middle[0].wait_send()
        to_middle[1].wait_send()
        to_end.wait_send()

    @pl.when(jnp.logical_not(inner))
    def ends():
        for flip in (3, 2, 1, 0):
            across[flip].start()
        for k in range(3):
            sums[3 - k] = fold(3 - k).astype(jnp.bfloat16)
            to_line[k].start()
        own = fold(0)
        to_end.wait_recv()
        out_ref[...] = own + part(5)
        for k in range(3):
            to_line[k].wait_send()

    for flip in range(4):
        across[flip].wait_send()


def scatter_owners(blocks, number):
    shape = blocks.shape[1:]
    return pl.pallas_call(
        scatter_kernel,
        out_shape=jax.ShapeDtypeStruct(shape, jnp.float32),
        scratch_shapes=[
            pltpu.VMEM((4,) + shape, jnp.bfloat16),
            pltpu.VMEM((4,) + shape, jnp.bfloat16),
            pltpu.VMEM((6,) + shape, jnp.bfloat16),
            pltpu.SemaphoreType.DMA((10,)),
            pltpu.SemaphoreType.DMA((10,)),
        ],
        compiler_params=pltpu.CompilerParams(
            collective_id=number, has_side_effects=True, vmem_limit_bytes=48 * 1024 * 1024
        ),
    )(blocks)


def opening_kernel(
    rows_ref, columns_ref, pack_ref, weights_ref, grads_ref,
    all_rows, all_columns, all_pack, pieces, all_grads,
    normed_ref, query_ref, keys_ref, values_ref, attended_ref,
    outgoing, flipped, sends, receives, line_sends, line_receives, locals_,
):
    z, y, c = lax.axis_index("dp"), lax.axis_index("expert"), lax.axis_index("ctx")
    greet([("dp", 1), ("dp", 2), ("dp", 3), ("expert", 1), ("ctx", 1), ("ctx", 2), ("ctx", 3)])
    link = Link(sends, receives)
    line = Line(grads_ref, all_grads, line_sends, line_receives)
    own = 2 * z + y
    count = weights_ref.shape[1]

    def z_at(flip):
        return near(z, "dp", flip) if flip else z

    def c_at(flip):
        return near(c, "ctx", flip) if flip else c

    keeps = [
        pltpu.make_async_copy(source, target, locals_.at[number])
        for number, (source, target) in enumerate(
            [
                (columns_ref.at[c], all_columns.at[own, c]),
                (rows_ref, all_rows.at[c]),
                (pack_ref, all_pack.at[z, y, c]),
                (grads_ref, all_grads.at[own]),
                (weights_ref.at[z], pieces.at[0, 0]),
            ]
        )
    ]
    for keep in keeps:
        keep.start()
    cut = [
        link.push(columns_ref.at[c_at(flip)], all_columns.at[own, c], "ctx", flip)
        for flip in (1, 2, 3)
    ]

    def share(*place):
        step, rest = place[0], place[1:]
        source = pieces.at[(step, 0) + rest]
        over = link.push(source, pieces.at[(step, 2) + rest], "ctx", 2)
        core = link.push(source, pieces.at[(step, 1) + rest], "ctx", 1)
        return over, core

    def hand_on(*place):
        step, rest = place[0], place[1:]
        return link.push(pieces.at[(step, 2) + rest], pieces.at[(step, 3) + rest], "ctx", 1)

    moved = {
        step: link.push(weights_ref.at[z_at(step)], pieces.at[step, 0], "dp", step)
        for step in (1, 2)
    }
    line.start()
    keeps[4].wait()
    shared = [share(0)]
    keeps[0].wait()
    for copy in cut:
        copy.wait_recv()
    column_line = [
        link.push(all_columns.at[own], all_columns.at[own], "dp", flip) for flip in (1, 2, 3)
    ]
    column_over = [link.push(all_columns.at[own], all_columns.at[own], "expert", 1)]
    rows_over = link.push(rows_ref, all_rows.at[c], "ctx", 2)
    rows_core = link.push(rows_ref, all_rows.at[c], "ctx", 1)
    pack_line = [link.push(pack_ref, all_pack.at[z, y, c], "dp", flip) for flip in (1, 2, 3)]
    line.first()
    for flip in (1, 2, 3):
        column_line[flip - 1].wait_recv()
        block = all_columns.at[2 * z_at(flip) + y]
        column_over.append(link.push(block, block, "expert", 1))
    rows_over.wait_recv()
    rows_pass = link.push(all_rows.at[c_at(2)], all_rows.at[c_at(2)], "ctx", 1)
    moved[1].wait_recv()
    shared.append(share(1))
    line.second()
    for copy in pack_line:
        copy.wait_recv()
    keeps[2].wait()
    pack_over = link.push(all_pack.at[:, y, c], all_pack.at[:, y, c], "expert", 1)
    for copy in [rows_core, rows_pass] + column_over:
        copy.wait_recv()
    keeps[1].wait()
    project_rows(
        all_rows,
        all_columns[...].reshape(D, all_columns.shape[-1]),
        normed_ref,
        query_ref,
        keys_ref,
        values_ref,
        flipped,
    )
    line.third()
    pack_over.wait_recv()
    pack_pair = link.push(all_pack.at[:, :, c], all_pack.at[:, :, c], "ctx", 2)
    pack_core = link.push(all_pack.at[:, :, c], all_pack.at[:, :, c], "ctx", 1)
    shared[0][0].wait_recv()
    passed = [hand_on(0)]
    moved[2].wait_recv()
    shared.append(share(2))

    def last_piece(item):
        return link.push(weights_ref.at[z_at(3), item], pieces.at[3, 0, item], "dp", 3)

    last = [last_piece(0), last_piece(1)]
    for index in range(all_rows.shape[0]):
        attend_rows(index, all_rows.shape[1], query_ref, keys_ref, outgoing, flipped)
    attended = [
        link.push(outgoing.at[c_at(flip)], attended_ref.at[c], "ctx", flip) for flip in (1, 2, 3)
    ]
    attended_ref[c] = outgoing[c]
    shared[1][0].wait_recv()
    passed.append(hand_on(1))
    for item in range(count):
        last[item].wait_recv()
        if item + 2 < count:
            last.append(last_piece(item + 2))
        shared.append(share(3, item))
    pack_pair.wait_recv()
    pack_last = link.push(all_pack.at[:, :, c_at(2)], all_pack.at[:, :, c_at(2)], "ctx", 1)
    shared[2][0].wait_recv()
    passed.append(hand_on(2))
    for item in range(count):
        shared[3 + item][0].wait_recv()
        passed.append(hand_on(3, item))
    keeps[3].wait()
    for copy in attended + [pack_core, pack_last] + passed:
        copy.wait_recv()
    for over, core in shared:
        core.wait_recv()
    line.finish()
    link.finish()


def opening(rows, columns, pack, weights, grads, heads, groups, number):
    ctx = columns.shape[0]
    shards, count = weights.shape[:2]
    kind = jnp.bfloat16
    copies = 24 + 10 + 4 * count
    far = pl.BlockSpec(memory_space=pl.ANY)
    held = pl.BlockSpec(memory_space=pltpu.VMEM)
    all_rows = (ctx,) + rows.shape
    return pl.pallas_call(
        opening_kernel,
        out_shape=(
            jax.ShapeDtypeStruct(all_rows, kind),
            jax.ShapeDtypeStruct((8,) + columns.shape, kind),
            jax.ShapeDtypeStruct((shards, 2, ctx) + pack.shape, kind),
            jax.ShapeDtypeStruct((shards, ctx) + weights.shape[1:], kind),
            jax.ShapeDtypeStruct((8,) + grads.shape, kind),
        )
        + attend_shapes(all_rows, heads, groups),
        in_specs=[far] * 5,
        out_specs=(held, held, far, far, far) + (held,) * 5,
        scratch_shapes=[
            pltpu.VMEM((ctx, rows.shape[0], heads * HD), kind),
            pltpu.VMEM((groups * HD, ctx * rows.shape[0]), kind),
            pltpu.SemaphoreType.DMA((copies,)),
            pltpu.SemaphoreType.DMA((copies,)),
            pltpu.SemaphoreType.DMA((9,)),
            pltpu.SemaphoreType.DMA((8,)),
            pltpu.SemaphoreType.DMA((5,)),
        ],
        compiler_params=pltpu.CompilerParams(
            collective_id=number, has_side_effects=True, vmem_limit_bytes=48 * 1024 * 1024
        ),
    )(rows, columns, pack, weights, grads)


def split_high_low(values):
    high = values.astype(jnp.bfloat16)
    return high, (values - high.astype(jnp.float32)).astype(jnp.bfloat16)


def pad_columns(like, columns):
    return jnp.zeros((like.shape[0], columns), like.dtype)


def gather_ctx(rows):
    ctx = lax.axis_size("ctx")
    column = lax.axis_index("ctx")
    pieces = {0: rows}
    flip = ctx // 2
    while flip:
        pieces.update({turn ^ flip: swap(item, "ctx", flip) for turn, item in pieces.items()})
        flip //= 2
    out = jnp.zeros((ctx,) + rows.shape, rows.dtype)
    for turn in range(ctx):
        out = lax.dynamic_update_index_in_dim(out, pieces[turn], column ^ turn, 0)
    return out


def exchange_ctx(blocks):
    column = lax.axis_index("ctx")
    out = jnp.zeros(blocks.shape, blocks.dtype)
    for turn in range(blocks.shape[0]):
        item = lax.dynamic_index_in_dim(blocks, column ^ turn, 0, keepdims=False)
        if turn:
            item = swap(item, "ctx", turn)
        out = lax.dynamic_update_index_in_dim(out, item, column ^ turn, 0)
    return out


def scatter_ctx(blocks):
    column = lax.axis_index("ctx")
    flip = 1
    held = blocks
    while flip < lax.axis_size("ctx"):
        pairs = held.reshape((held.shape[0] // 2, 2) + held.shape[1:])
        bit = (column // flip) % 2
        keep = lax.dynamic_index_in_dim(pairs, bit, 1, keepdims=False)
        give = lax.dynamic_index_in_dim(pairs, 1 - bit, 1, keepdims=False)
        held = keep.astype(jnp.float32) + swap(give, "ctx", flip).astype(jnp.float32)
        flip *= 2
        if flip < lax.axis_size("ctx"):
            held = held.astype(jnp.bfloat16)
    return held[0]


def group_columns(rows, ctx):
    depth = rows.shape[0]
    cuts = (rows[:, : H * HD], rows[:, H * HD : (H + KV) * HD], rows[:, (H + KV) * HD :])
    return jnp.concatenate([cut.reshape(depth, ctx, -1) for cut in cuts], -1).transpose(1, 0, 2)


def ungroup_columns(groups):
    ctx, depth, _ = groups.shape
    query, key = H * HD // ctx, KV * HD // ctx
    cuts = (groups[..., :query], groups[..., query : query + key], groups[..., query + key :])
    return jnp.concatenate([cut.transpose(1, 0, 2).reshape(depth, -1) for cut in cuts], 1)


def block_order():
    shards, ctx = lax.axis_size("dp"), lax.axis_size("ctx")
    place, column = lax.axis_index("dp"), lax.axis_index("ctx")
    return place, column, shards, ctx


def fold_weights(expert_in, expert_out):
    deep = expert_out.shape[1]
    folds = expert_in.shape[1] // deep
    cuts = [expert_in[:, fold * deep : (fold + 1) * deep] for fold in range(folds)]
    return jnp.concatenate(cuts + [expert_out], -1)


def piece_order():
    place, column, shards, ctx = block_order()
    blocks = [
        (place ^ step) * ctx + (column ^ turn) for step in range(shards) for turn in range(ctx)
    ]
    return jnp.stack(blocks).astype(jnp.int32)


def spread_weights(expert_in, expert_out):
    shards = lax.axis_size("dp")
    count, depth = expert_in.shape[:2]
    part = FFE // shards
    cut = expert_in.reshape(count, depth, 2, shards, part).transpose(3, 0, 1, 2, 4)
    moved_in = lax.all_to_all(cut, "dp", split_axis=0, concat_axis=0, tiled=True)
    all_in = lax.all_gather(moved_in.transpose(1, 0, 2, 3, 4), "ctx", axis=2, tiled=True)
    all_out = lax.all_gather(expert_out, "ctx", axis=1, tiled=True)
    return [all_in.reshape(count, -1, 2 * part), all_out]


def collect_weights(order, rows, grads, grad_hidden, gated, expert_in, expert_out, close):
    place, column, shards, ctx = block_order()
    depth_in, depth_out = expert_in.shape[1], expert_out.shape[1]
    if close:
        count = expert_in.shape[0] // shards
        folds = depth_in // depth_out
        sent, slots = [], []
        for step in reversed(range(shards)):
            for bit in (1, 0):
                sent.append((ctx // 2, count, depth_out, folds * 2 * FFE + D))
                slots += [step * ctx + turn for turn in range(bit, ctx, 2)]
        order = jnp.stack([order[slot] for slot in slots])
        parts = weight_grads(order, rows, grads, grad_hidden, gated, sent)
        received = []
        for number, step in enumerate(reversed(range(shards))):
            give, keep = parts[2 * number], parts[2 * number + 1]
            flip = 1
            while True:
                total = keep.astype(jnp.float32) + swap(give, "ctx", flip).astype(jnp.float32)
                total = total.astype(jnp.bfloat16)
                flip *= 2
                if flip == ctx:
                    break
                keep, give = total[0::2], total[1::2]
            piece = swap(total[0], "dp", step) if step else total[0]
            received.append((place ^ step, piece))
        return received
    count = expert_in.shape[0]
    part = FFE // shards
    blocks = shards * ctx
    shapes = ((count, blocks * depth_in, 2 * part), (count, part, D))
    grad_in, grad_out = weight_grads(order, rows, grads, grad_hidden, gated, shapes)
    part_in = lax.psum_scatter(
        grad_in.reshape(count, shards, -1, 2, part), "ctx", scatter_dimension=2, tiled=True
    )
    own_in = lax.all_to_all(
        part_in.transpose(1, 0, 2, 3, 4), "dp", split_axis=0, concat_axis=0, tiled=True
    )
    own_in = own_in.transpose(1, 2, 3, 0, 4).reshape(count, -1, 2 * FFE)
    own_out = lax.psum_scatter(grad_out, "ctx", scatter_dimension=1, tiled=True)
    return [(0, fold_weights(own_in, own_out))]


def expert_step_kernel(first_ref, grad_ref, *refs):
    states, outs = refs[:6], refs[-8:]
    wide = states[0].shape[2]
    deep = states[3].shape[1]
    folds = states[0].shape[1] // deep
    rates = learn_rates()
    for fold in range(folds):
        span = pl.ds(fold * deep, deep)
        grad = grad_ref[0, :, fold * wide : (fold + 1) * wide].astype(jnp.float32)
        news = adam_step(
            states[0][0, span, :], states[1][0, span, :], states[2][0, span, :], grad, DECAY_RATE, rates[5]
        )
        for out, new in zip(outs[:4], news):
            out[0, span, :] = new
    grad = grad_ref[0, :, folds * wide :].astype(jnp.float32)
    news = adam_step(states[3][0], states[4][0], states[5][0], grad, DECAY_RATE, rates[6])
    for out, new in zip(outs[4:], news):
        out[0] = new


def expert_step(first, folded, states, outs):
    shapes = [states[1].shape] * 4 + [states[4].shape] * 4
    moved = lambda e, f: (f[0] + e, 0, 0)
    block = lambda shape: pl.BlockSpec((1,) + shape[1:], moved)
    begun = [] if outs is None else list(outs)
    return pl.pallas_call(
        expert_step_kernel,
        grid_spec=pltpu.PrefetchScalarGridSpec(
            num_scalar_prefetch=1,
            grid=(folded.shape[0],),
            in_specs=[pl.BlockSpec((1,) + folded.shape[1:], lambda e, f: (e, 0, 0))]
            + [block(state.shape) for state in states]
            + [pl.BlockSpec(memory_space=pl.ANY) for _ in begun],
            out_specs=tuple(block(shape) for shape in shapes),
        ),
        out_shape=tuple(jax.ShapeDtypeStruct(shape, jnp.float32) for shape in shapes),
        input_output_aliases={8 + index: index for index in range(len(begun))},
        compiler_params=pltpu.CompilerParams(vmem_limit_bytes=40 * 1024 * 1024),
        cost_estimate=pl.CostEstimate(flops=1, bytes_accessed=1, transcendentals=0),
    )(first, folded, *states, *begun)


def local(
    tokens,
    cotangent,
    routes,
    positions,
    gain_attend,
    gain_attend_mean,
    gain_attend_square,
    project_in,
    project_in_mean,
    project_in_square,
    project_out,
    project_out_mean,
    project_out_square,
    gain_expert,
    gain_expert_mean,
    gain_expert_square,
    router_weight,
    router_weight_mean,
    router_weight_square,
    expert_in,
    expert_in_mean,
    expert_in_square,
    expert_out,
    expert_out_mean,
    expert_out_square,
):
    everywhere = ("dp", "expert", "ctx")
    owners = ("dp", "expert")
    shards = lax.axis_size("dp")
    planes = lax.axis_size("expert")
    ctx = lax.axis_size("ctx")
    rows_local = tokens.shape[0]
    local_count = expert_in.shape[0]
    close = (shards, planes, ctx) == (4, 2, 4) and local_count % shards == 0
    heads, groups = H // ctx, KV // ctx
    hidden_in = tokens.astype(jnp.float32)

    half = HD // 2
    freqs = ROPE_BASE ** (-jnp.arange(half, dtype=jnp.float32) * 2.0 / HD)
    angles = positions.astype(jnp.float32)[:, None] * freqs[None, :]
    table = jnp.concatenate(split_high_low(jnp.cos(angles)) + split_high_low(jnp.sin(angles)), 1)
    gain_attend_wide = gain_attend.astype(jnp.float32)[:, None]
    scaled_in = (gain_attend_wide * project_in.astype(jnp.float32)).astype(jnp.bfloat16)
    rows = jnp.concatenate([tokens, table], 1)
    columns = group_columns(scaled_in, ctx)
    pack_out = jnp.concatenate(
        [project_out, router_weight, gain_expert[:, None], pad_columns(project_out, 87)], 1
    )
    order = piece_order()
    if close:
        folded = fold_weights(expert_in, expert_out)
        folded = folded.reshape((shards, -1) + folded.shape[1:])
        (
            seq_rows, own_in, full_pack_out, pieces, all_grads,
            seq_normed, query, keys, values, attended,
        ) = opening(rows, columns, pack_out, folded, cotangent, heads, groups, 1)
        pieces = [pieces.reshape((-1,) + pieces.shape[2:])]
    else:
        seq_rows = gather_ctx(rows)
        own_in = lax.all_gather(exchange_ctx(columns), owners, axis=0, tiled=False)
        full_pack_out = lax.all_gather(pack_out, everywhere, axis=0, tiled=True)
        all_grads = lax.all_gather(cotangent, owners, axis=0, tiled=False)
        pieces = spread_weights(expert_in, expert_out)
        seq_normed, query, keys, values, seq_attended = attend_forward(
            seq_rows, own_in.reshape(D, -1), heads, groups
        )
        attended = exchange_ctx(seq_attended)
    seq_rows = seq_rows.reshape(-1, D + 128)
    own_in = own_in.reshape(D, -1)
    full_pack_out = full_pack_out.reshape(H * HD, -1)
    full_out = full_pack_out[:, :D]
    full_router = full_pack_out[:, D : D + EXPERTS]
    gain_two = full_pack_out[:, D + EXPERTS].astype(jnp.float32)

    attended = attended.transpose(1, 0, 2).reshape(rows_local, H * HD)
    branch = jnp.dot(attended, full_out, preferred_element_type=jnp.float32)
    after = hidden_in + RESIDUAL_SCALE * branch
    normed_two, factor_two = normalize(after)
    expert_input = (normed_two * gain_two).astype(jnp.bfloat16)
    logits = jnp.dot(expert_input, full_router, preferred_element_type=jnp.float32)
    chosen = jnp.any(routes[:, :, None] == jnp.arange(EXPERTS, dtype=jnp.int32), axis=1)
    peak = jnp.max(jnp.where(chosen, logits, -3e38), axis=-1, keepdims=True)
    raised = jnp.where(chosen, jnp.exp(jnp.where(chosen, logits - peak, 0.0)), 0.0)
    gates = raised / jnp.sum(raised, axis=-1, keepdims=True)
    packed = jnp.concatenate(
        (expert_input,)
        + split_high_low(gates)
        + (chosen.astype(jnp.bfloat16), pad_columns(expert_input, 128 - 3 * EXPERTS)),
        1,
    )
    if close:
        all_packed = gather_owners(packed, 2)
    else:
        all_packed = lax.all_gather(packed, owners, axis=0, tiled=False)

    first = lax.axis_index("expert") * local_count
    count = local_count
    hidden = FFE // shards
    if close:
        count = local_count // shards
        hidden = FFE
        first = first + lax.axis_index("dp") * count
    first = first.astype(jnp.int32).reshape(1)
    slot_rows, slot_grads, pick = dispatch(first, all_packed, all_grads, count)
    produced, grad_rows, grad_hidden, gated = run_experts(
        first, order, slot_rows, slot_grads, pieces, hidden
    )
    shared_grads = combine(pick, grad_rows)
    if close:
        grad_routed = scatter_owners(shared_grads, 3)
    else:
        grad_routed = lax.psum_scatter(
            shared_grads, owners, scatter_dimension=0, tiled=False
        ).astype(jnp.float32)
    expert_grads = collect_weights(
        order, slot_rows, slot_grads, grad_hidden, gated, expert_in, expert_out, close
    )
    produced, grad_routed = lax.optimization_barrier((produced, grad_routed))
    moe = lax.psum_scatter(
        combine(pick, produced), owners, scatter_dimension=0, tiled=False
    ).astype(jnp.float32)
    block_output = (after + RESIDUAL_SCALE * moe).astype(jnp.bfloat16)

    grad_final = cotangent.astype(jnp.float32)
    grad_gates = grad_routed[:, D : D + EXPERTS] + grad_routed[:, D + EXPERTS : D + 2 * EXPERTS]
    grad_picked = gates * (grad_gates - jnp.sum(gates * grad_gates, axis=-1, keepdims=True))
    grad_logits = grad_picked.astype(jnp.bfloat16)
    grad_from_router = jnp.einsum(
        "te,de->td", grad_logits, full_router, preferred_element_type=jnp.float32
    )
    grad_input = grad_from_router + grad_routed[:, :D]
    grad_after = grad_final + norm_back(grad_input * gain_two, normed_two, factor_two)
    grad_branch = (RESIDUAL_SCALE * grad_after).astype(jnp.bfloat16)
    grad_attended = jnp.einsum(
        "td,cd->tc", grad_branch, full_out, preferred_element_type=jnp.float32
    ).astype(jnp.bfloat16)
    seq_grad = exchange_ctx(
        grad_attended.reshape(rows_local, ctx, heads * HD).transpose(1, 0, 2)
    ).reshape(ctx * rows_local, heads * HD)
    grad_mixed = attend_backward(seq_rows[:, D:], query, keys, values, seq_grad)
    grad_in_part = jnp.einsum(
        "td,tc->dc", seq_normed, grad_mixed, preferred_element_type=jnp.float32
    ).astype(jnp.bfloat16)
    grad_in_part = grad_in_part.reshape(shards * planes, -1, grad_in_part.shape[1])
    if close:
        shard_columns = scatter_owners(grad_in_part, 4).astype(jnp.bfloat16)
    else:
        shard_columns = lax.psum_scatter(
            grad_in_part, owners, scatter_dimension=0, tiled=False
        )
    shard_scaled = ungroup_columns(
        exchange_ctx(shard_columns.reshape(ctx, -1, shard_columns.shape[-1]))
    ).astype(jnp.float32)
    shard_in = gain_attend_wide * shard_scaled
    shard_attend = jnp.sum(shard_scaled * project_in.astype(jnp.float32), axis=1)
    grad_scaled = jnp.einsum(
        "tc,dc->td", grad_mixed, own_in, preferred_element_type=jnp.float32
    ).astype(jnp.bfloat16)
    grad_normed = scatter_ctx(grad_scaled.reshape(ctx, rows_local, D))
    normed_one, factor_one = normalize(hidden_in)
    input_grad = grad_after + norm_back(grad_normed, normed_one, factor_one)

    grad_project_out = jnp.einsum(
        "tc,td->cd", attended, grad_branch, preferred_element_type=jnp.float32
    ).astype(jnp.bfloat16)
    ones = jnp.where(jnp.arange(128) == EXPERTS, 1.0, 0.0).astype(jnp.bfloat16)
    grad_small = jnp.einsum(
        "td,te->de",
        jnp.concatenate([expert_input, (grad_input * normed_two).astype(jnp.bfloat16)], 0),
        jnp.concatenate(
            [
                jnp.pad(grad_logits, ((0, 0), (0, 128 - EXPERTS))),
                jnp.broadcast_to(ones, (rows_local, 128)),
            ],
            0,
        ),
        preferred_element_type=jnp.float32,
    ).astype(jnp.bfloat16)
    grad_pack_out = jnp.concatenate([grad_project_out, grad_small], 1)
    shard_pack_out = lax.psum_scatter(
        grad_pack_out, everywhere, scatter_dimension=0, tiled=True
    ).astype(jnp.float32)
    shard_out = shard_pack_out[:, :D]
    shard_router = shard_pack_out[:, D : D + EXPERTS]
    shard_expert = shard_pack_out[:, D + EXPERTS]
    rates = learn_rates()
    results = [block_output, input_grad]
    results.extend(
        adam_step(gain_attend, gain_attend_mean, gain_attend_square, shard_attend, 0.0, rates[0])
    )
    results.extend(
        adam_step(project_in, project_in_mean, project_in_square, shard_in, DECAY_RATE, rates[1])
    )
    results.extend(
        adam_step(
            project_out, project_out_mean, project_out_square, shard_out, DECAY_RATE, rates[2]
        )
    )
    results.extend(
        adam_step(gain_expert, gain_expert_mean, gain_expert_square, shard_expert, 0.0, rates[3])
    )
    results.extend(
        adam_step(
            router_weight,
            router_weight_mean,
            router_weight_square,
            shard_router,
            DECAY_RATE,
            rates[4],
        )
    )
    states = (expert_in, expert_in_mean, expert_in_square, expert_out, expert_out_mean, expert_out_square)
    expert_outs = None
    for place, folded in expert_grads:
        base = jnp.asarray(place * folded.shape[0], jnp.int32).reshape(1)
        expert_outs = expert_step(base, folded, states, expert_outs)
    results.extend(expert_outs)
    return tuple(results)


def solution(mesh):
    placed = (
        P(("dp", "expert", "ctx"), None),
        P(("dp", "expert", "ctx"), None),
        P(("dp", "expert", "ctx"), None),
        P(("dp", "expert", "ctx")),
        P(("dp", "expert", "ctx")),
        P(("dp", "expert", "ctx")),
        P(("dp", "expert", "ctx")),
        P(("dp", "expert", "ctx"), None),
        P(("dp", "expert", "ctx"), None),
        P(("dp", "expert", "ctx"), None),
        P(("dp", "expert", "ctx"), None),
        P(("dp", "expert", "ctx"), None),
        P(("dp", "expert", "ctx"), None),
        P(("dp", "expert", "ctx")),
        P(("dp", "expert", "ctx")),
        P(("dp", "expert", "ctx")),
        P(("dp", "expert", "ctx"), None),
        P(("dp", "expert", "ctx"), None),
        P(("dp", "expert", "ctx"), None),
        P("expert", ("dp", "ctx"), None),
        P("expert", ("dp", "ctx"), None),
        P("expert", ("dp", "ctx"), None),
        P("expert", ("dp", "ctx"), None),
        P("expert", ("dp", "ctx"), None),
        P("expert", ("dp", "ctx"), None),
    )
    return jax.shard_map(
        local,
        mesh=mesh,
        in_specs=placed,
        out_specs=(
            P(("dp", "expert", "ctx"), None),
            P(("dp", "expert", "ctx"), None),
            P(("dp", "expert", "ctx")),
            P(("dp", "expert", "ctx")),
            P(("dp", "expert", "ctx")),
            P(("dp", "expert", "ctx")),
            P(("dp", "expert", "ctx"), None),
            P(("dp", "expert", "ctx"), None),
            P(("dp", "expert", "ctx"), None),
            P(("dp", "expert", "ctx"), None),
            P(("dp", "expert", "ctx"), None),
            P(("dp", "expert", "ctx"), None),
            P(("dp", "expert", "ctx"), None),
            P(("dp", "expert", "ctx"), None),
            P(("dp", "expert", "ctx")),
            P(("dp", "expert", "ctx")),
            P(("dp", "expert", "ctx")),
            P(("dp", "expert", "ctx")),
            P(("dp", "expert", "ctx"), None),
            P(("dp", "expert", "ctx"), None),
            P(("dp", "expert", "ctx"), None),
            P(("dp", "expert", "ctx"), None),
            P("expert", ("dp", "ctx"), None),
            P("expert", ("dp", "ctx"), None),
            P("expert", ("dp", "ctx"), None),
            P("expert", ("dp", "ctx"), None),
            P("expert", ("dp", "ctx"), None),
            P("expert", ("dp", "ctx"), None),
            P("expert", ("dp", "ctx"), None),
            P("expert", ("dp", "ctx"), None),
        ),
        check_vma=False,
    )
```

```python
import functools

import jax
import jax.numpy as jnp
from jax import lax
from jax.experimental import pallas as pl
from jax.experimental.pallas import tpu as pltpu
from jax.sharding import PartitionSpec as P

D = 1536
H = 24
KV = 8
HD = 64
FFE = 512
EXPERTS = 40
TOP = 8
STEP = 8
CAP = 64


EPS_NORM = 1e-06
ATTN_SCALE = 0.015625
RESIDUAL_SCALE = 0.22
BETA_ONE = 0.9
BETA_TWO = 0.95
ADAM_EPS = 1e-08
DECAY_RATE = 0.1
ROPE_BASE = 10000.0


def normalize(rows):
    factor = lax.rsqrt(jnp.mean(rows * rows, axis=-1, keepdims=True) + EPS_NORM)
    return (rows * factor, factor)


def norm_back(grad_normed, normed, factor):
    return factor * (grad_normed - normed * jnp.mean(grad_normed * normed, axis=-1, keepdims=True))


def learn_rates():
    return (
        0.3,
        3.0 / (D // 16) ** 0.5,
        3.0 / (D // 12) ** 0.5,
        0.3,
        3.0 / (4 * D) ** 0.5,
        3.0 / D**0.5,
        3.0 / (FFE // 32) ** 0.5,
    )


def adam_step(weight, first, second, grad, decay, rate):
    new_first = BETA_ONE * first + (1.0 - BETA_ONE) * grad
    new_second = BETA_TWO * second + (1.0 - BETA_TWO) * grad * grad
    corrected = (
        new_first
        / (1.0 - BETA_ONE**STEP)
        / (jnp.sqrt(new_second / (1.0 - BETA_TWO**STEP)) + ADAM_EPS)
    )
    old = weight.astype(jnp.float32)
    return (grad, new_first, new_second, old - rate * (corrected + decay * old))


def lane_tables(table):
    half = HD // 2
    source = lax.broadcasted_iota(jnp.int32, (128, 128), 0)
    target = lax.broadcasted_iota(jnp.int32, (128, 128), 1)
    same = (source % half) == (target % half)
    group = source // half
    first = (target % HD) < half
    cosine = jnp.where(same & (group < 2), 1.0, 0.0).astype(jnp.bfloat16)
    ahead = jnp.where(same & (group >= 2) & first, -1.0, 0.0).astype(jnp.bfloat16)
    behind = jnp.where(same & (group >= 2) & jnp.logical_not(first), 1.0, 0.0).astype(jnp.bfloat16)
    return tuple(
        jnp.dot(table, item, preferred_element_type=jnp.float32)
        for item in (cosine, ahead, behind)
    )


def turn_lanes(block, tables, sign):
    cosine, ahead, behind = tables
    half = HD // 2
    turned = pltpu.roll(block, 128 - half, 1) * ahead + pltpu.roll(block, half, 1) * behind
    return block * cosine + sign * turned


def scores_of(keys, query, start, length):
    scores = (
        lax.dot_general(
            keys, query, (((1,), (1,)), ((), ())), preferred_element_type=jnp.float32
        )
        * ATTN_SCALE
    )
    rows = lax.broadcasted_iota(jnp.int32, scores.shape, 0)
    columns = lax.broadcasted_iota(jnp.int32, scores.shape, 1) + start
    return jnp.where(rows <= columns, scores, -1e30)


def project_rows(rows_ref, weight, normed_ref, query_ref, keys_ref, values_ref, flipped):
    blocks, block = rows_ref.shape[:2]
    heads, groups = query_ref.shape[0], keys_ref.shape[0]
    wide = heads * HD
    for index in range(blocks):
        span = pl.ds(index * block, block)
        rows = rows_ref[index, :, :D].astype(jnp.float32)
        factor = lax.rsqrt(jnp.mean(rows * rows, axis=-1, keepdims=True) + EPS_NORM)
        normed = (rows * factor).astype(jnp.bfloat16)
        normed_ref[span, :] = normed
        tables = lane_tables(rows_ref[index, :, D : D + 128])
        mixed = jnp.dot(normed, weight, preferred_element_type=jnp.float32)
        for column in range(0, wide + 2 * groups * HD, 128):
            part = mixed[:, column : column + 128]
            if column < wide + groups * HD:
                part = turn_lanes(part, tables, 1.0)
            else:
                flipped[column - wide - groups * HD : column - wide - groups * HD + 128, span] = (
                    part.T.astype(jnp.bfloat16)
                )
            part = part.astype(jnp.bfloat16)
            for half in range(2):
                head = column // HD + half
                piece = part[:, half * HD : (half + 1) * HD]
                if head < heads:
                    query_ref[head, span, :] = piece
                elif head < heads + groups:
                    keys_ref[head - heads, span, :] = piece
                else:
                    values_ref[head - heads - groups, span, :] = piece


def attend_rows(index, block, query_ref, keys_ref, out_ref, flipped):
    heads, groups = query_ref.shape[0], keys_ref.shape[0]
    length = (index + 1) * block
    span = pl.ds(index * block, block)
    outputs = []
    for head in range(heads):
        group = head // (heads // groups)
        scores = scores_of(
            keys_ref[group, :length, :], query_ref[head, span, :], index * block, length
        )
        peak = jnp.max(scores, axis=0, keepdims=True)
        raised = jnp.exp(scores - peak)
        total = jnp.sum(raised, axis=0, keepdims=True)
        probs = (raised * (1.0 / total)).astype(jnp.bfloat16)
        outputs.append(
            jnp.dot(
                flipped[group * HD : (group + 1) * HD, :length],
                probs,
                preferred_element_type=jnp.float32,
            )
        )
    out_ref[index] = jnp.concatenate(outputs, 0).T.astype(jnp.bfloat16)


def attend_kernel(rows_ref, weight_ref, normed_ref, query_ref, keys_ref, values_ref, out_ref, flipped):
    project_rows(rows_ref, weight_ref[...], normed_ref, query_ref, keys_ref, values_ref, flipped)
    for index in range(rows_ref.shape[0]):
        attend_rows(index, rows_ref.shape[1], query_ref, keys_ref, out_ref, flipped)


def attend_shapes(rows, heads, groups):
    blocks, block = rows[:2]
    length = blocks * block
    return (
        jax.ShapeDtypeStruct((length, D), jnp.bfloat16),
        jax.ShapeDtypeStruct((heads, length, HD), jnp.bfloat16),
        jax.ShapeDtypeStruct((groups, length, HD), jnp.bfloat16),
        jax.ShapeDtypeStruct((groups, length, HD), jnp.bfloat16),
        jax.ShapeDtypeStruct((blocks, block, heads * HD), jnp.bfloat16),
    )


def attend_back(rows_ref, query_ref, keys_ref, values_ref, grad_ref, out_ref, flipped, grad_keys, grad_values):
    block = 256
    blocks = rows_ref.shape[0] // block
    heads, groups = query_ref.shape[0], keys_ref.shape[0]
    repeat = heads // groups
    wide = heads * HD
    for group in range(groups):
        flipped[group * HD : (group + 1) * HD, :] = (
            keys_ref[group].astype(jnp.float32).T.astype(jnp.bfloat16)
        )
    grad_keys[...] = jnp.zeros_like(grad_keys)
    grad_values[...] = jnp.zeros_like(grad_values)
    for index in range(blocks):
        length = (index + 1) * block
        span = pl.ds(index * block, block)
        outputs = []
        for head in range(heads):
            group = head // repeat
            query = query_ref[head, span, :]
            grad = grad_ref[index, :, head * HD : (head + 1) * HD]
            scores = scores_of(keys_ref[group, :length, :], query, index * block, length)
            peak = jnp.max(scores, axis=0, keepdims=True)
            raised = jnp.exp(scores - peak)
            total = jnp.sum(raised, axis=0, keepdims=True)
            probs = raised * (1.0 / total)
            grad_probs = lax.dot_general(
                values_ref[group, :length, :],
                grad,
                (((1,), (1,)), ((), ())),
                preferred_element_type=jnp.float32,
            )
            middle = jnp.sum(probs * grad_probs, axis=0, keepdims=True)
            grad_scores = (probs * (grad_probs - middle)).astype(jnp.bfloat16)
            grad_keys[group, :length, :] += jnp.dot(
                grad_scores, query, preferred_element_type=jnp.float32
            )
            grad_values[group, :length, :] += jnp.dot(
                probs.astype(jnp.bfloat16), grad, preferred_element_type=jnp.float32
            )
            outputs.append(
                jnp.dot(
                    flipped[group * HD : (group + 1) * HD, :length],
                    grad_scores,
                    preferred_element_type=jnp.float32,
                )
            )
        tables = lane_tables(rows_ref[span, :])
        stacked = jnp.concatenate(outputs, 0).T * ATTN_SCALE
        for column in range(0, wide, 128):
            out_ref[span, column : column + 128] = turn_lanes(
                stacked[:, column : column + 128], tables, -1.0
            ).astype(jnp.bfloat16)
    for index in range(blocks):
        span = pl.ds(index * block, block)
        tables = lane_tables(rows_ref[span, :])
        keys = jnp.concatenate([grad_keys[group, span, :] for group in range(groups)], 1)
        values = jnp.concatenate([grad_values[group, span, :] for group in range(groups)], 1)
        keys = turn_lanes(keys * ATTN_SCALE, tables, -1.0)
        out_ref[span, wide : wide + groups * HD] = keys.astype(jnp.bfloat16)
        out_ref[span, wide + groups * HD :] = values.astype(jnp.bfloat16)


def attend_forward(rows, weight, heads, groups):
    return pl.pallas_call(
        attend_kernel,
        out_shape=attend_shapes(rows.shape, heads, groups),
        scratch_shapes=[pltpu.VMEM((groups * HD, rows.shape[0] * rows.shape[1]), jnp.bfloat16)],
        compiler_params=pltpu.CompilerParams(vmem_limit_bytes=48 * 1024 * 1024),
        cost_estimate=pl.CostEstimate(flops=1, bytes_accessed=1, transcendentals=0),
    )(rows, weight)


def attend_backward(table, query, keys, values, grad):
    heads, length = query.shape[:2]
    groups = keys.shape[0]
    return pl.pallas_call(
        attend_back,
        out_shape=jax.ShapeDtypeStruct((length, (heads + 2 * groups) * HD), jnp.bfloat16),
        scratch_shapes=[
            pltpu.VMEM((groups * HD, length), jnp.bfloat16),
            pltpu.VMEM((groups, length, HD), jnp.float32),
            pltpu.VMEM((groups, length, HD), jnp.float32),
        ],
        compiler_params=pltpu.CompilerParams(vmem_limit_bytes=48 * 1024 * 1024),
        cost_estimate=pl.CostEstimate(flops=1, bytes_accessed=1, transcendentals=0),
    )(table, query, keys, values, grad)


def dispatch_kernel(first_ref, rows_ref, grads_ref, out_rows, out_grads, out_pick):
    count = out_rows.shape[0]
    tokens = rows_ref.shape[1]
    padded = -(-count // 16) * 16
    tail = rows_ref[0, :, D:]
    lane = lax.broadcasted_iota(jnp.int32, (padded, 128), 1)
    row = lax.broadcasted_iota(jnp.int32, (padded, 128), 0)
    wanted = (lane == 2 * EXPERTS + first_ref[0] + row) & (row < count)
    marks = lax.dot_general(
        wanted.astype(jnp.bfloat16),
        tail,
        (((1,), (1,)), ((), ())),
        preferred_element_type=jnp.float32,
    )
    earlier = lax.broadcasted_iota(jnp.int32, (tokens, tokens), 0) < lax.broadcasted_iota(
        jnp.int32, (tokens, tokens), 1
    )
    rank = jnp.dot(
        marks.astype(jnp.bfloat16),
        earlier.astype(jnp.bfloat16),
        preferred_element_type=jnp.float32,
    )
    slot = lax.broadcasted_iota(jnp.int32, (CAP, tokens), 0).astype(jnp.float32)
    pick = jnp.concatenate(
        [
            jnp.where(
                rank[item : item + 1, :] == slot, marks[item : item + 1, :], 0.0
            ).astype(jnp.bfloat16)
            for item in range(count)
        ],
        0,
    )
    out_pick[0] = pick
    moved = jnp.dot(pick, rows_ref[0], preferred_element_type=jnp.float32).astype(jnp.bfloat16)
    moved_grads = jnp.dot(pick, grads_ref[0], preferred_element_type=jnp.float32).astype(
        jnp.bfloat16
    )
    for item in range(count):
        out_rows[item] = moved[item * CAP : (item + 1) * CAP]
        out_grads[item] = moved_grads[item * CAP : (item + 1) * CAP]


def dispatch(first, rows, grads, count):
    sources, tokens, wide = rows.shape
    return pl.pallas_call(
        dispatch_kernel,
        grid_spec=pltpu.PrefetchScalarGridSpec(
            num_scalar_prefetch=1,
            grid=(sources,),
            in_specs=[
                pl.BlockSpec((1, tokens, wide), lambda s, f: (s, 0, 0)),
                pl.BlockSpec((1, tokens, D), lambda s, f: (s, 0, 0)),
            ],
            out_specs=(
                pl.BlockSpec((count, CAP, wide), lambda s, f: (0, s, 0)),
                pl.BlockSpec((count, CAP, D), lambda s, f: (0, s, 0)),
                pl.BlockSpec((1, count * CAP, tokens), lambda s, f: (s, 0, 0)),
            ),
        ),
        out_shape=(
            jax.ShapeDtypeStruct((count, sources * CAP, wide), jnp.bfloat16),
            jax.ShapeDtypeStruct((count, sources * CAP, D), jnp.bfloat16),
            jax.ShapeDtypeStruct((sources, count * CAP, tokens), jnp.bfloat16),
        ),
        compiler_params=pltpu.CompilerParams(vmem_limit_bytes=62 * 1024 * 1024),
        cost_estimate=pl.CostEstimate(flops=1, bytes_accessed=1, transcendentals=0),
    )(first, rows, grads)


def combine_kernel(pick_ref, rows_ref, out_ref):
    rows = jnp.concatenate([rows_ref[item] for item in range(rows_ref.shape[0])], 0)
    out_ref[0] = lax.dot_general(
        pick_ref[0], rows, (((0,), (0,)), ((), ())), preferred_element_type=jnp.float32
    ).astype(jnp.bfloat16)


def combine(pick, rows):
    sources, slots, tokens = pick.shape
    count, _, wide = rows.shape
    return pl.pallas_call(
        combine_kernel,
        grid=(sources,),
        in_specs=[
            pl.BlockSpec((1, slots, tokens), lambda s: (s, 0, 0)),
            pl.BlockSpec((count, CAP, wide), lambda s: (0, s, 0)),
        ],
        out_specs=pl.BlockSpec((1, tokens, wide), lambda s: (s, 0, 0)),
        out_shape=jax.ShapeDtypeStruct((sources, tokens, wide), jnp.bfloat16),
        compiler_params=pltpu.CompilerParams(vmem_limit_bytes=62 * 1024 * 1024),
        cost_estimate=pl.CostEstimate(flops=1, bytes_accessed=1, transcendentals=0),
    )(pick, rows)


def expert_kernel(first_ref, order_ref, rows_ref, grads_ref, *refs):
    produced_ref, grad_rows_ref, grad_hidden_ref, gated_ref, whole_in, whole_out = refs[-6:]
    pieces = refs[:-6]
    expert = first_ref[0] + pl.program_id(0)

    @pl.when(pl.program_id(1) == 0)
    def assemble():
        if len(pieces[0].shape) == 3:
            whole_in[...] = pieces[0][0]
            whole_out[...] = pieces[1][0]
            return
        for index in range(pieces[0].shape[0]):
            block = order_ref[index]
            for piece, whole in zip(pieces, (whole_in, whole_out)):
                deep = piece.shape[2]
                whole[pl.ds(pl.multiple_of(block * deep, deep), deep), :] = piece[index, 0]

    tail = rows_ref[0, :, D:].astype(jnp.float32)
    lane = lax.broadcasted_iota(jnp.int32, tail.shape, 1)
    own = (lane == expert) | (lane == EXPERTS + expert)
    gate = jnp.sum(jnp.where(own, tail, 0.0), axis=-1, keepdims=True)
    hidden = whole_out.shape[0]
    gate_up = jnp.dot(rows_ref[0, :, :D], whole_in[...], preferred_element_type=jnp.float32)
    gate_half = gate_up[:, :hidden]
    up_half = gate_up[:, hidden:]
    sigma = 1.0 / (1.0 + jnp.exp(-gate_half))
    activated = gate_half * sigma
    middle = activated * up_half
    gated = (gate * middle).astype(jnp.bfloat16)
    gated_ref[0] = gated
    produced_ref[0] = jnp.dot(gated, whole_out[...], preferred_element_type=jnp.float32).astype(
        jnp.bfloat16
    )
    grad_middle = RESIDUAL_SCALE * lax.dot_general(
        grads_ref[0],
        whole_out[...],
        (((1,), (1,)), ((), ())),
        preferred_element_type=jnp.float32,
    )
    grad_gate = jnp.sum(middle * grad_middle, axis=-1, keepdims=True)
    grad_middle = gate * grad_middle
    slope = sigma * (1.0 + gate_half * (1.0 - sigma))
    grad_hidden = jnp.concatenate(
        [grad_middle * up_half * slope, grad_middle * activated], -1
    ).astype(jnp.bfloat16)
    grad_hidden_ref[0] = grad_hidden
    grad_rows_ref[0, :, :D] = lax.dot_general(
        grad_hidden,
        whole_in[...],
        (((1,), (1,)), ((), ())),
        preferred_element_type=jnp.float32,
    ).astype(jnp.bfloat16)
    high = grad_gate.astype(jnp.bfloat16).astype(jnp.float32)
    spread = jnp.where(
        lane == expert, high, jnp.where(lane == EXPERTS + expert, grad_gate - high, 0.0)
    )
    grad_rows_ref[0, :, D:] = spread.astype(jnp.bfloat16)


def run_experts(first, order, rows, grads, pieces, hidden):
    count, slots, wide = rows.shape
    chunk = min(512, slots)
    by_chunk = lambda e, c, *_: (e, c, 0)
    if len(pieces[0].shape) == 4:
        piece_specs = [
            pl.BlockSpec((piece.shape[0], 1) + piece.shape[2:], lambda e, c, *_: (0, e, 0, 0))
            for piece in pieces
        ]
    else:
        piece_specs = [
            pl.BlockSpec((1,) + piece.shape[1:], lambda e, c, *_: (e, 0, 0)) for piece in pieces
        ]
    return pl.pallas_call(
        expert_kernel,
        grid_spec=pltpu.PrefetchScalarGridSpec(
            num_scalar_prefetch=2,
            grid=(count, slots // chunk),
            in_specs=[
                pl.BlockSpec((1, chunk, wide), by_chunk),
                pl.BlockSpec((1, chunk, D), by_chunk),
            ]
            + piece_specs,
            out_specs=(
                pl.BlockSpec((1, chunk, D), by_chunk),
                pl.BlockSpec((1, chunk, wide), by_chunk),
                pl.BlockSpec((1, chunk, 2 * hidden), by_chunk),
                pl.BlockSpec((1, chunk, hidden), by_chunk),
            ),
            scratch_shapes=[
                pltpu.VMEM((D, 2 * hidden), jnp.bfloat16),
                pltpu.VMEM((hidden, D), jnp.bfloat16),
            ],
        ),
        out_shape=(
            jax.ShapeDtypeStruct((count, slots, D), jnp.bfloat16),
            jax.ShapeDtypeStruct((count, slots, wide), jnp.bfloat16),
            jax.ShapeDtypeStruct((count, slots, 2 * hidden), jnp.bfloat16),
            jax.ShapeDtypeStruct((count, slots, hidden), jnp.bfloat16),
        ),
        compiler_params=pltpu.CompilerParams(vmem_limit_bytes=62 * 1024 * 1024),
        cost_estimate=pl.CostEstimate(flops=1, bytes_accessed=1, transcendentals=0),
    )(first, order, rows, grads, *pieces)


def weight_grad_kernel(order_ref, rows_ref, grads_ref, hidden_ref, gated_ref, *refs):
    outs, total_in, total_out = refs[:-2], refs[-2], refs[-1]
    chunk = pl.program_id(1)
    part_in = lax.dot_general(
        rows_ref[0, :, :D],
        hidden_ref[0],
        (((0,), (0,)), ((), ())),
        preferred_element_type=jnp.float32,
    )
    part_out = RESIDUAL_SCALE * lax.dot_general(
        gated_ref[0],
        grads_ref[0],
        (((0,), (0,)), ((), ())),
        preferred_element_type=jnp.float32,
    )

    @pl.when(chunk == 0)
    def store():
        total_in[...] = part_in
        total_out[...] = part_out

    @pl.when(chunk > 0)
    def add():
        total_in[...] += part_in
        total_out[...] += part_out

    @pl.when(chunk == pl.num_programs(1) - 1)
    def finish():
        if len(outs) == 2:
            outs[0][0] = total_in[...].astype(jnp.bfloat16)
            outs[1][0] = total_out[...].astype(jnp.bfloat16)
            return
        wide = total_in.shape[1]
        turns = outs[0].shape[0]
        deep = outs[0].shape[2]
        folds = (outs[0].shape[3] - D) // wide
        for number, out in enumerate(outs):
            for turn in range(turns):
                block = order_ref[number * turns + turn]
                for fold in range(folds):
                    start = pl.multiple_of((block * folds + fold) * deep, deep)
                    out[turn, 0, :, fold * wide : (fold + 1) * wide] = total_in[
                        pl.ds(start, deep), :
                    ].astype(jnp.bfloat16)
                start = pl.multiple_of(block * deep, deep)
                out[turn, 0, :, folds * wide :] = total_out[pl.ds(start, deep), :].astype(
                    jnp.bfloat16
                )


def weight_grads(order, rows, grads, grad_hidden, gated, shapes):
    count, slots, wide = rows.shape
    hidden = gated.shape[2]
    chunk = min(512, slots)
    by_chunk = lambda e, c, *_: (e, c, 0)
    if len(shapes) == 2:
        out_specs = tuple(pl.BlockSpec((1,) + s[1:], lambda e, c, *_: (e, 0, 0)) for s in shapes)
    else:
        out_specs = tuple(
            pl.BlockSpec((s[0], 1) + s[2:], lambda e, c, *_: (0, e, 0, 0)) for s in shapes
        )
    return pl.pallas_call(
        weight_grad_kernel,
        grid_spec=pltpu.PrefetchScalarGridSpec(
            num_scalar_prefetch=1,
            grid=(count, slots // chunk),
            in_specs=[
                pl.BlockSpec((1, chunk, wide), by_chunk),
                pl.BlockSpec((1, chunk, D), by_chunk),
                pl.BlockSpec((1, chunk, 2 * hidden), by_chunk),
                pl.BlockSpec((1, chunk, hidden), by_chunk),
            ],
            out_specs=out_specs,
            scratch_shapes=[
                pltpu.VMEM((D, 2 * hidden), jnp.float32),
                pltpu.VMEM((hidden, D), jnp.float32),
            ],
        ),
        out_shape=tuple(jax.ShapeDtypeStruct(s, jnp.bfloat16) for s in shapes),
        compiler_params=pltpu.CompilerParams(vmem_limit_bytes=62 * 1024 * 1024),
        cost_estimate=pl.CostEstimate(flops=1, bytes_accessed=1, transcendentals=0),
    )(order, rows, grads, grad_hidden, gated)


def swap(rows, axis, flip):
    size = lax.axis_size(axis)
    return lax.ppermute(rows, axis, [(i, i ^ flip) for i in range(size)])


def near(place, axis, flip):
    if lax.axis_size(axis) == 2:
        return 1 - place
    if flip == 1:
        return place + 1 - 2 * lax.rem(place, 2)
    if flip == 2:
        return lax.rem(place + 2, 4)
    return 3 - place


def greet(partners):
    barrier = pltpu.get_barrier_semaphore()
    for axis, flip in partners:
        pl.semaphore_signal(
            barrier,
            inc=1,
            device_id={axis: near(lax.axis_index(axis), axis, flip)},
            device_id_type=pl.DeviceIdType.MESH,
        )
    pl.semaphore_wait(barrier, len(partners))


class Link:
    def __init__(self, sends, receives):
        self.sends, self.receives, self.used, self.started = sends, receives, 0, []

    def push(self, source, target, axis, flip):
        copy = pltpu.make_async_remote_copy(
            src_ref=source,
            dst_ref=target,
            send_sem=self.sends.at[self.used],
            recv_sem=self.receives.at[self.used],
            device_id={axis: near(lax.axis_index(axis), axis, flip)},
            device_id_type=pl.DeviceIdType.MESH,
        )
        copy.start()
        self.used += 1
        self.started.append(copy)
        return copy

    def finish(self):
        for copy in self.started:
            copy.wait_send()


class Line:
    def __init__(self, rows_ref, out_ref, sends, receives):
        z, y = lax.axis_index("dp"), lax.axis_index("expert")
        self.inner = z * (3 - z) > 0
        self.outer = z * (3 - z) < 1

        def slot(flip):
            return 2 * (near(z, "dp", flip) if flip else z) + y

        def hand(sent, received, source, target, flip, axis="dp"):
            return pltpu.make_async_remote_copy(
                src_ref=source,
                dst_ref=target,
                send_sem=sends.at[sent],
                recv_sem=receives.at[received],
                device_id={axis: near(lax.axis_index(axis), axis, flip)},
                device_id_type=pl.DeviceIdType.MESH,
            )

        def block(flip):
            return out_ref.at[slot(flip)]

        self.to_first = hand(0, 1, rows_ref, block(0), 1)
        self.across_own = hand(1, 3, rows_ref, block(0), 3)
        self.across_first = hand(2, 2, block(1), block(1), 3)
        self.pass_third = hand(3, 2, block(3), block(3), 1)
        self.pass_second = hand(8, 3, block(2), block(2), 1)
        self.over = [
            hand(4 + flip, 4 + flip, block(flip) if flip else rows_ref, block(flip), 1, "expert")
            for flip in range(4)
        ]
        self.got = [None] + [hand(0, flip, block(flip), block(flip), 1) for flip in range(1, 4)]
        self.got_over = [
            hand(0, 4 + flip, block(flip), out_ref.at[slot(flip) + 1 - 2 * y], 1, "expert")
            for flip in range(4)
        ]

    def start(self):
        self.to_first.start()

        @pl.when(self.inner)
        def inner():
            self.across_own.start()

        self.over[0].start()

    def first(self):
        self.got[1].wait_recv()

        @pl.when(self.inner)
        def inner():
            self.across_first.start()

        self.over[1].start()

    def second(self):
        @pl.when(self.inner)
        def inner():
            self.got[3].wait_recv()
            self.pass_third.start()
            self.over[3].start()

        @pl.when(self.outer)
        def outer():
            self.got[2].wait_recv()
            self.over[2].start()

    def third(self):
        @pl.when(self.inner)
        def inner():
            self.got[2].wait_recv()
            self.pass_second.start()
            self.over[2].start()

        @pl.when(self.outer)
        def outer():
            self.got[3].wait_recv()
            self.over[3].start()

    def finish(self):
        self.to_first.wait_send()

        @pl.when(self.inner)
        def inner():
            for copy in (self.across_own, self.across_first, self.pass_third, self.pass_second):
                copy.wait_send()

        for copy in self.over:
            copy.wait_send()
        for copy in self.got_over:
            copy.wait_recv()


class Fold:
    def __init__(self, blocks_ref, out_ref, over, sums, parts, sends, receives):
        z, y = lax.axis_index("dp"), lax.axis_index("expert")
        self.inner = z * (3 - z) > 0
        self.outer = z * (3 - z) < 1
        self.blocks, self.out, self.over, self.sums, self.parts = blocks_ref, out_ref, over, sums, parts
        self.y = y

        def slot(flip, plane):
            return 2 * (near(z, "dp", flip) if flip else z) + plane

        def hand(number, source, target, flip, axis="dp"):
            return pltpu.make_async_remote_copy(
                src_ref=source,
                dst_ref=target,
                send_sem=sends.at[number],
                recv_sem=receives.at[number],
                device_id={axis: near(lax.axis_index(axis), axis, flip)},
                device_id_type=pl.DeviceIdType.MESH,
            )

        self.slot = slot
        self.across = [
            hand(flip, blocks_ref.at[slot(flip, 1 - y)], over.at[flip], 1, "expert")
            for flip in range(4)
        ]
        self.to_line = [hand(4 + k, sums.at[3 - k], parts.at[k], 1) for k in range(3)]
        self.to_middle = [hand(7 + k, sums.at[2 + k], parts.at[3 + k], 3) for k in range(2)]
        self.to_end = hand(9, sums.at[1], parts.at[5], 1)

    def own(self, flip):
        self.across[flip].wait_recv()
        return self.blocks[self.slot(flip, self.y)].astype(jnp.float32) + self.over[flip].astype(
            jnp.float32
        )

    def part(self, number):
        return self.parts[number].astype(jnp.float32)

    def start(self):
        @pl.when(self.inner)
        def inner():
            for flip in (2, 3, 1, 0):
                self.across[flip].start()

        @pl.when(self.outer)
        def outer():
            for flip in (3, 2, 1, 0):
                self.across[flip].start()

    def early(self, k):
        @pl.when(self.inner)
        def inner():
            total = self.own(2 + k)
            self.to_line[k].wait_recv()
            self.sums[2 + k] = (total + self.part(k)).astype(jnp.bfloat16)
            self.to_middle[k].start()

        @pl.when(self.outer)
        def outer():
            self.sums[3 - k] = self.own(3 - k).astype(jnp.bfloat16)
            self.to_line[k].start()

    def late(self):
        @pl.when(self.inner)
        def inner():
            total = self.own(1)
            self.to_middle[0].wait_recv()
            self.sums[1] = (total + self.part(3)).astype(jnp.bfloat16)
            self.to_end.start()

        @pl.when(self.outer)
        def outer():
            self.sums[1] = self.own(1).astype(jnp.bfloat16)
            self.to_line[2].start()

    def last(self):
        @pl.when(self.inner)
        def inner():
            total = self.own(0)
            self.to_line[2].wait_recv()
            self.to_middle[1].wait_recv()
            self.out[...] = (total + self.part(2) + self.part(4)).astype(self.out.dtype)

        @pl.when(self.outer)
        def outer():
            total = self.own(0)
            self.to_end.wait_recv()
            self.out[...] = (total + self.part(5)).astype(self.out.dtype)

    def finish(self):
        @pl.when(self.inner)
        def inner():
            for copy in self.to_middle + [self.to_end]:
                copy.wait_send()

        @pl.when(self.outer)
        def outer():
            for copy in self.to_line:
                copy.wait_send()

        for copy in self.across:
            copy.wait_send()


def fold_scratch(shape):
    return [
        pltpu.VMEM((4,) + shape, jnp.bfloat16),
        pltpu.VMEM((4,) + shape, jnp.bfloat16),
        pltpu.VMEM((6,) + shape, jnp.bfloat16),
        pltpu.SemaphoreType.DMA((10,)),
        pltpu.SemaphoreType.DMA((10,)),
    ]


def add_into(target, sources):
    def body(item, carry):
        total = sources[0][item].astype(jnp.float32)
        for source in sources[1:]:
            total = total + source[item].astype(jnp.float32)
        target[item] = total.astype(jnp.bfloat16)
        return carry

    lax.fori_loop(0, target.shape[0], body, 0)


def fetch(pairs, local):
    copies = [
        pltpu.make_async_copy(source, target, local.at[number])
        for number, (source, target) in enumerate(pairs)
    ]
    for copy in copies:
        copy.start()
    for copy in copies:
        copy.wait()


EVERYONE = [("dp", 1), ("dp", 2), ("dp", 3), ("expert", 1), ("ctx", 1), ("ctx", 2), ("ctx", 3)]


def returning_kernel(
    blocks_ref, give3, keep3, give2, keep2, give1, keep1, give0,
    after_ref, input_ref, gates_ref, grad_ref, gain_ref, pack_ref, attended_ref,
    grad_after_ref, seq_grad_ref, grad_pack_ref, arrived, done3, ready2, ready1,
    routed, over, sums, parts, fold_sends, fold_receives,
    sent, crossed, stage, outgoing, sends, receives, local,
):
    z, c = lax.axis_index("dp"), lax.axis_index("ctx")
    greet(EVERYONE)
    link = Link(sends, receives)
    fold = Fold(blocks_ref, routed, over, sums, parts, fold_sends, fold_receives)
    gives = {3: give3, 2: give2, 1: give1, 0: give0}
    keeps = {3: keep3, 2: keep2, 1: keep1}
    core = {step: link.push(gives[step], arrived.at[step], "ctx", 1) for step in (3, 2, 1, 0)}
    fold.start()
    pair = {}
    count = stage.shape[1]

    def cross(step, cut):
        core[step].wait_recv()
        fetch([(keeps[step].at[1], stage.at[0]), (arrived.at[step, 1], stage.at[1])], local)
        add_into(sent.at[step - 1], [stage.at[0], stage.at[1]])
        source, target = sent.at[step - 1], crossed.at[step - 1]
        if cut:
            pair[step] = [
                link.push(source.at[item], target.at[item], "ctx", 2) for item in range(count)
            ]
        else:
            pair[step] = [link.push(source, target, "ctx", 2)]

    def close(step):
        fetch([(keeps[step].at[0], stage.at[2]), (arrived.at[step, 0], stage.at[3])], local)
        for copy in pair[step]:
            copy.wait_recv()
            copy.wait_send()
        add_into(sent.at[step - 1], [stage.at[2], stage.at[3], crossed.at[step - 1]])

    line = []

    def close_one(item):
        pair[3][item].wait_recv()
        pair[3][item].wait_send()
        sent[2, item] = (
            stage[2, item].astype(jnp.float32)
            + stage[3, item].astype(jnp.float32)
            + crossed[2, item].astype(jnp.float32)
        ).astype(jnp.bfloat16)
        line.append(link.push(sent.at[2, item], done3.at[item], "dp", 3))

    cross(3, True)
    fetch([(keep3.at[0], stage.at[2]), (arrived.at[3, 0], stage.at[3])], local)
    close_one(0)
    fold.early(0)
    close_one(1)
    cross(2, False)
    close_one(2)
    fold.early(1)
    for item in range(3, count):
        close_one(item)
    cross(1, False)
    fold.late()
    fold.last()

    gates = gates_ref[...]
    high = routed[:, D:]
    lane = lax.broadcasted_iota(jnp.int32, high.shape, 1)
    grad_gates = jnp.where(lane < EXPERTS, high + pltpu.roll(high, 128 - EXPERTS, 1), 0.0)
    grad_picked = gates * (grad_gates - jnp.sum(gates * grad_gates, axis=-1, keepdims=True))
    grad_logits = grad_picked.astype(jnp.bfloat16)
    grad_input = routed[:, :D] + lax.dot_general(
        grad_logits,
        pack_ref[:, D:],
        (((1,), (1,)), ((), ())),
        preferred_element_type=jnp.float32,
    )
    normed, factor = normalize(after_ref[...])
    grad_after = grad_ref[...].astype(jnp.float32) + norm_back(
        grad_input * gain_ref[...], normed, factor
    )
    grad_after_ref[...] = grad_after
    grad_branch = (RESIDUAL_SCALE * grad_after).astype(jnp.bfloat16)
    wide = outgoing.shape[2]
    for index in range(outgoing.shape[0]):
        outgoing[index] = lax.dot_general(
            grad_branch,
            pack_ref[index * wide : (index + 1) * wide, :D],
            (((1,), (1,)), ((), ())),
            preferred_element_type=jnp.float32,
        ).astype(jnp.bfloat16)
    seq_grad_ref[c] = outgoing[c]
    spread = [
        link.push(outgoing.at[near(c, "ctx", flip)], seq_grad_ref.at[c], "ctx", flip)
        for flip in (1, 2, 3)
    ]
    close(2)
    keep_ready = [pltpu.make_async_copy(sent.at[1], ready2, local.at[0])]
    keep_ready[0].start()
    turned = (((0,), (0,)), ((), ()))
    column = (lane == EXPERTS).astype(jnp.bfloat16)
    small = lax.dot_general(
        input_ref[...], grad_logits, turned, preferred_element_type=jnp.float32
    ) + lax.dot_general(
        (grad_input * normed).astype(jnp.bfloat16),
        column,
        turned,
        preferred_element_type=jnp.float32,
    )
    small = small.astype(jnp.bfloat16).reshape(grad_pack_ref.shape[:3] + (128,))
    grad_pack_ref[..., D:] = small
    some = grad_pack_ref.shape[0] // outgoing.shape[0]
    for index in range(outgoing.shape[0]):
        part = lax.dot_general(
            attended_ref[index], grad_branch, turned, preferred_element_type=jnp.float32
        ).astype(jnp.bfloat16)
        grad_pack_ref[index * some : (index + 1) * some, :, :, :D] = part.reshape(
            (some,) + grad_pack_ref.shape[1:3] + (D,)
        )
    keep_ready[0].wait()
    close(1)
    fetch([(sent.at[0], ready1)], local)
    for copy in spread + line + [core[0]]:
        copy.wait_recv()
    fold.finish()
    for copy in list(core.values()) + spread + line:
        copy.wait_send()


def returning(blocks, parts, after, expert_input, gates, grads, gain, pack, attended, number):
    kind = jnp.bfloat16
    far = pl.BlockSpec(memory_space=pl.ANY)
    held = pl.BlockSpec(memory_space=pltpu.VMEM)
    give3, keep3, give2, keep2, give1, keep1, give0, _ = parts
    piece = give3.shape[1:]
    ctx, tokens, wide = attended.shape
    shape = blocks.shape[1:]
    return pl.pallas_call(
        returning_kernel,
        out_shape=(
            jax.ShapeDtypeStruct((tokens, D), jnp.float32),
            jax.ShapeDtypeStruct(attended.shape, kind),
            jax.ShapeDtypeStruct((8, ctx, D // (8 * ctx), shape[1]), kind),
            jax.ShapeDtypeStruct((4,) + give3.shape, kind),
            jax.ShapeDtypeStruct(piece, kind),
            jax.ShapeDtypeStruct(piece, kind),
            jax.ShapeDtypeStruct(piece, kind),
        ),
        in_specs=[held] + [far] * 7 + [held] * 7,
        out_specs=(held, held, held, far, far, far, far),
        scratch_shapes=[pltpu.VMEM(shape, jnp.float32)]
        + fold_scratch(shape)
        + [
            pltpu.VMEM((3,) + piece, kind),
            pltpu.VMEM((3,) + piece, kind),
            pltpu.VMEM((4,) + piece, kind),
            pltpu.VMEM(attended.shape, kind),
            pltpu.SemaphoreType.DMA((9 + 2 * piece[0],)),
            pltpu.SemaphoreType.DMA((9 + 2 * piece[0],)),
            pltpu.SemaphoreType.DMA((2,)),
        ],
        compiler_params=pltpu.CompilerParams(
            collective_id=number, has_side_effects=True, vmem_limit_bytes=62 * 1024 * 1024
        ),
    )(
        blocks, give3, keep3, give2, keep2, give1, keep1, give0,
        after, expert_input, gates, grads, gain, pack, attended,
    )


def closing_kernel(
    ready2, ready1, keep0, arrived, table_ref, query_ref, keys_ref, values_ref, seq_grad_ref,
    normed_ref, columns_ref, grad_pack_ref, rows_ref, grad_after_ref,
    done2, done1, done0, input_grad_ref, shard_columns_ref, shard_pack_ref,
    sent, crossed, stage, mixed, flipped, grad_keys, grad_values,
    pack_core, pack_pair, pack_sent, pack_blocks, pack_over, pack_sums, pack_parts, pack_sends, pack_receives,
    scaled, scaled_core, scaled_pair, scaled_sent,
    part_blocks, part_out, part_over, part_sums, part_parts, part_sends, part_receives,
    sends, receives, local,
):
    z, c = lax.axis_index("dp"), lax.axis_index("ctx")
    greet(EVERYONE)
    link = Link(sends, receives)

    def c_at(flip):
        return near(c, "ctx", flip) if flip else c

    to_core = [
        link.push(grad_pack_ref.at[:, c_at(flip)], pack_core.at[number], "ctx", 1)
        for number, flip in enumerate((3, 1))
    ]
    line = [link.push(ready2, done2, "dp", 2), link.push(ready1, done1, "dp", 1)]
    zones = grad_pack_ref.shape[0]
    to_core[0].wait_recv()
    for zone in range(zones):
        pack_sent[zone] = (
            grad_pack_ref[zone, c_at(2)].astype(jnp.float32)
            + pack_core[0, zone].astype(jnp.float32)
        ).astype(jnp.bfloat16)
    pack_over_pair = link.push(pack_sent, pack_pair, "ctx", 2)
    fetch([(keep0.at[1], stage.at[0]), (arrived.at[0, 1], stage.at[1])], local)
    add_into(sent, [stage.at[0], stage.at[1]])
    pair = link.push(sent, crossed, "ctx", 2)
    attend_back(
        table_ref, query_ref, keys_ref, values_ref, seq_grad_ref, mixed, flipped, grad_keys, grad_values
    )
    blocks, block = scaled.shape[:2]
    for index in range(blocks):
        scaled[index] = lax.dot_general(
            mixed[index * block : (index + 1) * block, :],
            columns_ref[...],
            (((1,), (1,)), ((), ())),
            preferred_element_type=jnp.float32,
        ).astype(jnp.bfloat16)
    scaled_to_core = [
        link.push(scaled.at[c_at(flip)], scaled_core.at[number], "ctx", 1)
        for number, flip in enumerate((3, 1))
    ]
    wide = normed_ref.shape[1] // blocks
    some = zones // blocks
    for index in range(blocks):
        part = lax.dot_general(
            normed_ref[:, index * wide : (index + 1) * wide],
            mixed[...],
            (((0,), (0,)), ((), ())),
            preferred_element_type=jnp.float32,
        ).astype(jnp.bfloat16)
        part_blocks[index * some : (index + 1) * some] = part.reshape(
            (some,) + part_blocks.shape[1:]
        )
    part_fold = Fold(
        part_blocks, part_out, part_over, part_sums, part_parts, part_sends, part_receives
    )
    part_fold.start()
    scaled_to_core[0].wait_recv()
    scaled_sent[...] = (
        scaled[c_at(2)].astype(jnp.float32) + scaled_core[0].astype(jnp.float32)
    ).astype(jnp.bfloat16)
    scaled_over_pair = link.push(scaled_sent, scaled_pair, "ctx", 2)
    to_core[1].wait_recv()
    pack_over_pair.wait_recv()
    for zone in range(zones):
        pack_blocks[zone] = (
            grad_pack_ref[zone, c].astype(jnp.float32)
            + pack_core[1, zone].astype(jnp.float32)
            + pack_pair[zone].astype(jnp.float32)
        ).astype(jnp.bfloat16)
    pack_fold = Fold(
        pack_blocks, shard_pack_ref, pack_over, pack_sums, pack_parts, pack_sends, pack_receives
    )
    pack_fold.start()
    part_fold.early(0)
    part_fold.early(1)
    pack_fold.early(0)
    pack_fold.early(1)
    part_fold.late()
    part_fold.last()
    apart = [
        link.push(part_out.at[c_at(flip)], shard_columns_ref.at[c], "ctx", flip)
        for flip in (1, 2, 3)
    ]
    shard_columns_ref[c] = part_out[c]
    scaled_to_core[1].wait_recv()
    scaled_over_pair.wait_recv()
    grad_normed = (
        scaled[c].astype(jnp.float32)
        + scaled_core[1].astype(jnp.float32)
        + scaled_pair[...].astype(jnp.float32)
    )
    normed, factor = normalize(rows_ref[...].astype(jnp.float32))
    input_grad_ref[...] = grad_after_ref[...] + norm_back(grad_normed, normed, factor)
    pack_fold.late()
    pack_fold.last()
    fetch([(keep0.at[0], stage.at[0]), (arrived.at[0, 0], stage.at[1])], local)
    pair.wait_recv()
    pair.wait_send()
    add_into(sent, [stage.at[0], stage.at[1], crossed])
    fetch([(sent, done0)], local)
    for copy in apart + line:
        copy.wait_recv()
    part_fold.finish()
    pack_fold.finish()
    for copy in link.started:
        if copy is not pair:
            copy.wait_send()


def closing(
    ready2, ready1, keep0, arrived, table, query, keys, values, seq_grad, normed, columns,
    grad_pack, rows, grad_after, number,
):
    kind = jnp.bfloat16
    far = pl.BlockSpec(memory_space=pl.ANY)
    held = pl.BlockSpec(memory_space=pltpu.VMEM)
    piece = ready2.shape
    heads, length = query.shape[:2]
    groups = keys.shape[0]
    zones, ctx, share, wide = grad_pack.shape
    width = columns.shape[1]
    pack = (zones, share, wide)
    block = (length // ctx, D)
    part = (ctx, share, width)
    return pl.pallas_call(
        closing_kernel,
        out_shape=(
            jax.ShapeDtypeStruct(piece, kind),
            jax.ShapeDtypeStruct(piece, kind),
            jax.ShapeDtypeStruct(piece, kind),
            jax.ShapeDtypeStruct(rows.shape, jnp.float32),
            jax.ShapeDtypeStruct(part, kind),
            jax.ShapeDtypeStruct((share, wide), jnp.float32),
        ),
        in_specs=[far] * 4 + [held] * 10,
        out_specs=(far, far, far, held, held, held),
        scratch_shapes=[
            pltpu.VMEM(piece, kind),
            pltpu.VMEM(piece, kind),
            pltpu.VMEM((2,) + piece, kind),
            pltpu.VMEM((length, width), kind),
            pltpu.VMEM((groups * HD, length), kind),
            pltpu.VMEM((groups, length, HD), jnp.float32),
            pltpu.VMEM((groups, length, HD), jnp.float32),
            pltpu.VMEM((2,) + pack, kind),
            pltpu.VMEM(pack, kind),
            pltpu.VMEM(pack, kind),
            pltpu.VMEM(pack, kind),
        ]
        + fold_scratch(pack[1:])
        + [
            pltpu.VMEM((ctx,) + block, kind),
            pltpu.VMEM((2,) + block, kind),
            pltpu.VMEM(block, kind),
            pltpu.VMEM(block, kind),
            pltpu.VMEM((zones,) + part, kind),
            pltpu.VMEM(part, kind),
        ]
        + fold_scratch(part)
        + [
            pltpu.SemaphoreType.DMA((12,)),
            pltpu.SemaphoreType.DMA((12,)),
            pltpu.SemaphoreType.DMA((2,)),
        ],
        compiler_params=pltpu.CompilerParams(
            collective_id=number, has_side_effects=True, vmem_limit_bytes=62 * 1024 * 1024
        ),
    )(
        ready2, ready1, keep0, arrived, table, query, keys, values, seq_grad, normed, columns,
        grad_pack, rows, grad_after,
    )


def route_rows(rows, pack_ref, attended_ref, routes_ref, after_ref, gates_ref, gain_ref, packed):
    quarters = attended_ref.shape[0]
    wide = pack_ref.shape[-1]
    branch = jnp.zeros((rows.shape[0], D), jnp.float32)
    tails = []
    for index in range(quarters):
        pack = pack_ref[index].reshape(-1, wide)
        branch += jnp.dot(attended_ref[index], pack[:, :D], preferred_element_type=jnp.float32)
        tails.append(pack[:, D:])
    tail = jnp.concatenate(tails, 0)
    after = rows.astype(jnp.float32) + RESIDUAL_SCALE * branch
    after_ref[...] = after
    normed, _ = normalize(after)
    single = lax.broadcasted_iota(jnp.int32, (8, 128), 1) == EXPERTS
    gain = lax.dot_general(
        single.astype(jnp.bfloat16),
        tail,
        (((1,), (1,)), ((), ())),
        preferred_element_type=jnp.float32,
    )[:1]
    gain_ref[...] = gain
    expert_input = (normed * gain).astype(jnp.bfloat16)
    logits = jnp.dot(expert_input, tail, preferred_element_type=jnp.float32)
    lane = lax.broadcasted_iota(jnp.int32, logits.shape, 1)
    marks = jnp.zeros(logits.shape, jnp.float32)
    for index in range(TOP):
        marks = jnp.where(lane == routes_ref[:, index : index + 1], 1.0, marks)
    chosen = marks > 0.0
    peak = jnp.max(jnp.where(chosen, logits, -3e38), axis=-1, keepdims=True)
    raised = jnp.where(chosen, jnp.exp(jnp.where(chosen, logits - peak, 0.0)), 0.0)
    gates = raised / jnp.sum(raised, axis=-1, keepdims=True)
    gates_ref[...] = gates
    high = gates.astype(jnp.bfloat16).astype(jnp.float32)
    packed[:, :D] = expert_input
    packed[:, D:] = (
        high + pltpu.roll(gates - high, EXPERTS, 1) + pltpu.roll(marks, 2 * EXPERTS, 1)
    ).astype(jnp.bfloat16)


def opening_kernel(
    rows_ref, columns_ref, pack_ref, weights_in, weights_out, grads_ref, routes_ref,
    all_rows, all_columns, all_pack, pieces_in, pieces_out, all_grads, all_packed,
    after_ref, gates_ref, gain_ref, packed,
    normed_ref, query_ref, keys_ref, values_ref, attended_ref,
    outgoing, flipped, sends, receives, line_sends, line_receives, token_sends, token_receives, locals_,
):
    z, y, c = lax.axis_index("dp"), lax.axis_index("expert"), lax.axis_index("ctx")
    greet(EVERYONE)
    link = Link(sends, receives)
    line = Line(grads_ref, all_grads, line_sends, line_receives)
    token_line = Line(packed, all_packed, token_sends, token_receives)
    own = 2 * z + y
    count = weights_in.shape[1]

    def z_at(flip):
        return near(z, "dp", flip) if flip else z

    def c_at(flip):
        return near(c, "ctx", flip) if flip else c

    def keep(number, source, target):
        copy = pltpu.make_async_copy(source, target, locals_.at[number])
        copy.start()
        return copy

    def both(target, source, axis, flip):
        return [link.push(source(ref), target(ref), axis, flip) for ref in (pieces_in, pieces_out)]

    def share(*place):
        step, rest = place[0], place[1:]
        source = lambda ref: ref.at[(step, 0) + rest]
        over = both(lambda ref: ref.at[(step, 2) + rest], source, "ctx", 2)
        core = both(lambda ref: ref.at[(step, 1) + rest], source, "ctx", 1)
        return over, core

    def hand_on(*place):
        step, rest = place[0], place[1:]
        return both(
            lambda ref: ref.at[(step, 3) + rest], lambda ref: ref.at[(step, 2) + rest], "ctx", 1
        )

    def move(step, *rest):
        return [
            link.push(weights.at[(z_at(step),) + rest], ref.at[(step, 0) + rest], "dp", step)
            for weights, ref in ((weights_in, pieces_in), (weights_out, pieces_out))
        ]

    def arrive(copies):
        for copy in copies:
            copy.wait_recv()

    kept = [
        keep(0, columns_ref.at[c], all_columns.at[own, c]),
        keep(1, weights_in.at[z], pieces_in.at[0, 0]),
        keep(2, weights_out.at[z], pieces_out.at[0, 0]),
        keep(3, rows_ref, all_rows.at[c]),
        keep(4, pack_ref, all_pack.at[z, y, c]),
        keep(5, grads_ref, all_grads.at[own]),
    ]
    cut = [
        link.push(columns_ref.at[c_at(flip)], all_columns.at[own, c], "ctx", flip)
        for flip in (1, 2, 3)
    ]
    rows_over = link.push(rows_ref, all_rows.at[c], "ctx", 2)
    rows_core = link.push(rows_ref, all_rows.at[c], "ctx", 1)
    pack_line = [link.push(pack_ref, all_pack.at[z, y, c], "dp", flip) for flip in (1, 2, 3)]
    kept[0].wait()
    arrive(cut)
    column_line = [
        link.push(all_columns.at[own], all_columns.at[own], "dp", flip) for flip in (1, 2, 3)
    ]
    column_over = [link.push(all_columns.at[own], all_columns.at[own], "expert", 1)]
    kept[1].wait()
    kept[2].wait()
    rows_over.wait_recv()
    rows_pass = link.push(all_rows.at[c_at(2)], all_rows.at[c_at(2)], "ctx", 1)
    shared = [share(0)]
    arrive(pack_line)
    kept[4].wait()
    pack_over = link.push(all_pack.at[:, y, c], all_pack.at[:, y, c], "expert", 1)
    for flip in (1, 2, 3):
        column_line[flip - 1].wait_recv()
        block = all_columns.at[2 * z_at(flip) + y]
        column_over.append(link.push(block, block, "expert", 1))
    moved = {1: move(1), 2: move(2)}
    line.start()
    arrive([pack_over])
    pack_pair = link.push(all_pack.at[:, :, c], all_pack.at[:, :, c], "ctx", 2)
    pack_core = link.push(all_pack.at[:, :, c], all_pack.at[:, :, c], "ctx", 1)
    arrive([rows_core, rows_pass] + column_over)
    kept[3].wait()
    project_rows(
        all_rows,
        all_columns[...].reshape(D, all_columns.shape[-1]),
        normed_ref,
        query_ref,
        keys_ref,
        values_ref,
        flipped,
    )
    for index in range(all_rows.shape[0]):
        attend_rows(index, all_rows.shape[1], query_ref, keys_ref, outgoing, flipped)
    attended = [
        link.push(outgoing.at[c_at(flip)], attended_ref.at[c], "ctx", flip) for flip in (1, 2, 3)
    ]
    attended_ref[c] = outgoing[c]
    line.first()
    arrive([pack_pair])
    pack_last = link.push(all_pack.at[:, :, c_at(2)], all_pack.at[:, :, c_at(2)], "ctx", 1)
    arrive(shared[0][0])
    passed = hand_on(0)
    arrive([pack_core, pack_last] + attended)
    route_rows(
        all_rows[c, :, :D], all_pack, attended_ref, routes_ref, after_ref, gates_ref, gain_ref, packed
    )
    token_line.start()
    kept.append(keep(6, packed, all_packed.at[own]))
    arrive(moved[1])
    shared.append(share(1))
    line.second()
    token_line.first()
    line.third()
    token_line.second()
    arrive(moved[2])
    shared.append(share(2))
    last = [move(3, 0), move(3, 1)]
    token_line.third()
    arrive(shared[1][0])
    passed += hand_on(1)

    def next_piece(item):
        arrive(last[item])
        if item + 2 < count:
            last.append(move(3, item + 2))
        shared.append(share(3, item))

    for item in range(count):
        next_piece(item)
    arrive(shared[2][0])
    passed += hand_on(2)
    for item in range(count):
        arrive(shared[3 + item][0])
        passed += hand_on(3, item)
    kept[5].wait()
    kept[6].wait()
    arrive(passed)
    for over, core in shared:
        arrive(core)
    line.finish()
    token_line.finish()
    link.finish()


def opening(rows, columns, pack, weights_in, weights_out, grads, routes, heads, groups, number):
    ctx = columns.shape[0]
    shards, count = weights_in.shape[:2]
    tokens = rows.shape[0]
    kind = jnp.bfloat16
    copies = 24 + 2 * (2 + 3 * 3 + 5 * count)
    far = pl.BlockSpec(memory_space=pl.ANY)
    held = pl.BlockSpec(memory_space=pltpu.VMEM)
    all_rows = (ctx,) + rows.shape
    return pl.pallas_call(
        opening_kernel,
        out_shape=(
            jax.ShapeDtypeStruct(all_rows, kind),
            jax.ShapeDtypeStruct((8,) + columns.shape, kind),
            jax.ShapeDtypeStruct((shards, 2, ctx) + pack.shape, kind),
            jax.ShapeDtypeStruct((shards, ctx) + weights_in.shape[1:], kind),
            jax.ShapeDtypeStruct((shards, ctx) + weights_out.shape[1:], kind),
            jax.ShapeDtypeStruct((8,) + grads.shape, kind),
            jax.ShapeDtypeStruct((8,) + rows.shape, kind),
            jax.ShapeDtypeStruct((tokens, D), jnp.float32),
            jax.ShapeDtypeStruct((tokens, 128), jnp.float32),
            jax.ShapeDtypeStruct((1, D), jnp.float32),
            jax.ShapeDtypeStruct(rows.shape, kind),
        )
        + attend_shapes(all_rows, heads, groups),
        in_specs=[far] * 6 + [held],
        out_specs=(held, held, held, far, far, far, far) + (held,) * 9,
        scratch_shapes=[
            pltpu.VMEM((ctx, rows.shape[0], heads * HD), kind),
            pltpu.VMEM((groups * HD, ctx * rows.shape[0]), kind),
            pltpu.SemaphoreType.DMA((copies,)),
            pltpu.SemaphoreType.DMA((copies,)),
            pltpu.SemaphoreType.DMA((9,)),
            pltpu.SemaphoreType.DMA((8,)),
            pltpu.SemaphoreType.DMA((9,)),
            pltpu.SemaphoreType.DMA((8,)),
            pltpu.SemaphoreType.DMA((7,)),
        ],
        compiler_params=pltpu.CompilerParams(
            collective_id=number, has_side_effects=True, vmem_limit_bytes=56 * 1024 * 1024
        ),
    )(rows, columns, pack, weights_in, weights_out, grads, routes)


def split_high_low(values):
    high = values.astype(jnp.bfloat16)
    return high, (values - high.astype(jnp.float32)).astype(jnp.bfloat16)


def pad_columns(like, columns):
    return jnp.zeros((like.shape[0], columns), like.dtype)


def gather_ctx(rows):
    ctx = lax.axis_size("ctx")
    column = lax.axis_index("ctx")
    pieces = {0: rows}
    flip = ctx // 2
    while flip:
        pieces.update({turn ^ flip: swap(item, "ctx", flip) for turn, item in pieces.items()})
        flip //= 2
    out = jnp.zeros((ctx,) + rows.shape, rows.dtype)
    for turn in range(ctx):
        out = lax.dynamic_update_index_in_dim(out, pieces[turn], column ^ turn, 0)
    return out


def exchange_ctx(blocks):
    column = lax.axis_index("ctx")
    out = jnp.zeros(blocks.shape, blocks.dtype)
    for turn in range(blocks.shape[0]):
        item = lax.dynamic_index_in_dim(blocks, column ^ turn, 0, keepdims=False)
        if turn:
            item = swap(item, "ctx", turn)
        out = lax.dynamic_update_index_in_dim(out, item, column ^ turn, 0)
    return out


def scatter_ctx(blocks):
    column = lax.axis_index("ctx")
    flip = 1
    held = blocks
    while flip < lax.axis_size("ctx"):
        pairs = held.reshape((held.shape[0] // 2, 2) + held.shape[1:])
        bit = (column // flip) % 2
        keep = lax.dynamic_index_in_dim(pairs, bit, 1, keepdims=False)
        give = lax.dynamic_index_in_dim(pairs, 1 - bit, 1, keepdims=False)
        held = keep.astype(jnp.float32) + swap(give, "ctx", flip).astype(jnp.float32)
        flip *= 2
        if flip < lax.axis_size("ctx"):
            held = held.astype(jnp.bfloat16)
    return held[0]


def group_columns(rows, ctx):
    depth = rows.shape[0]
    cuts = (rows[:, : H * HD], rows[:, H * HD : (H + KV) * HD], rows[:, (H + KV) * HD :])
    return jnp.concatenate([cut.reshape(depth, ctx, -1) for cut in cuts], -1).transpose(1, 0, 2)


def ungroup_columns(groups):
    ctx, depth, _ = groups.shape
    query, key = H * HD // ctx, KV * HD // ctx
    cuts = (groups[..., :query], groups[..., query : query + key], groups[..., query + key :])
    return jnp.concatenate([cut.transpose(1, 0, 2).reshape(depth, -1) for cut in cuts], 1)


def block_order():
    shards, ctx = lax.axis_size("dp"), lax.axis_size("ctx")
    place, column = lax.axis_index("dp"), lax.axis_index("ctx")
    return place, column, shards, ctx


def fold_weights(expert_in, expert_out):
    deep = expert_out.shape[1]
    folds = expert_in.shape[1] // deep
    cuts = [expert_in[:, fold * deep : (fold + 1) * deep] for fold in range(folds)]
    return jnp.concatenate(cuts + [expert_out], -1)


def piece_order():
    place, column, shards, ctx = block_order()
    blocks = [
        (place ^ step) * ctx + (column ^ turn) for step in range(shards) for turn in range(ctx)
    ]
    return jnp.stack(blocks).astype(jnp.int32)


def spread_weights(expert_in, expert_out):
    shards = lax.axis_size("dp")
    count, depth = expert_in.shape[:2]
    part = FFE // shards
    cut = expert_in.reshape(count, depth, 2, shards, part).transpose(3, 0, 1, 2, 4)
    moved_in = lax.all_to_all(cut, "dp", split_axis=0, concat_axis=0, tiled=True)
    all_in = lax.all_gather(moved_in.transpose(1, 0, 2, 3, 4), "ctx", axis=2, tiled=True)
    all_out = lax.all_gather(expert_out, "ctx", axis=1, tiled=True)
    return [all_in.reshape(count, -1, 2 * part), all_out]


def piece_grads(order, rows, grads, grad_hidden, gated, pieces_in, pieces_out):
    _, _, shards, ctx = block_order()
    count, deep = pieces_out.shape[1:3]
    folds = pieces_in.shape[2] // deep
    shape = (ctx // 2, count, deep, folds * pieces_in.shape[3] + pieces_out.shape[3])
    slots = []
    for step in reversed(range(shards)):
        for bit in (1, 0):
            slots += [step * ctx + turn for turn in range(bit, ctx, 2)]
    order = jnp.stack([order[slot] for slot in slots])
    return weight_grads(order, rows, grads, grad_hidden, gated, [shape] * (2 * shards))


def collect_weights(order, rows, grads, grad_hidden, gated, expert_in, expert_out):
    place, column, shards, ctx = block_order()
    depth_in, depth_out = expert_in.shape[1], expert_out.shape[1]
    count = expert_in.shape[0]
    part = FFE // shards
    blocks = shards * ctx
    shapes = ((count, blocks * depth_in, 2 * part), (count, part, D))
    grad_in, grad_out = weight_grads(order, rows, grads, grad_hidden, gated, shapes)
    part_in = lax.psum_scatter(
        grad_in.reshape(count, shards, -1, 2, part), "ctx", scatter_dimension=2, tiled=True
    )
    own_in = lax.all_to_all(
        part_in.transpose(1, 0, 2, 3, 4), "dp", split_axis=0, concat_axis=0, tiled=True
    )
    own_in = own_in.transpose(1, 2, 3, 0, 4).reshape(count, -1, 2 * FFE)
    own_out = lax.psum_scatter(grad_out, "ctx", scatter_dimension=1, tiled=True)
    return [(0, fold_weights(own_in, own_out))]


def expert_step_kernel(places_ref, *refs):
    states, outs = refs[-14:-8], refs[-8:]
    grads = refs[:-14]
    number = pl.program_id(0)
    wide = states[0].shape[2]
    deep = states[3].shape[1]
    folds = states[0].shape[1] // deep
    rates = learn_rates()

    def update(grad_ref):
        for fold in range(folds):
            span = pl.ds(fold * deep, deep)
            grad = grad_ref[0, :, fold * wide : (fold + 1) * wide].astype(jnp.float32)
            news = adam_step(
                states[0][0, span, :],
                states[1][0, span, :],
                states[2][0, span, :],
                grad,
                DECAY_RATE,
                rates[5],
            )
            for out, new in zip(outs[:4], news):
                out[0, span, :] = new
        grad = grad_ref[0, :, folds * wide :].astype(jnp.float32)
        news = adam_step(states[3][0], states[4][0], states[5][0], grad, DECAY_RATE, rates[6])
        for out, new in zip(outs[4:], news):
            out[0] = new

    count = pl.num_programs(0) // len(grads)
    for index, grad_ref in enumerate(grads):
        pl.when(number // count == index)(functools.partial(update, grad_ref))


def expert_step(places, grads, states):
    count = grads[0].shape[0]
    shapes = [states[1].shape] * 4 + [states[4].shape] * 4
    moved = lambda e, p: (p[e // count] * count + e % count, 0, 0)
    block = lambda shape: pl.BlockSpec((1,) + shape[1:], moved)

    def grad_spec(index):
        return pl.BlockSpec(
            (1,) + grads[0].shape[1:], lambda e, p: (jnp.clip(e - index * count, 0, count - 1), 0, 0)
        )

    return pl.pallas_call(
        expert_step_kernel,
        grid_spec=pltpu.PrefetchScalarGridSpec(
            num_scalar_prefetch=1,
            grid=(count * len(grads),),
            in_specs=[grad_spec(index) for index in range(len(grads))]
            + [block(state.shape) for state in states],
            out_specs=tuple(block(shape) for shape in shapes),
        ),
        out_shape=tuple(jax.ShapeDtypeStruct(shape, jnp.float32) for shape in shapes),
        compiler_params=pltpu.CompilerParams(vmem_limit_bytes=62 * 1024 * 1024),
        cost_estimate=pl.CostEstimate(flops=1, bytes_accessed=1, transcendentals=0),
    )(places, *grads, *states)


def local(
    tokens,
    cotangent,
    routes,
    positions,
    gain_attend,
    gain_attend_mean,
    gain_attend_square,
    project_in,
    project_in_mean,
    project_in_square,
    project_out,
    project_out_mean,
    project_out_square,
    gain_expert,
    gain_expert_mean,
    gain_expert_square,
    router_weight,
    router_weight_mean,
    router_weight_square,
    expert_in,
    expert_in_mean,
    expert_in_square,
    expert_out,
    expert_out_mean,
    expert_out_square,
):
    everywhere = ("dp", "expert", "ctx")
    owners = ("dp", "expert")
    shards = lax.axis_size("dp")
    planes = lax.axis_size("expert")
    ctx = lax.axis_size("ctx")
    rows_local = tokens.shape[0]
    local_count = expert_in.shape[0]
    close = (shards, planes, ctx) == (4, 2, 4) and local_count % shards == 0
    heads, groups = H // ctx, KV // ctx
    hidden_in = tokens.astype(jnp.float32)

    half = HD // 2
    freqs = ROPE_BASE ** (-jnp.arange(half, dtype=jnp.float32) * 2.0 / HD)
    angles = positions.astype(jnp.float32)[:, None] * freqs[None, :]
    table = jnp.concatenate(split_high_low(jnp.cos(angles)) + split_high_low(jnp.sin(angles)), 1)
    gain_attend_wide = gain_attend.astype(jnp.float32)[:, None]
    scaled_in = (gain_attend_wide * project_in.astype(jnp.float32)).astype(jnp.bfloat16)
    rows = jnp.concatenate([tokens, table], 1)
    columns = group_columns(scaled_in, ctx)
    pack_out = jnp.concatenate(
        [project_out, router_weight, gain_expert[:, None], pad_columns(project_out, 87)], 1
    )
    order = piece_order()
    if close:
        parted = lambda array: array.reshape((shards, -1) + array.shape[1:])
        (
            seq_rows, own_in, full_pack_out, all_in, all_out, all_grads, all_packed,
            after, gates_wide, gain_two, packed,
            seq_normed, query, keys, values, attended_heads,
        ) = opening(
            rows, columns, pack_out, parted(expert_in), parted(expert_out), cotangent, routes,
            heads, groups, 1,
        )
        expert_input = packed[:, :D]
        pieces = [array.reshape((-1,) + array.shape[2:]) for array in (all_in, all_out)]
    else:
        seq_rows = gather_ctx(rows)
        own_in = lax.all_gather(exchange_ctx(columns), owners, axis=0, tiled=False)
        full_pack_out = lax.all_gather(pack_out, everywhere, axis=0, tiled=True)
        all_grads = lax.all_gather(cotangent, owners, axis=0, tiled=False)
        pieces = spread_weights(expert_in, expert_out)
        seq_normed, query, keys, values, seq_attended = attend_forward(
            seq_rows, own_in.reshape(D, -1), heads, groups
        )
        attended_heads = exchange_ctx(seq_attended)
    seq_rows = seq_rows.reshape(-1, D + 128)
    own_in = own_in.reshape(D, -1)
    full_pack_out = full_pack_out.reshape(H * HD, -1)
    if not close:
        full_out = full_pack_out[:, :D]
        full_router = full_pack_out[:, D : D + EXPERTS]
        gain_two = full_pack_out[:, D + EXPERTS].astype(jnp.float32)[None]
        attended = attended_heads.transpose(1, 0, 2).reshape(rows_local, H * HD)
        branch = jnp.dot(attended, full_out, preferred_element_type=jnp.float32)
        after = hidden_in + RESIDUAL_SCALE * branch
        normed_two, factor_two = normalize(after)
        expert_input = (normed_two * gain_two).astype(jnp.bfloat16)
        logits = jnp.dot(expert_input, full_router, preferred_element_type=jnp.float32)
        chosen = jnp.any(routes[:, :, None] == jnp.arange(EXPERTS, dtype=jnp.int32), axis=1)
        peak = jnp.max(jnp.where(chosen, logits, -3e38), axis=-1, keepdims=True)
        raised = jnp.where(chosen, jnp.exp(jnp.where(chosen, logits - peak, 0.0)), 0.0)
        gates = raised / jnp.sum(raised, axis=-1, keepdims=True)
        packed = jnp.concatenate(
            (expert_input,)
            + split_high_low(gates)
            + (chosen.astype(jnp.bfloat16), pad_columns(expert_input, 128 - 3 * EXPERTS)),
            1,
        )
        all_packed = lax.all_gather(packed, owners, axis=0, tiled=False)

    first = lax.axis_index("expert") * local_count
    count = local_count
    hidden = FFE // shards
    if close:
        count = local_count // shards
        hidden = FFE
        first = first + lax.axis_index("dp") * count
    first = first.astype(jnp.int32).reshape(1)
    slot_rows, slot_grads, pick = dispatch(first, all_packed, all_grads, count)
    produced, grad_rows, grad_hidden, gated = run_experts(
        first, order, slot_rows, slot_grads, pieces, hidden
    )
    shared_grads = combine(pick, grad_rows)
    shared = combine(pick, produced)
    gated, shared = lax.optimization_barrier((gated, shared))
    moe = lax.psum_scatter(shared, owners, scatter_dimension=0, tiled=False).astype(jnp.float32)
    if close:
        place = lax.axis_index("dp")
        parts = piece_grads(order, slot_rows, slot_grads, grad_hidden, gated, *pieces)
        grad_after, seq_grad, grad_pack_out, arrived, done3, ready2, ready1 = returning(
            shared_grads,
            parts,
            after,
            expert_input,
            gates_wide,
            cotangent,
            gain_two,
            full_pack_out,
            attended_heads,
            3,
        )
        done2, done1, done0, input_grad, shard_columns, shard_pack_out = closing(
            ready2,
            ready1,
            parts[7],
            arrived,
            seq_rows[:, D:],
            query,
            keys,
            values,
            seq_grad,
            seq_normed,
            own_in,
            grad_pack_out,
            tokens,
            grad_after,
            4,
        )
        expert_grads = [
            (near(place, "dp", 3), done3),
            (near(place, "dp", 2), done2),
            (near(place, "dp", 1), done1),
            (place, done0),
        ]
    else:
        grad_routed = lax.psum_scatter(
            shared_grads, owners, scatter_dimension=0, tiled=False
        ).astype(jnp.float32)
        expert_grads = collect_weights(
            order, slot_rows, slot_grads, grad_hidden, gated, expert_in, expert_out
        )
        grad_final = cotangent.astype(jnp.float32)
        grad_gates = grad_routed[:, D : D + EXPERTS] + grad_routed[:, D + EXPERTS : D + 2 * EXPERTS]
        grad_picked = gates * (grad_gates - jnp.sum(gates * grad_gates, axis=-1, keepdims=True))
        grad_logits = grad_picked.astype(jnp.bfloat16)
        grad_from_router = jnp.einsum(
            "te,de->td", grad_logits, full_router, preferred_element_type=jnp.float32
        )
        grad_input = grad_from_router + grad_routed[:, :D]
        grad_after = grad_final + norm_back(grad_input * gain_two, normed_two, factor_two)
        grad_branch = (RESIDUAL_SCALE * grad_after).astype(jnp.bfloat16)
        grad_attended = jnp.einsum(
            "td,cd->tc", grad_branch, full_out, preferred_element_type=jnp.float32
        ).astype(jnp.bfloat16)
        seq_grad = exchange_ctx(
            grad_attended.reshape(rows_local, ctx, heads * HD).transpose(1, 0, 2)
        )
        grad_mixed = attend_backward(seq_rows[:, D:], query, keys, values, seq_grad)
        grad_in_part = jnp.einsum(
            "td,tc->dc", seq_normed, grad_mixed, preferred_element_type=jnp.float32
        ).astype(jnp.bfloat16)
        grad_in_part = grad_in_part.reshape(shards * planes, -1, grad_in_part.shape[1])
        shard_columns = lax.psum_scatter(grad_in_part, owners, scatter_dimension=0, tiled=False)
        shard_columns = exchange_ctx(shard_columns.reshape(ctx, -1, shard_columns.shape[-1]))
        grad_scaled = jnp.einsum(
            "tc,dc->td", grad_mixed, own_in, preferred_element_type=jnp.float32
        ).astype(jnp.bfloat16)
        grad_normed = scatter_ctx(grad_scaled.reshape(ctx, rows_local, D))
        normed_one, factor_one = normalize(hidden_in)
        input_grad = grad_after + norm_back(grad_normed, normed_one, factor_one)
        grad_project_out = jnp.einsum(
            "tc,td->cd", attended, grad_branch, preferred_element_type=jnp.float32
        ).astype(jnp.bfloat16)
        ones = jnp.where(jnp.arange(128) == EXPERTS, 1.0, 0.0).astype(jnp.bfloat16)
        grad_small = jnp.einsum(
            "td,te->de",
            jnp.concatenate([expert_input, (grad_input * normed_two).astype(jnp.bfloat16)], 0),
            jnp.concatenate(
                [
                    jnp.pad(grad_logits, ((0, 0), (0, 128 - EXPERTS))),
                    jnp.broadcast_to(ones, (rows_local, 128)),
                ],
                0,
            ),
            preferred_element_type=jnp.float32,
        ).astype(jnp.bfloat16)
        grad_pack_out = jnp.concatenate([grad_project_out, grad_small], 1)
        shard_pack_out = lax.psum_scatter(
            grad_pack_out, everywhere, scatter_dimension=0, tiled=True
        ).astype(jnp.float32)
    block_output = (after + RESIDUAL_SCALE * moe).astype(jnp.bfloat16)
    shard_scaled = ungroup_columns(shard_columns).astype(jnp.float32)
    shard_in = gain_attend_wide * shard_scaled
    shard_attend = jnp.sum(shard_scaled * project_in.astype(jnp.float32), axis=1)
    shard_out = shard_pack_out[:, :D]
    shard_router = shard_pack_out[:, D : D + EXPERTS]
    shard_expert = shard_pack_out[:, D + EXPERTS]
    rates = learn_rates()
    results = [block_output, input_grad]
    results.extend(
        adam_step(gain_attend, gain_attend_mean, gain_attend_square, shard_attend, 0.0, rates[0])
    )
    results.extend(
        adam_step(project_in, project_in_mean, project_in_square, shard_in, DECAY_RATE, rates[1])
    )
    results.extend(
        adam_step(
            project_out, project_out_mean, project_out_square, shard_out, DECAY_RATE, rates[2]
        )
    )
    results.extend(
        adam_step(gain_expert, gain_expert_mean, gain_expert_square, shard_expert, 0.0, rates[3])
    )
    results.extend(
        adam_step(
            router_weight,
            router_weight_mean,
            router_weight_square,
            shard_router,
            DECAY_RATE,
            rates[4],
        )
    )
    states = (expert_in, expert_in_mean, expert_in_square, expert_out, expert_out_mean, expert_out_square)
    places = jnp.stack([jnp.asarray(place, jnp.int32) for place, _ in expert_grads])
    expert_outs = expert_step(places, [folded for _, folded in expert_grads], states)
    results.extend(expert_outs)
    return tuple(results)


def solution(mesh):
    placed = (
        P(("dp", "expert", "ctx"), None),
        P(("dp", "expert", "ctx"), None),
        P(("dp", "expert", "ctx"), None),
        P(("dp", "expert", "ctx")),
        P(("dp", "expert", "ctx")),
        P(("dp", "expert", "ctx")),
        P(("dp", "expert", "ctx")),
        P(("dp", "expert", "ctx"), None),
        P(("dp", "expert", "ctx"), None),
        P(("dp", "expert", "ctx"), None),
        P(("dp", "expert", "ctx"), None),
        P(("dp", "expert", "ctx"), None),
        P(("dp", "expert", "ctx"), None),
        P(("dp", "expert", "ctx")),
        P(("dp", "expert", "ctx")),
        P(("dp", "expert", "ctx")),
        P(("dp", "expert", "ctx"), None),
        P(("dp", "expert", "ctx"), None),
        P(("dp", "expert", "ctx"), None),
        P("expert", ("dp", "ctx"), None),
        P("expert", ("dp", "ctx"), None),
        P("expert", ("dp", "ctx"), None),
        P("expert", ("dp", "ctx"), None),
        P("expert", ("dp", "ctx"), None),
        P("expert", ("dp", "ctx"), None),
    )
    return jax.shard_map(
        local,
        mesh=mesh,
        in_specs=placed,
        out_specs=(
            P(("dp", "expert", "ctx"), None),
            P(("dp", "expert", "ctx"), None),
            P(("dp", "expert", "ctx")),
            P(("dp", "expert", "ctx")),
            P(("dp", "expert", "ctx")),
            P(("dp", "expert", "ctx")),
            P(("dp", "expert", "ctx"), None),
            P(("dp", "expert", "ctx"), None),
            P(("dp", "expert", "ctx"), None),
            P(("dp", "expert", "ctx"), None),
            P(("dp", "expert", "ctx"), None),
            P(("dp", "expert", "ctx"), None),
            P(("dp", "expert", "ctx"), None),
            P(("dp", "expert", "ctx"), None),
            P(("dp", "expert", "ctx")),
            P(("dp", "expert", "ctx")),
            P(("dp", "expert", "ctx")),
            P(("dp", "expert", "ctx")),
            P(("dp", "expert", "ctx"), None),
            P(("dp", "expert", "ctx"), None),
            P(("dp", "expert", "ctx"), None),
            P(("dp", "expert", "ctx"), None),
            P("expert", ("dp", "ctx"), None),
            P("expert", ("dp", "ctx"), None),
            P("expert", ("dp", "ctx"), None),
            P("expert", ("dp", "ctx"), None),
            P("expert", ("dp", "ctx"), None),
            P("expert", ("dp", "ctx"), None),
            P("expert", ("dp", "ctx"), None),
            P("expert", ("dp", "ctx"), None),
        ),
        check_vma=False,
    )
```

```python
import functools

import jax
import jax.numpy as jnp
from jax import lax
from jax.experimental import pallas as pl
from jax.experimental.pallas import tpu as pltpu
from jax.sharding import PartitionSpec as P

D = 1536
H = 24
KV = 8
HD = 64
FFE = 512
EXPERTS = 40
TOP = 8
STEP = 8
CAP = 64


EPS_NORM = 1e-06
ATTN_SCALE = 0.015625
RESIDUAL_SCALE = 0.22
BETA_ONE = 0.9
BETA_TWO = 0.95
ADAM_EPS = 1e-08
DECAY_RATE = 0.1
ROPE_BASE = 10000.0


def normalize(rows):
    factor = lax.rsqrt(jnp.mean(rows * rows, axis=-1, keepdims=True) + EPS_NORM)
    return (rows * factor, factor)


def norm_back(grad_normed, normed, factor):
    return factor * (grad_normed - normed * jnp.mean(grad_normed * normed, axis=-1, keepdims=True))


def learn_rates():
    return (
        0.3,
        3.0 / (D // 16) ** 0.5,
        3.0 / (D // 12) ** 0.5,
        0.3,
        3.0 / (4 * D) ** 0.5,
        3.0 / D**0.5,
        3.0 / (FFE // 32) ** 0.5,
    )


def adam_step(weight, first, second, grad, decay, rate):
    new_first = BETA_ONE * first + (1.0 - BETA_ONE) * grad
    new_second = BETA_TWO * second + (1.0 - BETA_TWO) * grad * grad
    corrected = (new_first * (1.0 / (1.0 - BETA_ONE**STEP))) / (
        jnp.sqrt(new_second * (1.0 / (1.0 - BETA_TWO**STEP))) + ADAM_EPS
    )
    old = weight.astype(jnp.float32)
    return (grad, new_first, new_second, old - rate * (corrected + decay * old))


def lane_tables(table):
    half = HD // 2
    source = lax.broadcasted_iota(jnp.int32, (128, 128), 0)
    target = lax.broadcasted_iota(jnp.int32, (128, 128), 1)
    same = (source % half) == (target % half)
    group = source // half
    first = (target % HD) < half
    cosine = jnp.where(same & (group < 2), 1.0, 0.0).astype(jnp.bfloat16)
    ahead = jnp.where(same & (group >= 2) & first, -1.0, 0.0).astype(jnp.bfloat16)
    behind = jnp.where(same & (group >= 2) & jnp.logical_not(first), 1.0, 0.0).astype(jnp.bfloat16)
    return tuple(
        jnp.dot(table, item, preferred_element_type=jnp.float32)
        for item in (cosine, ahead, behind)
    )


def turn_lanes(block, tables, sign):
    cosine, ahead, behind = tables
    half = HD // 2
    turned = pltpu.roll(block, 128 - half, 1) * ahead + pltpu.roll(block, half, 1) * behind
    return block * cosine + sign * turned


def scores_of(keys, query, start, length):
    scores = (
        lax.dot_general(
            keys, query, (((1,), (1,)), ((), ())), preferred_element_type=jnp.float32
        )
        * ATTN_SCALE
    )
    rows = lax.broadcasted_iota(jnp.int32, scores.shape, 0)
    columns = lax.broadcasted_iota(jnp.int32, scores.shape, 1) + start
    return jnp.where(rows <= columns, scores, -1e30)


def project_rows(rows_ref, table_ref, weight, normed_ref, query_ref, keys_ref, values_ref, flipped):
    blocks, block = rows_ref.shape[:2]
    heads, groups = query_ref.shape[0], keys_ref.shape[0]
    wide = heads * HD
    for index in range(blocks):
        span = pl.ds(index * block, block)
        rows = rows_ref[index].astype(jnp.float32)
        factor = lax.rsqrt(jnp.mean(rows * rows, axis=-1, keepdims=True) + EPS_NORM)
        normed = (rows * factor).astype(jnp.bfloat16)
        normed_ref[span, :] = normed
        tables = lane_tables(table_ref[index])
        mixed = jnp.dot(normed, weight, preferred_element_type=jnp.float32)
        for column in range(0, wide + 2 * groups * HD, 128):
            part = mixed[:, column : column + 128]
            if column < wide + groups * HD:
                part = turn_lanes(part, tables, 1.0)
            else:
                flipped[column - wide - groups * HD : column - wide - groups * HD + 128, span] = (
                    part.T.astype(jnp.bfloat16)
                )
            part = part.astype(jnp.bfloat16)
            for half in range(2):
                head = column // HD + half
                piece = part[:, half * HD : (half + 1) * HD]
                if head < heads:
                    query_ref[head, span, :] = piece
                elif head < heads + groups:
                    keys_ref[head - heads, span, :] = piece
                else:
                    values_ref[head - heads - groups, span, :] = piece


def attend_rows(index, block, query_ref, keys_ref, out_ref, flipped):
    heads, groups = query_ref.shape[0], keys_ref.shape[0]
    length = (index + 1) * block
    span = pl.ds(index * block, block)
    outputs = []
    for head in range(heads):
        group = head // (heads // groups)
        scores = scores_of(
            keys_ref[group, :length, :], query_ref[head, span, :], index * block, length
        )
        peak = jnp.max(scores, axis=0, keepdims=True)
        raised = jnp.exp(scores - peak)
        total = jnp.sum(raised, axis=0, keepdims=True)
        probs = (raised * (1.0 / total)).astype(jnp.bfloat16)
        outputs.append(
            jnp.dot(
                flipped[group * HD : (group + 1) * HD, :length],
                probs,
                preferred_element_type=jnp.float32,
            )
        )
    out_ref[index] = jnp.concatenate(outputs, 0).T.astype(jnp.bfloat16)


def attend_kernel(rows_ref, table_ref, weight_ref, normed_ref, query_ref, keys_ref, values_ref, out_ref, flipped):
    project_rows(rows_ref, table_ref, weight_ref[...], normed_ref, query_ref, keys_ref, values_ref, flipped)
    for index in range(rows_ref.shape[0]):
        attend_rows(index, rows_ref.shape[1], query_ref, keys_ref, out_ref, flipped)


def attend_shapes(rows, heads, groups):
    blocks, block = rows[:2]
    length = blocks * block
    return (
        jax.ShapeDtypeStruct((length, D), jnp.bfloat16),
        jax.ShapeDtypeStruct((heads, length, HD), jnp.bfloat16),
        jax.ShapeDtypeStruct((groups, length, HD), jnp.bfloat16),
        jax.ShapeDtypeStruct((groups, length, HD), jnp.bfloat16),
        jax.ShapeDtypeStruct((blocks, block, heads * HD), jnp.bfloat16),
    )


def attend_back(rows_ref, query_ref, keys_ref, values_ref, grad_ref, out_ref, flipped, grad_keys, grad_values):
    block = 256
    blocks = rows_ref.shape[0] // block
    heads, groups = query_ref.shape[0], keys_ref.shape[0]
    repeat = heads // groups
    wide = heads * HD
    for group in range(groups):
        flipped[group * HD : (group + 1) * HD, :] = (
            keys_ref[group].astype(jnp.float32).T.astype(jnp.bfloat16)
        )
    grad_keys[...] = jnp.zeros_like(grad_keys)
    grad_values[...] = jnp.zeros_like(grad_values)
    for index in range(blocks):
        length = (index + 1) * block
        span = pl.ds(index * block, block)
        outputs = []
        for head in range(heads):
            group = head // repeat
            query = query_ref[head, span, :]
            grad = grad_ref[index, :, head * HD : (head + 1) * HD]
            scores = scores_of(keys_ref[group, :length, :], query, index * block, length)
            peak = jnp.max(scores, axis=0, keepdims=True)
            raised = jnp.exp(scores - peak)
            total = jnp.sum(raised, axis=0, keepdims=True)
            probs = raised * (1.0 / total)
            grad_probs = lax.dot_general(
                values_ref[group, :length, :],
                grad,
                (((1,), (1,)), ((), ())),
                preferred_element_type=jnp.float32,
            )
            middle = jnp.sum(probs * grad_probs, axis=0, keepdims=True)
            grad_scores = (probs * (grad_probs - middle)).astype(jnp.bfloat16)
            grad_keys[group, :length, :] += jnp.dot(
                grad_scores, query, preferred_element_type=jnp.float32
            )
            grad_values[group, :length, :] += jnp.dot(
                probs.astype(jnp.bfloat16), grad, preferred_element_type=jnp.float32
            )
            outputs.append(
                jnp.dot(
                    flipped[group * HD : (group + 1) * HD, :length],
                    grad_scores,
                    preferred_element_type=jnp.float32,
                )
            )
        tables = lane_tables(rows_ref[span, :])
        stacked = jnp.concatenate(outputs, 0).T * ATTN_SCALE
        for column in range(0, wide, 128):
            out_ref[span, column : column + 128] = turn_lanes(
                stacked[:, column : column + 128], tables, -1.0
            ).astype(jnp.bfloat16)
    for index in range(blocks):
        span = pl.ds(index * block, block)
        tables = lane_tables(rows_ref[span, :])
        keys = jnp.concatenate([grad_keys[group, span, :] for group in range(groups)], 1)
        values = jnp.concatenate([grad_values[group, span, :] for group in range(groups)], 1)
        keys = turn_lanes(keys * ATTN_SCALE, tables, -1.0)
        out_ref[span, wide : wide + groups * HD] = keys.astype(jnp.bfloat16)
        out_ref[span, wide + groups * HD :] = values.astype(jnp.bfloat16)


def attend_forward(rows, table, weight, heads, groups):
    return pl.pallas_call(
        attend_kernel,
        out_shape=attend_shapes(rows.shape, heads, groups),
        scratch_shapes=[pltpu.VMEM((groups * HD, rows.shape[0] * rows.shape[1]), jnp.bfloat16)],
        compiler_params=pltpu.CompilerParams(vmem_limit_bytes=48 * 1024 * 1024),
        cost_estimate=pl.CostEstimate(flops=1, bytes_accessed=1, transcendentals=0),
    )(rows, table, weight)


def attend_backward(table, query, keys, values, grad):
    heads, length = query.shape[:2]
    groups = keys.shape[0]
    return pl.pallas_call(
        attend_back,
        out_shape=jax.ShapeDtypeStruct((length, (heads + 2 * groups) * HD), jnp.bfloat16),
        scratch_shapes=[
            pltpu.VMEM((groups * HD, length), jnp.bfloat16),
            pltpu.VMEM((groups, length, HD), jnp.float32),
            pltpu.VMEM((groups, length, HD), jnp.float32),
        ],
        compiler_params=pltpu.CompilerParams(vmem_limit_bytes=48 * 1024 * 1024),
        cost_estimate=pl.CostEstimate(flops=1, bytes_accessed=1, transcendentals=0),
    )(table, query, keys, values, grad)


def dispatch_kernel(first_ref, rows_ref, grads_ref, out_rows, out_grads, out_pick):
    count = out_rows.shape[0]
    tokens = rows_ref.shape[1]
    padded = -(-count // 16) * 16
    tail = rows_ref[0, :, D:]
    lane = lax.broadcasted_iota(jnp.int32, (padded, 128), 1)
    row = lax.broadcasted_iota(jnp.int32, (padded, 128), 0)
    wanted = (lane == 2 * EXPERTS + first_ref[0] + row) & (row < count)
    marks = lax.dot_general(
        wanted.astype(jnp.bfloat16),
        tail,
        (((1,), (1,)), ((), ())),
        preferred_element_type=jnp.float32,
    )
    earlier = lax.broadcasted_iota(jnp.int32, (tokens, tokens), 0) < lax.broadcasted_iota(
        jnp.int32, (tokens, tokens), 1
    )
    rank = jnp.dot(
        marks.astype(jnp.bfloat16),
        earlier.astype(jnp.bfloat16),
        preferred_element_type=jnp.float32,
    )
    slot = lax.broadcasted_iota(jnp.int32, (CAP, tokens), 0).astype(jnp.float32)
    pick = jnp.concatenate(
        [
            jnp.where(
                rank[item : item + 1, :] == slot, marks[item : item + 1, :], 0.0
            ).astype(jnp.bfloat16)
            for item in range(count)
        ],
        0,
    )
    out_pick[0] = pick
    moved = jnp.dot(pick, rows_ref[0], preferred_element_type=jnp.float32).astype(jnp.bfloat16)
    moved_grads = jnp.dot(pick, grads_ref[0], preferred_element_type=jnp.float32).astype(
        jnp.bfloat16
    )
    for item in range(count):
        out_rows[item] = moved[item * CAP : (item + 1) * CAP]
        out_grads[item] = moved_grads[item * CAP : (item + 1) * CAP]


def dispatch(first, rows, grads, count):
    sources, tokens, wide = rows.shape
    return pl.pallas_call(
        dispatch_kernel,
        grid_spec=pltpu.PrefetchScalarGridSpec(
            num_scalar_prefetch=1,
            grid=(sources,),
            in_specs=[
                pl.BlockSpec((1, tokens, wide), lambda s, f: (s, 0, 0)),
                pl.BlockSpec((1, tokens, D), lambda s, f: (s, 0, 0)),
            ],
            out_specs=(
                pl.BlockSpec((count, CAP, wide), lambda s, f: (0, s, 0)),
                pl.BlockSpec((count, CAP, D), lambda s, f: (0, s, 0)),
                pl.BlockSpec((1, count * CAP, tokens), lambda s, f: (s, 0, 0)),
            ),
        ),
        out_shape=(
            jax.ShapeDtypeStruct((count, sources * CAP, wide), jnp.bfloat16),
            jax.ShapeDtypeStruct((count, sources * CAP, D), jnp.bfloat16),
            jax.ShapeDtypeStruct((sources, count * CAP, tokens), jnp.bfloat16),
        ),
        compiler_params=pltpu.CompilerParams(vmem_limit_bytes=62 * 1024 * 1024),
        cost_estimate=pl.CostEstimate(flops=1, bytes_accessed=1, transcendentals=0),
    )(first, rows, grads)


def combine_kernel(pick_ref, rows_ref, out_ref):
    rows = jnp.concatenate([rows_ref[item] for item in range(rows_ref.shape[0])], 0)
    out_ref[0] = lax.dot_general(
        pick_ref[0], rows, (((0,), (0,)), ((), ())), preferred_element_type=jnp.float32
    ).astype(jnp.bfloat16)


def combine(pick, rows):
    sources, slots, tokens = pick.shape
    count, _, wide = rows.shape
    return pl.pallas_call(
        combine_kernel,
        grid=(sources,),
        in_specs=[
            pl.BlockSpec((1, slots, tokens), lambda s: (s, 0, 0)),
            pl.BlockSpec((count, CAP, wide), lambda s: (0, s, 0)),
        ],
        out_specs=pl.BlockSpec((1, tokens, wide), lambda s: (s, 0, 0)),
        out_shape=jax.ShapeDtypeStruct((sources, tokens, wide), jnp.bfloat16),
        compiler_params=pltpu.CompilerParams(vmem_limit_bytes=62 * 1024 * 1024),
        cost_estimate=pl.CostEstimate(flops=1, bytes_accessed=1, transcendentals=0),
    )(pick, rows)


def expert_kernel(first_ref, order_ref, slots_ref, rows_ref, grads_ref, *refs):
    whole_in, whole_out, total_in, total_out = refs[-4:]
    pieces, (produced_ref, grad_rows_ref), outs = refs[:2], refs[2:4], refs[4:-4]
    expert = first_ref[0] + pl.program_id(0)
    chunk = pl.program_id(1)
    parted = len(pieces[0].shape) == 4

    @pl.when(chunk == 0)
    def assemble():
        if not parted:
            whole_in[...] = pieces[0][0]
            whole_out[...] = pieces[1][0]
            return
        for index in range(pieces[0].shape[0]):
            block = order_ref[index]
            for piece, whole in zip(pieces, (whole_in, whole_out)):
                deep = piece.shape[2]
                whole[pl.ds(pl.multiple_of(block * deep, deep), deep), :] = piece[index, 0]

    tail = rows_ref[0, :, D:].astype(jnp.float32)
    lane = lax.broadcasted_iota(jnp.int32, tail.shape, 1)
    own = (lane == expert) | (lane == EXPERTS + expert)
    gate = jnp.sum(jnp.where(own, tail, 0.0), axis=-1, keepdims=True)
    hidden = whole_out.shape[0]
    gate_up = jnp.dot(rows_ref[0, :, :D], whole_in[...], preferred_element_type=jnp.float32)
    gate_half = gate_up[:, :hidden]
    up_half = gate_up[:, hidden:]
    sigma = 1.0 / (1.0 + jnp.exp(-gate_half))
    activated = gate_half * sigma
    middle = activated * up_half
    gated = (gate * middle).astype(jnp.bfloat16)
    produced_ref[0] = jnp.dot(gated, whole_out[...], preferred_element_type=jnp.float32).astype(
        jnp.bfloat16
    )
    grad_middle = RESIDUAL_SCALE * lax.dot_general(
        grads_ref[0],
        whole_out[...],
        (((1,), (1,)), ((), ())),
        preferred_element_type=jnp.float32,
    )
    grad_gate = jnp.sum(middle * grad_middle, axis=-1, keepdims=True)
    grad_middle = gate * grad_middle
    slope = sigma * (1.0 + gate_half * (1.0 - sigma))
    grad_hidden = jnp.concatenate(
        [grad_middle * up_half * slope, grad_middle * activated], -1
    ).astype(jnp.bfloat16)
    grad_rows_ref[0, :, :D] = lax.dot_general(
        grad_hidden,
        whole_in[...],
        (((1,), (1,)), ((), ())),
        preferred_element_type=jnp.float32,
    ).astype(jnp.bfloat16)
    high = grad_gate.astype(jnp.bfloat16).astype(jnp.float32)
    spread = jnp.where(
        lane == expert, high, jnp.where(lane == EXPERTS + expert, grad_gate - high, 0.0)
    )
    grad_rows_ref[0, :, D:] = spread.astype(jnp.bfloat16)

    turned = (((0,), (0,)), ((), ()))
    part_in = lax.dot_general(
        rows_ref[0, :, :D], grad_hidden, turned, preferred_element_type=jnp.float32
    )
    part_out = RESIDUAL_SCALE * lax.dot_general(
        gated, grads_ref[0], turned, preferred_element_type=jnp.float32
    )

    @pl.when(chunk == 0)
    def store():
        total_in[...] = part_in
        total_out[...] = part_out

    @pl.when(chunk > 0)
    def add():
        total_in[...] += part_in
        total_out[...] += part_out

    @pl.when(chunk == pl.num_programs(1) - 1)
    def finish():
        if not parted:
            outs[0][0] = total_in[...].astype(jnp.bfloat16)
            outs[1][0] = total_out[...].astype(jnp.bfloat16)
            return
        wide = total_in.shape[1]
        turns = outs[0].shape[0]
        deep = outs[0].shape[2]
        folds = (outs[0].shape[3] - D) // wide
        for number, out in enumerate(outs):
            for turn in range(turns):
                block = slots_ref[number * turns + turn]
                for fold in range(folds):
                    start = pl.multiple_of((block * folds + fold) * deep, deep)
                    out[turn, 0, :, fold * wide : (fold + 1) * wide] = total_in[
                        pl.ds(start, deep), :
                    ].astype(jnp.bfloat16)
                start = pl.multiple_of(block * deep, deep)
                out[turn, 0, :, folds * wide :] = total_out[pl.ds(start, deep), :].astype(
                    jnp.bfloat16
                )


def run_experts(first, order, rows, grads, pieces, hidden, parted):
    count, slots, wide = rows.shape
    chunk = min(512, slots)
    by_chunk = lambda e, c, *_: (e, c, 0)
    by_expert = lambda e, c, *_: (e, 0, 0)
    by_turn = lambda e, c, *_: (0, e, 0, 0)
    if parted:
        _, _, shards, ctx = block_order()
        places = []
        for step in reversed(range(shards)):
            for bit in (1, 0):
                places += [step * ctx + turn for turn in range(bit, ctx, 2)]
        places = jnp.stack([order[place] for place in places])
        deep = pieces[1].shape[2]
        folds = pieces[0].shape[2] // deep
        shapes = [(ctx // 2, count, deep, folds * 2 * hidden + D)] * (2 * shards)
        block = lambda shape: pl.BlockSpec((shape[0], 1) + shape[2:], by_turn)
    else:
        places = order
        shapes = [(count, D, 2 * hidden), (count, hidden, D)]
        block = lambda shape: pl.BlockSpec((1,) + shape[1:], by_expert)
    outs = pl.pallas_call(
        expert_kernel,
        grid_spec=pltpu.PrefetchScalarGridSpec(
            num_scalar_prefetch=3,
            grid=(count, slots // chunk),
            in_specs=[
                pl.BlockSpec((1, chunk, wide), by_chunk),
                pl.BlockSpec((1, chunk, D), by_chunk),
            ]
            + [block(piece.shape) for piece in pieces],
            out_specs=(
                pl.BlockSpec((1, chunk, D), by_chunk),
                pl.BlockSpec((1, chunk, wide), by_chunk),
            )
            + tuple(block(shape) for shape in shapes),
            scratch_shapes=[
                pltpu.VMEM((D, 2 * hidden), jnp.bfloat16),
                pltpu.VMEM((hidden, D), jnp.bfloat16),
                pltpu.VMEM((D, 2 * hidden), jnp.float32),
                pltpu.VMEM((hidden, D), jnp.float32),
            ],
        ),
        out_shape=(
            jax.ShapeDtypeStruct((count, slots, D), jnp.bfloat16),
            jax.ShapeDtypeStruct((count, slots, wide), jnp.bfloat16),
        )
        + tuple(jax.ShapeDtypeStruct(shape, jnp.bfloat16) for shape in shapes),
        compiler_params=pltpu.CompilerParams(vmem_limit_bytes=62 * 1024 * 1024),
        cost_estimate=pl.CostEstimate(flops=1, bytes_accessed=1, transcendentals=0),
    )(first, order, places, rows, grads, *pieces)
    return outs[0], outs[1], outs[2:]


def swap(rows, axis, flip):
    size = lax.axis_size(axis)
    return lax.ppermute(rows, axis, [(i, i ^ flip) for i in range(size)])


def near(place, axis, flip):
    if lax.axis_size(axis) == 2:
        return 1 - place
    if flip == 1:
        return place + 1 - 2 * lax.rem(place, 2)
    if flip == 2:
        return lax.rem(place + 2, 4)
    return 3 - place


def greet(partners):
    barrier = pltpu.get_barrier_semaphore()
    for axis, flip in partners:
        pl.semaphore_signal(
            barrier,
            inc=1,
            device_id={axis: near(lax.axis_index(axis), axis, flip)},
            device_id_type=pl.DeviceIdType.MESH,
        )
    pl.semaphore_wait(barrier, len(partners))


class Link:
    def __init__(self, sends, receives):
        self.sends, self.receives, self.used, self.started = sends, receives, 0, []

    def push(self, source, target, axis, flip):
        copy = pltpu.make_async_remote_copy(
            src_ref=source,
            dst_ref=target,
            send_sem=self.sends.at[self.used],
            recv_sem=self.receives.at[self.used],
            device_id={axis: near(lax.axis_index(axis), axis, flip)},
            device_id_type=pl.DeviceIdType.MESH,
        )
        copy.start()
        self.used += 1
        self.started.append(copy)
        return copy

    def finish(self):
        for copy in self.started:
            copy.wait_send()


class Line:
    def __init__(self, rows_ref, out_ref, sends, receives):
        z, y = lax.axis_index("dp"), lax.axis_index("expert")
        self.inner = z * (3 - z) > 0
        self.outer = z * (3 - z) < 1

        def slot(flip):
            return 2 * (near(z, "dp", flip) if flip else z) + y

        def hand(sent, received, source, target, flip, axis="dp"):
            return pltpu.make_async_remote_copy(
                src_ref=source,
                dst_ref=target,
                send_sem=sends.at[sent],
                recv_sem=receives.at[received],
                device_id={axis: near(lax.axis_index(axis), axis, flip)},
                device_id_type=pl.DeviceIdType.MESH,
            )

        def block(flip):
            return out_ref.at[slot(flip)]

        self.to_first = hand(0, 1, rows_ref, block(0), 1)
        self.across_own = hand(1, 3, rows_ref, block(0), 3)
        self.across_first = hand(2, 2, block(1), block(1), 3)
        self.pass_third = hand(3, 2, block(3), block(3), 1)
        self.pass_second = hand(8, 3, block(2), block(2), 1)
        self.over = [
            hand(4 + flip, 4 + flip, block(flip) if flip else rows_ref, block(flip), 1, "expert")
            for flip in range(4)
        ]
        self.got = [None] + [hand(0, flip, block(flip), block(flip), 1) for flip in range(1, 4)]
        self.got_over = [
            hand(0, 4 + flip, block(flip), out_ref.at[slot(flip) + 1 - 2 * y], 1, "expert")
            for flip in range(4)
        ]

    def start(self):
        self.to_first.start()

        @pl.when(self.inner)
        def inner():
            self.across_own.start()

        self.over[0].start()

    def first(self):
        self.got[1].wait_recv()

        @pl.when(self.inner)
        def inner():
            self.across_first.start()

        self.over[1].start()

    def second(self):
        @pl.when(self.inner)
        def inner():
            self.got[3].wait_recv()
            self.pass_third.start()
            self.over[3].start()

        @pl.when(self.outer)
        def outer():
            self.got[2].wait_recv()
            self.over[2].start()

    def third(self):
        @pl.when(self.inner)
        def inner():
            self.got[2].wait_recv()
            self.pass_second.start()
            self.over[2].start()

        @pl.when(self.outer)
        def outer():
            self.got[3].wait_recv()
            self.over[3].start()

    def finish(self):
        self.to_first.wait_send()

        @pl.when(self.inner)
        def inner():
            for copy in (self.across_own, self.across_first, self.pass_third, self.pass_second):
                copy.wait_send()

        for copy in self.over:
            copy.wait_send()
        for copy in self.got_over:
            copy.wait_recv()


class Fold:
    def __init__(self, blocks_ref, out_ref, over, sums, parts, sends, receives, local=None):
        z, y = lax.axis_index("dp"), lax.axis_index("expert")
        self.inner = z * (3 - z) > 0
        self.outer = z * (3 - z) < 1
        self.blocks, self.out, self.over, self.sums, self.parts = blocks_ref, out_ref, over, sums, parts
        self.y = y

        def slot(flip, plane):
            return 2 * (near(z, "dp", flip) if flip else z) + plane

        def hand(number, source, target, flip, axis="dp"):
            return pltpu.make_async_remote_copy(
                src_ref=source,
                dst_ref=target,
                send_sem=sends.at[number],
                recv_sem=receives.at[number],
                device_id={axis: near(lax.axis_index(axis), axis, flip)},
                device_id_type=pl.DeviceIdType.MESH,
            )

        self.slot = slot
        self.staged = [
            pltpu.make_async_copy(blocks_ref.at[slot(flip, y)], sums.at[flip], local.at[flip])
            for flip in range(4 if local is not None else 0)
        ]
        self.across = [
            hand(flip, blocks_ref.at[slot(flip, 1 - y)], over.at[flip], 1, "expert")
            for flip in range(4)
        ]
        self.to_line = [hand(4 + k, sums.at[3 - k], parts.at[k], 1) for k in range(3)]
        self.to_middle = [hand(7 + k, sums.at[2 + k], parts.at[3 + k], 3) for k in range(2)]
        self.to_end = hand(9, sums.at[1], parts.at[5], 1)

    def own(self, flip):
        self.across[flip].wait_recv()
        if self.staged:
            self.staged[flip].wait()
            held = self.sums[flip]
        else:
            held = self.blocks[self.slot(flip, self.y)]
        return held.astype(jnp.float32) + self.over[flip].astype(jnp.float32)

    def part(self, number):
        return self.parts[number].astype(jnp.float32)

    def start(self):
        @pl.when(self.inner)
        def inner():
            for flip in (2, 3, 1, 0):
                self.across[flip].start()

        @pl.when(self.outer)
        def outer():
            for flip in (3, 2, 1, 0):
                self.across[flip].start()

        for copy in self.staged:
            copy.start()

    def early(self, k, ends=True, middle=True):
        if middle:

            @pl.when(self.inner)
            def inner():
                total = self.own(2 + k)
                self.to_line[k].wait_recv()
                self.sums[2 + k] = (total + self.part(k)).astype(jnp.bfloat16)
                self.to_middle[k].start()

        if ends:

            @pl.when(self.outer)
            def outer():
                self.sums[3 - k] = self.own(3 - k).astype(jnp.bfloat16)
                self.to_line[k].start()

    def late(self):
        @pl.when(self.inner)
        def inner():
            total = self.own(1)
            self.to_middle[0].wait_recv()
            self.sums[1] = (total + self.part(3)).astype(jnp.bfloat16)
            self.to_end.start()

        @pl.when(self.outer)
        def outer():
            self.sums[1] = self.own(1).astype(jnp.bfloat16)
            self.to_line[2].start()

    def last(self):
        @pl.when(self.inner)
        def inner():
            total = self.own(0)
            self.to_line[2].wait_recv()
            self.to_middle[1].wait_recv()
            self.out[...] = (total + self.part(2) + self.part(4)).astype(self.out.dtype)

        @pl.when(self.outer)
        def outer():
            total = self.own(0)
            self.to_end.wait_recv()
            self.out[...] = (total + self.part(5)).astype(self.out.dtype)

    def finish(self):
        @pl.when(self.inner)
        def inner():
            for copy in self.to_middle + [self.to_end]:
                copy.wait_send()

        @pl.when(self.outer)
        def outer():
            for copy in self.to_line:
                copy.wait_send()

        for copy in self.across:
            copy.wait_send()


def fold_scratch(shape):
    return [
        pltpu.VMEM((4,) + shape, jnp.bfloat16),
        pltpu.VMEM((4,) + shape, jnp.bfloat16),
        pltpu.VMEM((6,) + shape, jnp.bfloat16),
        pltpu.SemaphoreType.DMA((10,)),
        pltpu.SemaphoreType.DMA((10,)),
    ]


def add_into(target, sources):
    def body(item, carry):
        total = sources[0][item].astype(jnp.float32)
        for source in sources[1:]:
            total = total + source[item].astype(jnp.float32)
        target[item] = total.astype(jnp.bfloat16)
        return carry

    lax.fori_loop(0, target.shape[0], body, 0)


def fetch(pairs, local):
    copies = [
        pltpu.make_async_copy(source, target, local.at[number])
        for number, (source, target) in enumerate(pairs)
    ]
    for copy in copies:
        copy.start()
    for copy in copies:
        copy.wait()


EVERYONE = [("dp", 1), ("dp", 2), ("dp", 3), ("expert", 1), ("ctx", 1), ("ctx", 2), ("ctx", 3)]


def returning_kernel(
    blocks_ref, moe_blocks, give3, keep3, give2, keep2, give1, keep1, give0,
    after_ref, input_ref, gates_ref, grad_ref, gain_ref, pack_ref, attended_ref,
    grad_after_ref, seq_grad_ref, grad_pack_ref, output_ref, arrived, done3, ready2, ready1,
    routed, over, sums, parts, fold_sends, fold_receives, fold_local,
    moe_over, moe_sums, moe_parts, moe_sends, moe_receives, moe_local,
    sent, crossed, stage, outgoing, sends, receives, local,
):
    z, c = lax.axis_index("dp"), lax.axis_index("ctx")
    greet(EVERYONE)
    link = Link(sends, receives)
    fold = Fold(blocks_ref, routed, over, sums, parts, fold_sends, fold_receives, fold_local)
    moe_fold = Fold(
        moe_blocks, routed.at[:, :D], moe_over, moe_sums, moe_parts, moe_sends, moe_receives, moe_local
    )
    gives = {3: give3, 2: give2, 1: give1, 0: give0}
    keeps = {3: keep3, 2: keep2, 1: keep1}
    core = {step: link.push(gives[step], arrived.at[step], "ctx", 1) for step in (3, 2, 1, 0)}
    fold.start()
    pair = {}
    count = stage.shape[1]

    def cross(step, cut):
        core[step].wait_recv()
        fetch([(keeps[step].at[1], stage.at[0]), (arrived.at[step, 1], stage.at[1])], local)
        add_into(sent.at[step - 1], [stage.at[0], stage.at[1]])
        source, target = sent.at[step - 1], crossed.at[step - 1]
        if cut:
            pair[step] = [
                link.push(source.at[item], target.at[item], "ctx", 2) for item in range(count)
            ]
        else:
            pair[step] = [link.push(source, target, "ctx", 2)]

    def close(step):
        fetch([(keeps[step].at[0], stage.at[2]), (arrived.at[step, 0], stage.at[3])], local)
        for copy in pair[step]:
            copy.wait_recv()
            copy.wait_send()
        add_into(sent.at[step - 1], [stage.at[2], stage.at[3], crossed.at[step - 1]])

    line = []

    def close_one(item):
        pair[3][item].wait_recv()
        pair[3][item].wait_send()
        sent[2, item] = (
            stage[2, item].astype(jnp.float32)
            + stage[3, item].astype(jnp.float32)
            + crossed[2, item].astype(jnp.float32)
        ).astype(jnp.bfloat16)
        line.append(link.push(sent.at[2, item], done3.at[item], "dp", 3))

    cross(3, True)
    fetch([(keep3.at[0], stage.at[2]), (arrived.at[3, 0], stage.at[3])], local)
    close_one(0)
    fold.early(0)
    close_one(1)
    cross(2, False)
    close_one(2)
    fold.early(1)
    for item in range(3, count):
        close_one(item)
    cross(1, False)
    fold.late()
    moe_fold.start()
    fold.last()
    moe_fold.early(0, middle=False)

    gates = gates_ref[...]
    high = routed[:, D:]
    lane = lax.broadcasted_iota(jnp.int32, high.shape, 1)
    grad_gates = jnp.where(lane < EXPERTS, high + pltpu.roll(high, 128 - EXPERTS, 1), 0.0)
    grad_picked = gates * (grad_gates - jnp.sum(gates * grad_gates, axis=-1, keepdims=True))
    grad_logits = grad_picked.astype(jnp.bfloat16)
    grad_input = routed[:, :D] + lax.dot_general(
        grad_logits,
        pack_ref[:, D:],
        (((1,), (1,)), ((), ())),
        preferred_element_type=jnp.float32,
    )
    normed, factor = normalize(after_ref[...])
    grad_after = grad_ref[...].astype(jnp.float32) + norm_back(
        grad_input * gain_ref[...], normed, factor
    )
    grad_after_ref[...] = grad_after
    grad_branch = (RESIDUAL_SCALE * grad_after).astype(jnp.bfloat16)
    wide = outgoing.shape[2]
    for index in range(outgoing.shape[0]):
        outgoing[index] = lax.dot_general(
            grad_branch,
            pack_ref[index * wide : (index + 1) * wide, :D],
            (((1,), (1,)), ((), ())),
            preferred_element_type=jnp.float32,
        ).astype(jnp.bfloat16)
    seq_grad_ref[c] = outgoing[c]
    spread = [
        link.push(outgoing.at[near(c, "ctx", flip)], seq_grad_ref.at[c], "ctx", flip)
        for flip in (1, 2, 3)
    ]
    moe_fold.early(0, ends=False)
    moe_fold.early(1, middle=False)
    close(2)
    keep_ready = [pltpu.make_async_copy(sent.at[1], ready2, local.at[0])]
    keep_ready[0].start()
    turned = (((0,), (0,)), ((), ()))
    column = (lane == EXPERTS).astype(jnp.bfloat16)
    small = lax.dot_general(
        input_ref[:, :D], grad_logits, turned, preferred_element_type=jnp.float32
    ) + lax.dot_general(
        (grad_input * normed).astype(jnp.bfloat16),
        column,
        turned,
        preferred_element_type=jnp.float32,
    )
    small = small.astype(jnp.bfloat16).reshape(grad_pack_ref.shape[:3] + (128,))
    grad_pack_ref[..., D:] = small
    moe_fold.early(1, ends=False)
    some = grad_pack_ref.shape[0] // outgoing.shape[0]
    for index in range(outgoing.shape[0]):
        part = lax.dot_general(
            attended_ref[index], grad_branch, turned, preferred_element_type=jnp.float32
        ).astype(jnp.bfloat16)
        grad_pack_ref[index * some : (index + 1) * some, :, :, :D] = part.reshape(
            (some,) + grad_pack_ref.shape[1:3] + (D,)
        )
    keep_ready[0].wait()
    moe_fold.late()
    close(1)
    fetch([(sent.at[0], ready1)], local)
    moe_fold.last()
    output_ref[...] = (after_ref[...] + RESIDUAL_SCALE * routed[:, :D]).astype(jnp.bfloat16)
    moe_fold.finish()
    for copy in spread + line + [core[0]]:
        copy.wait_recv()
    fold.finish()
    for copy in list(core.values()) + spread + line:
        copy.wait_send()


def returning(blocks, moe_blocks, parts, after, expert_input, gates, grads, gain, pack, attended, number):
    kind = jnp.bfloat16
    far = pl.BlockSpec(memory_space=pl.ANY)
    held = pl.BlockSpec(memory_space=pltpu.VMEM)
    give3, keep3, give2, keep2, give1, keep1, give0, _ = parts
    piece = give3.shape[1:]
    ctx, tokens, wide = attended.shape
    shape = blocks.shape[1:]
    return pl.pallas_call(
        returning_kernel,
        out_shape=(
            jax.ShapeDtypeStruct((tokens, D), jnp.float32),
            jax.ShapeDtypeStruct(attended.shape, kind),
            jax.ShapeDtypeStruct((8, ctx, D // (8 * ctx), shape[1]), kind),
            jax.ShapeDtypeStruct((tokens, D), kind),
            jax.ShapeDtypeStruct((4,) + give3.shape, kind),
            jax.ShapeDtypeStruct(piece, kind),
            jax.ShapeDtypeStruct(piece, kind),
            jax.ShapeDtypeStruct(piece, kind),
        ),
        in_specs=[far] * 9 + [held] * 7,
        out_specs=(held, held, held, held, far, far, far, far),
        scratch_shapes=[pltpu.VMEM(shape, jnp.float32)]
        + fold_scratch(shape)
        + [pltpu.SemaphoreType.DMA((4,))]
        + fold_scratch((tokens, D))
        + [
            pltpu.SemaphoreType.DMA((4,)),
            pltpu.VMEM((3,) + piece, kind),
            pltpu.VMEM((3,) + piece, kind),
            pltpu.VMEM((4,) + piece, kind),
            pltpu.VMEM(attended.shape, kind),
            pltpu.SemaphoreType.DMA((9 + 2 * piece[0],)),
            pltpu.SemaphoreType.DMA((9 + 2 * piece[0],)),
            pltpu.SemaphoreType.DMA((2,)),
        ],
        compiler_params=pltpu.CompilerParams(
            collective_id=number, has_side_effects=True, vmem_limit_bytes=63 * 1024 * 1024
        ),
    )(
        blocks, moe_blocks, give3, keep3, give2, keep2, give1, keep1, give0,
        after, expert_input, gates, grads, gain, pack, attended,
    )


def closing_kernel(
    ready2, ready1, keep0, arrived, table_ref, query_ref, keys_ref, values_ref, seq_grad_ref,
    normed_ref, columns_ref, grad_pack_ref, rows_ref, grad_after_ref,
    done2, done1, done0, input_grad_ref, shard_columns_ref, shard_pack_ref,
    sent, crossed, stage, mixed, flipped, grad_keys, grad_values,
    pack_core, pack_pair, pack_sent, pack_blocks, pack_over, pack_sums, pack_parts, pack_sends, pack_receives,
    scaled, scaled_core, scaled_pair, scaled_sent,
    part_blocks, part_out, part_over, part_sums, part_parts, part_sends, part_receives,
    sends, receives, local,
):
    z, c = lax.axis_index("dp"), lax.axis_index("ctx")
    greet(EVERYONE)
    link = Link(sends, receives)

    def c_at(flip):
        return near(c, "ctx", flip) if flip else c

    to_core = [
        link.push(grad_pack_ref.at[:, c_at(flip)], pack_core.at[number], "ctx", 1)
        for number, flip in enumerate((3, 1))
    ]
    line = [link.push(ready2, done2, "dp", 2), link.push(ready1, done1, "dp", 1)]
    zones = grad_pack_ref.shape[0]
    to_core[0].wait_recv()
    for zone in range(zones):
        pack_sent[zone] = (
            grad_pack_ref[zone, c_at(2)].astype(jnp.float32)
            + pack_core[0, zone].astype(jnp.float32)
        ).astype(jnp.bfloat16)
    pack_over_pair = link.push(pack_sent, pack_pair, "ctx", 2)
    fetch([(keep0.at[1], stage.at[0]), (arrived.at[0, 1], stage.at[1])], local)
    add_into(sent, [stage.at[0], stage.at[1]])
    pair = link.push(sent, crossed, "ctx", 2)
    attend_back(
        table_ref, query_ref, keys_ref, values_ref, seq_grad_ref, mixed, flipped, grad_keys, grad_values
    )
    blocks, block = scaled.shape[:2]
    for index in range(blocks):
        scaled[index] = lax.dot_general(
            mixed[index * block : (index + 1) * block, :],
            columns_ref[...],
            (((1,), (1,)), ((), ())),
            preferred_element_type=jnp.float32,
        ).astype(jnp.bfloat16)
    scaled_to_core = [
        link.push(scaled.at[c_at(flip)], scaled_core.at[number], "ctx", 1)
        for number, flip in enumerate((3, 1))
    ]
    wide = normed_ref.shape[1] // blocks
    some = zones // blocks
    for index in range(blocks):
        part = lax.dot_general(
            normed_ref[:, index * wide : (index + 1) * wide],
            mixed[...],
            (((0,), (0,)), ((), ())),
            preferred_element_type=jnp.float32,
        ).astype(jnp.bfloat16)
        part_blocks[index * some : (index + 1) * some] = part.reshape(
            (some,) + part_blocks.shape[1:]
        )
    part_fold = Fold(
        part_blocks, part_out, part_over, part_sums, part_parts, part_sends, part_receives
    )
    part_fold.start()
    scaled_to_core[0].wait_recv()
    scaled_sent[...] = (
        scaled[c_at(2)].astype(jnp.float32) + scaled_core[0].astype(jnp.float32)
    ).astype(jnp.bfloat16)
    scaled_over_pair = link.push(scaled_sent, scaled_pair, "ctx", 2)
    to_core[1].wait_recv()
    pack_over_pair.wait_recv()
    for zone in range(zones):
        pack_blocks[zone] = (
            grad_pack_ref[zone, c].astype(jnp.float32)
            + pack_core[1, zone].astype(jnp.float32)
            + pack_pair[zone].astype(jnp.float32)
        ).astype(jnp.bfloat16)
    pack_fold = Fold(
        pack_blocks, shard_pack_ref, pack_over, pack_sums, pack_parts, pack_sends, pack_receives
    )
    pack_fold.start()
    part_fold.early(0)
    part_fold.early(1)
    pack_fold.early(0)
    pack_fold.early(1)
    part_fold.late()
    part_fold.last()
    apart = [
        link.push(part_out.at[c_at(flip)], shard_columns_ref.at[c], "ctx", flip)
        for flip in (1, 2, 3)
    ]
    shard_columns_ref[c] = part_out[c]
    scaled_to_core[1].wait_recv()
    scaled_over_pair.wait_recv()
    grad_normed = (
        scaled[c].astype(jnp.float32)
        + scaled_core[1].astype(jnp.float32)
        + scaled_pair[...].astype(jnp.float32)
    )
    normed, factor = normalize(rows_ref[...].astype(jnp.float32))
    input_grad_ref[...] = grad_after_ref[...] + norm_back(grad_normed, normed, factor)
    pack_fold.late()
    pack_fold.last()
    fetch([(keep0.at[0], stage.at[0]), (arrived.at[0, 0], stage.at[1])], local)
    pair.wait_recv()
    pair.wait_send()
    add_into(sent, [stage.at[0], stage.at[1], crossed])
    fetch([(sent, done0)], local)
    for copy in apart + line:
        copy.wait_recv()
    part_fold.finish()
    pack_fold.finish()
    for copy in link.started:
        if copy is not pair:
            copy.wait_send()


def closing(
    ready2, ready1, keep0, arrived, table, query, keys, values, seq_grad, normed, columns,
    grad_pack, rows, grad_after, number,
):
    kind = jnp.bfloat16
    far = pl.BlockSpec(memory_space=pl.ANY)
    held = pl.BlockSpec(memory_space=pltpu.VMEM)
    piece = ready2.shape
    heads, length = query.shape[:2]
    groups = keys.shape[0]
    zones, ctx, share, wide = grad_pack.shape
    width = columns.shape[1]
    pack = (zones, share, wide)
    block = (length // ctx, D)
    part = (ctx, share, width)
    return pl.pallas_call(
        closing_kernel,
        out_shape=(
            jax.ShapeDtypeStruct(piece, kind),
            jax.ShapeDtypeStruct(piece, kind),
            jax.ShapeDtypeStruct(piece, kind),
            jax.ShapeDtypeStruct(rows.shape, jnp.float32),
            jax.ShapeDtypeStruct(part, kind),
            jax.ShapeDtypeStruct((share, wide), jnp.float32),
        ),
        in_specs=[far] * 4 + [held] * 10,
        out_specs=(far, far, far, held, held, held),
        scratch_shapes=[
            pltpu.VMEM(piece, kind),
            pltpu.VMEM(piece, kind),
            pltpu.VMEM((2,) + piece, kind),
            pltpu.VMEM((length, width), kind),
            pltpu.VMEM((groups * HD, length), kind),
            pltpu.VMEM((groups, length, HD), jnp.float32),
            pltpu.VMEM((groups, length, HD), jnp.float32),
            pltpu.VMEM((2,) + pack, kind),
            pltpu.VMEM(pack, kind),
            pltpu.VMEM(pack, kind),
            pltpu.VMEM(pack, kind),
        ]
        + fold_scratch(pack[1:])
        + [
            pltpu.VMEM((ctx,) + block, kind),
            pltpu.VMEM((2,) + block, kind),
            pltpu.VMEM(block, kind),
            pltpu.VMEM(block, kind),
            pltpu.VMEM((zones,) + part, kind),
            pltpu.VMEM(part, kind),
        ]
        + fold_scratch(part)
        + [
            pltpu.SemaphoreType.DMA((12,)),
            pltpu.SemaphoreType.DMA((12,)),
            pltpu.SemaphoreType.DMA((2,)),
        ],
        compiler_params=pltpu.CompilerParams(
            collective_id=number, has_side_effects=True, vmem_limit_bytes=62 * 1024 * 1024
        ),
    )(
        ready2, ready1, keep0, arrived, table, query, keys, values, seq_grad, normed, columns,
        grad_pack, rows, grad_after,
    )


def route_rows(rows, pack_ref, attended_ref, routes_ref, after_ref, gates_ref, gain_ref, packed):
    quarters = attended_ref.shape[0]
    wide = pack_ref.shape[-1]
    branch = jnp.zeros((rows.shape[0], D), jnp.float32)
    tails = []
    for index in range(quarters):
        pack = pack_ref[index].reshape(-1, wide)
        branch += jnp.dot(attended_ref[index], pack[:, :D], preferred_element_type=jnp.float32)
        tails.append(pack[:, D:])
    tail = jnp.concatenate(tails, 0)
    after = rows.astype(jnp.float32) + RESIDUAL_SCALE * branch
    after_ref[...] = after
    normed, _ = normalize(after)
    single = lax.broadcasted_iota(jnp.int32, (8, 128), 1) == EXPERTS
    gain = lax.dot_general(
        single.astype(jnp.bfloat16),
        tail,
        (((1,), (1,)), ((), ())),
        preferred_element_type=jnp.float32,
    )[:1]
    gain_ref[...] = gain
    expert_input = (normed * gain).astype(jnp.bfloat16)
    logits = jnp.dot(expert_input, tail, preferred_element_type=jnp.float32)
    lane = lax.broadcasted_iota(jnp.int32, logits.shape, 1)
    marks = jnp.zeros(logits.shape, jnp.float32)
    for index in range(TOP):
        marks = jnp.where(lane == routes_ref[:, index : index + 1], 1.0, marks)
    chosen = marks > 0.0
    peak = jnp.max(jnp.where(chosen, logits, -3e38), axis=-1, keepdims=True)
    raised = jnp.where(chosen, jnp.exp(jnp.where(chosen, logits - peak, 0.0)), 0.0)
    gates = raised / jnp.sum(raised, axis=-1, keepdims=True)
    gates_ref[...] = gates
    high = gates.astype(jnp.bfloat16).astype(jnp.float32)
    packed[:, :D] = expert_input
    packed[:, D:] = (
        high + pltpu.roll(gates - high, EXPERTS, 1) + pltpu.roll(marks, 2 * EXPERTS, 1)
    ).astype(jnp.bfloat16)


def opening_kernel(
    rows_ref, table_ref, columns_ref, pack_ref, weights_in, weights_out, grads_ref, routes_ref,
    all_rows, all_table, all_columns, all_pack, pieces_in, pieces_out, all_grads, all_packed,
    after_ref, gates_ref, gain_ref, packed,
    normed_ref, query_ref, keys_ref, values_ref, attended_ref,
    outgoing, flipped, sends, receives, line_sends, line_receives, token_sends, token_receives, locals_,
):
    z, y, c = lax.axis_index("dp"), lax.axis_index("expert"), lax.axis_index("ctx")
    greet(EVERYONE)
    link = Link(sends, receives)
    line = Line(grads_ref, all_grads, line_sends, line_receives)
    token_line = Line(packed, all_packed, token_sends, token_receives)
    own = 2 * z + y
    count = weights_in.shape[1]

    def z_at(flip):
        return near(z, "dp", flip) if flip else z

    def c_at(flip):
        return near(c, "ctx", flip) if flip else c

    def keep(number, source, target):
        copy = pltpu.make_async_copy(source, target, locals_.at[number])
        copy.start()
        return copy

    def both(target, source, axis, flip):
        return [link.push(source(ref), target(ref), axis, flip) for ref in (pieces_in, pieces_out)]

    def share(*place):
        step, rest = place[0], place[1:]
        source = lambda ref: ref.at[(step, 0) + rest]
        over = both(lambda ref: ref.at[(step, 2) + rest], source, "ctx", 2)
        core = both(lambda ref: ref.at[(step, 1) + rest], source, "ctx", 1)
        return over, core

    def hand_on(*place):
        step, rest = place[0], place[1:]
        return both(
            lambda ref: ref.at[(step, 3) + rest], lambda ref: ref.at[(step, 2) + rest], "ctx", 1
        )

    def move(step, *rest):
        return [
            link.push(weights.at[(z_at(step),) + rest], ref.at[(step, 0) + rest], "dp", step)
            for weights, ref in ((weights_in, pieces_in), (weights_out, pieces_out))
        ]

    def arrive(copies):
        for copy in copies:
            copy.wait_recv()

    kept = [
        keep(0, columns_ref.at[c], all_columns.at[own, c]),
        keep(1, weights_in.at[z], pieces_in.at[0, 0]),
        keep(2, weights_out.at[z], pieces_out.at[0, 0]),
        keep(3, rows_ref, all_rows.at[c]),
        keep(4, pack_ref, all_pack.at[z, y, c]),
        keep(5, grads_ref, all_grads.at[own]),
        keep(7, table_ref, all_table.at[c]),
    ]
    cut = [
        link.push(columns_ref.at[c_at(flip)], all_columns.at[own, c], "ctx", flip)
        for flip in (1, 2, 3)
    ]
    table_all = [link.push(table_ref, all_table.at[c], "ctx", flip) for flip in (1, 2, 3)]
    rows_over = link.push(rows_ref, all_rows.at[c], "ctx", 2)
    rows_core = link.push(rows_ref, all_rows.at[c], "ctx", 1)
    pack_line = [link.push(pack_ref, all_pack.at[z, y, c], "dp", flip) for flip in (1, 2, 3)]
    kept[0].wait()
    arrive(cut)
    column_line = [
        link.push(all_columns.at[own], all_columns.at[own], "dp", flip) for flip in (1, 2, 3)
    ]
    column_over = [link.push(all_columns.at[own], all_columns.at[own], "expert", 1)]
    kept[1].wait()
    kept[2].wait()
    rows_over.wait_recv()
    rows_pass = link.push(all_rows.at[c_at(2)], all_rows.at[c_at(2)], "ctx", 1)
    shared = [share(0)]
    arrive(pack_line)
    kept[4].wait()
    pack_over = link.push(all_pack.at[:, y, c], all_pack.at[:, y, c], "expert", 1)
    for flip in (1, 2, 3):
        column_line[flip - 1].wait_recv()
        block = all_columns.at[2 * z_at(flip) + y]
        column_over.append(link.push(block, block, "expert", 1))
    moved = {1: move(1), 2: move(2)}
    line.start()
    arrive([pack_over])
    pack_pair = link.push(all_pack.at[:, :, c], all_pack.at[:, :, c], "ctx", 2)
    pack_core = link.push(all_pack.at[:, :, c], all_pack.at[:, :, c], "ctx", 1)
    arrive([rows_core, rows_pass] + column_over + table_all)
    kept[3].wait()
    kept[6].wait()
    project_rows(
        all_rows,
        all_table,
        all_columns[...].reshape(D, all_columns.shape[-1]),
        normed_ref,
        query_ref,
        keys_ref,
        values_ref,
        flipped,
    )
    for index in range(all_rows.shape[0]):
        attend_rows(index, all_rows.shape[1], query_ref, keys_ref, outgoing, flipped)
    attended = [
        link.push(outgoing.at[c_at(flip)], attended_ref.at[c], "ctx", flip) for flip in (1, 2, 3)
    ]
    attended_ref[c] = outgoing[c]
    arrive([pack_pair])
    pack_last = link.push(all_pack.at[:, :, c_at(2)], all_pack.at[:, :, c_at(2)], "ctx", 1)
    arrive([pack_core, pack_last] + attended)
    route_rows(
        all_rows[c], all_pack, attended_ref, routes_ref, after_ref, gates_ref, gain_ref, packed
    )
    token_line.start()
    kept.append(keep(6, packed, all_packed.at[own]))
    line.first()
    arrive(shared[0][0])
    passed = hand_on(0)
    arrive(moved[1])
    shared.append(share(1))
    line.second()
    token_line.first()
    line.third()
    token_line.second()
    arrive(moved[2])
    shared.append(share(2))
    last = [move(3, 0), move(3, 1)]
    token_line.third()
    arrive(shared[1][0])
    passed += hand_on(1)

    def next_piece(item):
        arrive(last[item])
        if item + 2 < count:
            last.append(move(3, item + 2))
        shared.append(share(3, item))

    for item in range(count):
        next_piece(item)
    arrive(shared[2][0])
    passed += hand_on(2)
    for item in range(count):
        arrive(shared[3 + item][0])
        passed += hand_on(3, item)
    kept[5].wait()
    kept[7].wait()
    arrive(passed)
    for over, core in shared:
        arrive(core)
    line.finish()
    token_line.finish()
    link.finish()


def opening(rows, table, columns, pack, weights_in, weights_out, grads, routes, heads, groups, number):
    ctx = columns.shape[0]
    shards, count = weights_in.shape[:2]
    tokens = rows.shape[0]
    kind = jnp.bfloat16
    copies = 27 + 2 * (2 + 3 * 3 + 5 * count)
    far = pl.BlockSpec(memory_space=pl.ANY)
    held = pl.BlockSpec(memory_space=pltpu.VMEM)
    all_rows = (ctx,) + rows.shape
    return pl.pallas_call(
        opening_kernel,
        out_shape=(
            jax.ShapeDtypeStruct(all_rows, kind),
            jax.ShapeDtypeStruct((ctx,) + table.shape, kind),
            jax.ShapeDtypeStruct((8,) + columns.shape, kind),
            jax.ShapeDtypeStruct((shards, 2, ctx) + pack.shape, kind),
            jax.ShapeDtypeStruct((shards, ctx) + weights_in.shape[1:], kind),
            jax.ShapeDtypeStruct((shards, ctx) + weights_out.shape[1:], kind),
            jax.ShapeDtypeStruct((8,) + grads.shape, kind),
            jax.ShapeDtypeStruct((8, tokens, D + 128), kind),
            jax.ShapeDtypeStruct((tokens, D), jnp.float32),
            jax.ShapeDtypeStruct((tokens, 128), jnp.float32),
            jax.ShapeDtypeStruct((1, D), jnp.float32),
            jax.ShapeDtypeStruct((tokens, D + 128), kind),
        )
        + attend_shapes(all_rows, heads, groups),
        in_specs=[far] * 7 + [held],
        out_specs=(held, held, held, held, far, far, far, far) + (held,) * 9,
        scratch_shapes=[
            pltpu.VMEM((ctx, rows.shape[0], heads * HD), kind),
            pltpu.VMEM((groups * HD, ctx * rows.shape[0]), kind),
            pltpu.SemaphoreType.DMA((copies,)),
            pltpu.SemaphoreType.DMA((copies,)),
            pltpu.SemaphoreType.DMA((9,)),
            pltpu.SemaphoreType.DMA((8,)),
            pltpu.SemaphoreType.DMA((9,)),
            pltpu.SemaphoreType.DMA((8,)),
            pltpu.SemaphoreType.DMA((8,)),
        ],
        compiler_params=pltpu.CompilerParams(
            collective_id=number, has_side_effects=True, vmem_limit_bytes=56 * 1024 * 1024
        ),
    )(rows, table, columns, pack, weights_in, weights_out, grads, routes)


def split_high_low(values):
    high = values.astype(jnp.bfloat16)
    return high, (values - high.astype(jnp.float32)).astype(jnp.bfloat16)


def pad_columns(like, columns):
    return jnp.zeros((like.shape[0], columns), like.dtype)


def gather_ctx(rows):
    ctx = lax.axis_size("ctx")
    column = lax.axis_index("ctx")
    pieces = {0: rows}
    flip = ctx // 2
    while flip:
        pieces.update({turn ^ flip: swap(item, "ctx", flip) for turn, item in pieces.items()})
        flip //= 2
    out = jnp.zeros((ctx,) + rows.shape, rows.dtype)
    for turn in range(ctx):
        out = lax.dynamic_update_index_in_dim(out, pieces[turn], column ^ turn, 0)
    return out


def exchange_ctx(blocks):
    column = lax.axis_index("ctx")
    out = jnp.zeros(blocks.shape, blocks.dtype)
    for turn in range(blocks.shape[0]):
        item = lax.dynamic_index_in_dim(blocks, column ^ turn, 0, keepdims=False)
        if turn:
            item = swap(item, "ctx", turn)
        out = lax.dynamic_update_index_in_dim(out, item, column ^ turn, 0)
    return out


def scatter_ctx(blocks):
    column = lax.axis_index("ctx")
    flip = 1
    held = blocks
    while flip < lax.axis_size("ctx"):
        pairs = held.reshape((held.shape[0] // 2, 2) + held.shape[1:])
        bit = (column // flip) % 2
        keep = lax.dynamic_index_in_dim(pairs, bit, 1, keepdims=False)
        give = lax.dynamic_index_in_dim(pairs, 1 - bit, 1, keepdims=False)
        held = keep.astype(jnp.float32) + swap(give, "ctx", flip).astype(jnp.float32)
        flip *= 2
        if flip < lax.axis_size("ctx"):
            held = held.astype(jnp.bfloat16)
    return held[0]


def group_columns(rows, ctx):
    depth = rows.shape[0]
    cuts = (rows[:, : H * HD], rows[:, H * HD : (H + KV) * HD], rows[:, (H + KV) * HD :])
    return jnp.concatenate([cut.reshape(depth, ctx, -1) for cut in cuts], -1).transpose(1, 0, 2)


def ungroup_columns(groups):
    ctx, depth, _ = groups.shape
    query, key = H * HD // ctx, KV * HD // ctx
    cuts = (groups[..., :query], groups[..., query : query + key], groups[..., query + key :])
    return jnp.concatenate([cut.transpose(1, 0, 2).reshape(depth, -1) for cut in cuts], 1)


def block_order():
    shards, ctx = lax.axis_size("dp"), lax.axis_size("ctx")
    place, column = lax.axis_index("dp"), lax.axis_index("ctx")
    return place, column, shards, ctx


def fold_weights(expert_in, expert_out):
    deep = expert_out.shape[1]
    folds = expert_in.shape[1] // deep
    cuts = [expert_in[:, fold * deep : (fold + 1) * deep] for fold in range(folds)]
    return jnp.concatenate(cuts + [expert_out], -1)


def piece_order():
    place, column, shards, ctx = block_order()
    blocks = [
        (place ^ step) * ctx + (column ^ turn) for step in range(shards) for turn in range(ctx)
    ]
    return jnp.stack(blocks).astype(jnp.int32)


def spread_weights(expert_in, expert_out):
    shards = lax.axis_size("dp")
    count, depth = expert_in.shape[:2]
    part = FFE // shards
    cut = expert_in.reshape(count, depth, 2, shards, part).transpose(3, 0, 1, 2, 4)
    moved_in = lax.all_to_all(cut, "dp", split_axis=0, concat_axis=0, tiled=True)
    all_in = lax.all_gather(moved_in.transpose(1, 0, 2, 3, 4), "ctx", axis=2, tiled=True)
    all_out = lax.all_gather(expert_out, "ctx", axis=1, tiled=True)
    return [all_in.reshape(count, -1, 2 * part), all_out]


def collect_weights(grad_in, grad_out):
    shards = lax.axis_size("dp")
    count = grad_in.shape[0]
    part = FFE // shards
    part_in = lax.psum_scatter(
        grad_in.reshape(count, shards, -1, 2, part), "ctx", scatter_dimension=2, tiled=True
    )
    own_in = lax.all_to_all(
        part_in.transpose(1, 0, 2, 3, 4), "dp", split_axis=0, concat_axis=0, tiled=True
    )
    own_in = own_in.transpose(1, 2, 3, 0, 4).reshape(count, -1, 2 * FFE)
    own_out = lax.psum_scatter(grad_out, "ctx", scatter_dimension=1, tiled=True)
    return [(0, fold_weights(own_in, own_out))]


def expert_step_kernel(places_ref, *refs):
    states, outs = refs[-14:-8], refs[-8:]
    grads = refs[:-14]
    number = pl.program_id(0)
    wide = states[0].shape[2]
    deep = states[3].shape[1]
    folds = states[0].shape[1] // deep
    rates = learn_rates()

    def update(grad_ref):
        for fold in range(folds):
            span = pl.ds(fold * deep, deep)
            grad = grad_ref[0, :, fold * wide : (fold + 1) * wide].astype(jnp.float32)
            news = adam_step(
                states[0][0, span, :],
                states[1][0, span, :],
                states[2][0, span, :],
                grad,
                DECAY_RATE,
                rates[5],
            )
            for out, new in zip(outs[:4], news):
                out[0, span, :] = new
        grad = grad_ref[0, :, folds * wide :].astype(jnp.float32)
        news = adam_step(states[3][0], states[4][0], states[5][0], grad, DECAY_RATE, rates[6])
        for out, new in zip(outs[4:], news):
            out[0] = new

    count = pl.num_programs(0) // len(grads)
    for index, grad_ref in enumerate(grads):
        pl.when(number // count == index)(functools.partial(update, grad_ref))


def expert_step(places, grads, states):
    count = grads[0].shape[0]
    shapes = [states[1].shape] * 4 + [states[4].shape] * 4
    moved = lambda e, p: (p[e // count] * count + e % count, 0, 0)
    block = lambda shape: pl.BlockSpec((1,) + shape[1:], moved)

    def grad_spec(index):
        return pl.BlockSpec(
            (1,) + grads[0].shape[1:], lambda e, p: (jnp.clip(e - index * count, 0, count - 1), 0, 0)
        )

    return pl.pallas_call(
        expert_step_kernel,
        grid_spec=pltpu.PrefetchScalarGridSpec(
            num_scalar_prefetch=1,
            grid=(count * len(grads),),
            in_specs=[grad_spec(index) for index in range(len(grads))]
            + [block(state.shape) for state in states],
            out_specs=tuple(block(shape) for shape in shapes),
        ),
        out_shape=tuple(jax.ShapeDtypeStruct(shape, jnp.float32) for shape in shapes),
        compiler_params=pltpu.CompilerParams(vmem_limit_bytes=62 * 1024 * 1024),
        cost_estimate=pl.CostEstimate(flops=1, bytes_accessed=1, transcendentals=0),
    )(places, *grads, *states)


def local(
    tokens,
    cotangent,
    routes,
    positions,
    gain_attend,
    gain_attend_mean,
    gain_attend_square,
    project_in,
    project_in_mean,
    project_in_square,
    project_out,
    project_out_mean,
    project_out_square,
    gain_expert,
    gain_expert_mean,
    gain_expert_square,
    router_weight,
    router_weight_mean,
    router_weight_square,
    expert_in,
    expert_in_mean,
    expert_in_square,
    expert_out,
    expert_out_mean,
    expert_out_square,
):
    everywhere = ("dp", "expert", "ctx")
    owners = ("dp", "expert")
    shards = lax.axis_size("dp")
    planes = lax.axis_size("expert")
    ctx = lax.axis_size("ctx")
    rows_local = tokens.shape[0]
    local_count = expert_in.shape[0]
    close = (shards, planes, ctx) == (4, 2, 4) and local_count % shards == 0
    heads, groups = H // ctx, KV // ctx
    hidden_in = tokens.astype(jnp.float32)

    half = HD // 2
    freqs = ROPE_BASE ** (-jnp.arange(half, dtype=jnp.float32) * 2.0 / HD)
    angles = positions.astype(jnp.float32)[:, None] * freqs[None, :]
    table = jnp.concatenate(split_high_low(jnp.cos(angles)) + split_high_low(jnp.sin(angles)), 1)
    gain_attend_wide = gain_attend.astype(jnp.float32)[:, None]
    scaled_in = (gain_attend_wide * project_in.astype(jnp.float32)).astype(jnp.bfloat16)
    columns = group_columns(scaled_in, ctx)
    pack_out = jnp.concatenate(
        [project_out, router_weight, gain_expert[:, None], pad_columns(project_out, 87)], 1
    )
    order = piece_order()
    if close:
        parted = lambda array: array.reshape((shards, -1) + array.shape[1:])
        (
            _, seq_table, own_in, full_pack_out, all_in, all_out, all_grads, all_packed,
            after, gates_wide, gain_two, packed,
            seq_normed, query, keys, values, attended_heads,
        ) = opening(
            tokens, table, columns, pack_out, parted(expert_in), parted(expert_out), cotangent, routes,
            heads, groups, 1,
        )
        pieces = [array.reshape((-1,) + array.shape[2:]) for array in (all_in, all_out)]
    else:
        seq_rows, seq_table = gather_ctx(tokens), gather_ctx(table)
        own_in = lax.all_gather(exchange_ctx(columns), owners, axis=0, tiled=False)
        full_pack_out = lax.all_gather(pack_out, everywhere, axis=0, tiled=True)
        all_grads = lax.all_gather(cotangent, owners, axis=0, tiled=False)
        pieces = spread_weights(expert_in, expert_out)
        seq_normed, query, keys, values, seq_attended = attend_forward(
            seq_rows, seq_table, own_in.reshape(D, -1), heads, groups
        )
        attended_heads = exchange_ctx(seq_attended)
    seq_table = seq_table.reshape(-1, 128)
    own_in = own_in.reshape(D, -1)
    full_pack_out = full_pack_out.reshape(H * HD, -1)
    if not close:
        full_out = full_pack_out[:, :D]
        full_router = full_pack_out[:, D : D + EXPERTS]
        gain_two = full_pack_out[:, D + EXPERTS].astype(jnp.float32)[None]
        attended = attended_heads.transpose(1, 0, 2).reshape(rows_local, H * HD)
        branch = jnp.dot(attended, full_out, preferred_element_type=jnp.float32)
        after = hidden_in + RESIDUAL_SCALE * branch
        normed_two, factor_two = normalize(after)
        expert_input = (normed_two * gain_two).astype(jnp.bfloat16)
        logits = jnp.dot(expert_input, full_router, preferred_element_type=jnp.float32)
        chosen = jnp.any(routes[:, :, None] == jnp.arange(EXPERTS, dtype=jnp.int32), axis=1)
        peak = jnp.max(jnp.where(chosen, logits, -3e38), axis=-1, keepdims=True)
        raised = jnp.where(chosen, jnp.exp(jnp.where(chosen, logits - peak, 0.0)), 0.0)
        gates = raised / jnp.sum(raised, axis=-1, keepdims=True)
        packed = jnp.concatenate(
            (expert_input,)
            + split_high_low(gates)
            + (chosen.astype(jnp.bfloat16), pad_columns(expert_input, 128 - 3 * EXPERTS)),
            1,
        )
        all_packed = lax.all_gather(packed, owners, axis=0, tiled=False)

    first = lax.axis_index("expert") * local_count
    count = local_count
    hidden = FFE // shards
    if close:
        count = local_count // shards
        hidden = FFE
        first = first + lax.axis_index("dp") * count
    first = first.astype(jnp.int32).reshape(1)
    slot_rows, slot_grads, pick = dispatch(first, all_packed, all_grads, count)
    produced, grad_rows, parts = run_experts(
        first, order, slot_rows, slot_grads, pieces, hidden, close
    )
    shared_grads = combine(pick, grad_rows)
    shared = combine(pick, produced)
    if close:
        place = lax.axis_index("dp")
        (
            grad_after, seq_grad, grad_pack_out, block_output, arrived, done3, ready2, ready1,
        ) = returning(
            shared_grads,
            shared,
            parts,
            after,
            packed,
            gates_wide,
            cotangent,
            gain_two,
            full_pack_out,
            attended_heads,
            3,
        )
        done2, done1, done0, input_grad, shard_columns, shard_pack_out = closing(
            ready2,
            ready1,
            parts[7],
            arrived,
            seq_table,
            query,
            keys,
            values,
            seq_grad,
            seq_normed,
            own_in,
            grad_pack_out,
            tokens,
            grad_after,
            4,
        )
        expert_grads = [
            (near(place, "dp", 3), done3),
            (near(place, "dp", 2), done2),
            (near(place, "dp", 1), done1),
            (place, done0),
        ]
    else:
        grad_routed = lax.psum_scatter(
            shared_grads, owners, scatter_dimension=0, tiled=False
        ).astype(jnp.float32)
        moe = lax.psum_scatter(shared, owners, scatter_dimension=0, tiled=False)
        block_output = (after + RESIDUAL_SCALE * moe.astype(jnp.float32)).astype(jnp.bfloat16)
        expert_grads = collect_weights(*parts)
        grad_final = cotangent.astype(jnp.float32)
        grad_gates = grad_routed[:, D : D + EXPERTS] + grad_routed[:, D + EXPERTS : D + 2 * EXPERTS]
        grad_picked = gates * (grad_gates - jnp.sum(gates * grad_gates, axis=-1, keepdims=True))
        grad_logits = grad_picked.astype(jnp.bfloat16)
        grad_from_router = jnp.einsum(
            "te,de->td", grad_logits, full_router, preferred_element_type=jnp.float32
        )
        grad_input = grad_from_router + grad_routed[:, :D]
        grad_after = grad_final + norm_back(grad_input * gain_two, normed_two, factor_two)
        grad_branch = (RESIDUAL_SCALE * grad_after).astype(jnp.bfloat16)
        grad_attended = jnp.einsum(
            "td,cd->tc", grad_branch, full_out, preferred_element_type=jnp.float32
        ).astype(jnp.bfloat16)
        seq_grad = exchange_ctx(
            grad_attended.reshape(rows_local, ctx, heads * HD).transpose(1, 0, 2)
        )
        grad_mixed = attend_backward(seq_table, query, keys, values, seq_grad)
        grad_in_part = jnp.einsum(
            "td,tc->dc", seq_normed, grad_mixed, preferred_element_type=jnp.float32
        ).astype(jnp.bfloat16)
        grad_in_part = grad_in_part.reshape(shards * planes, -1, grad_in_part.shape[1])
        shard_columns = lax.psum_scatter(grad_in_part, owners, scatter_dimension=0, tiled=False)
        shard_columns = exchange_ctx(shard_columns.reshape(ctx, -1, shard_columns.shape[-1]))
        grad_scaled = jnp.einsum(
            "tc,dc->td", grad_mixed, own_in, preferred_element_type=jnp.float32
        ).astype(jnp.bfloat16)
        grad_normed = scatter_ctx(grad_scaled.reshape(ctx, rows_local, D))
        normed_one, factor_one = normalize(hidden_in)
        input_grad = grad_after + norm_back(grad_normed, normed_one, factor_one)
        grad_project_out = jnp.einsum(
            "tc,td->cd", attended, grad_branch, preferred_element_type=jnp.float32
        ).astype(jnp.bfloat16)
        ones = jnp.where(jnp.arange(128) == EXPERTS, 1.0, 0.0).astype(jnp.bfloat16)
        grad_small = jnp.einsum(
            "td,te->de",
            jnp.concatenate([expert_input, (grad_input * normed_two).astype(jnp.bfloat16)], 0),
            jnp.concatenate(
                [
                    jnp.pad(grad_logits, ((0, 0), (0, 128 - EXPERTS))),
                    jnp.broadcast_to(ones, (rows_local, 128)),
                ],
                0,
            ),
            preferred_element_type=jnp.float32,
        ).astype(jnp.bfloat16)
        grad_pack_out = jnp.concatenate([grad_project_out, grad_small], 1)
        shard_pack_out = lax.psum_scatter(
            grad_pack_out, everywhere, scatter_dimension=0, tiled=True
        ).astype(jnp.float32)
    shard_scaled = ungroup_columns(shard_columns).astype(jnp.float32)
    shard_in = gain_attend_wide * shard_scaled
    shard_attend = jnp.sum(shard_scaled * project_in.astype(jnp.float32), axis=1)
    shard_out = shard_pack_out[:, :D]
    shard_router = shard_pack_out[:, D : D + EXPERTS]
    shard_expert = shard_pack_out[:, D + EXPERTS]
    rates = learn_rates()
    results = [block_output, input_grad]
    results.extend(
        adam_step(gain_attend, gain_attend_mean, gain_attend_square, shard_attend, 0.0, rates[0])
    )
    results.extend(
        adam_step(project_in, project_in_mean, project_in_square, shard_in, DECAY_RATE, rates[1])
    )
    results.extend(
        adam_step(
            project_out, project_out_mean, project_out_square, shard_out, DECAY_RATE, rates[2]
        )
    )
    results.extend(
        adam_step(gain_expert, gain_expert_mean, gain_expert_square, shard_expert, 0.0, rates[3])
    )
    results.extend(
        adam_step(
            router_weight,
            router_weight_mean,
            router_weight_square,
            shard_router,
            DECAY_RATE,
            rates[4],
        )
    )
    states = (expert_in, expert_in_mean, expert_in_square, expert_out, expert_out_mean, expert_out_square)
    places = jnp.stack([jnp.asarray(place, jnp.int32) for place, _ in expert_grads])
    expert_outs = expert_step(places, [folded for _, folded in expert_grads], states)
    results.extend(expert_outs)
    return tuple(results)


def solution(mesh):
    placed = (
        P(("dp", "expert", "ctx"), None),
        P(("dp", "expert", "ctx"), None),
        P(("dp", "expert", "ctx"), None),
        P(("dp", "expert", "ctx")),
        P(("dp", "expert", "ctx")),
        P(("dp", "expert", "ctx")),
        P(("dp", "expert", "ctx")),
        P(("dp", "expert", "ctx"), None),
        P(("dp", "expert", "ctx"), None),
        P(("dp", "expert", "ctx"), None),
        P(("dp", "expert", "ctx"), None),
        P(("dp", "expert", "ctx"), None),
        P(("dp", "expert", "ctx"), None),
        P(("dp", "expert", "ctx")),
        P(("dp", "expert", "ctx")),
        P(("dp", "expert", "ctx")),
        P(("dp", "expert", "ctx"), None),
        P(("dp", "expert", "ctx"), None),
        P(("dp", "expert", "ctx"), None),
        P("expert", ("dp", "ctx"), None),
        P("expert", ("dp", "ctx"), None),
        P("expert", ("dp", "ctx"), None),
        P("expert", ("dp", "ctx"), None),
        P("expert", ("dp", "ctx"), None),
        P("expert", ("dp", "ctx"), None),
    )
    return jax.shard_map(
        local,
        mesh=mesh,
        in_specs=placed,
        out_specs=(
            P(("dp", "expert", "ctx"), None),
            P(("dp", "expert", "ctx"), None),
            P(("dp", "expert", "ctx")),
            P(("dp", "expert", "ctx")),
            P(("dp", "expert", "ctx")),
            P(("dp", "expert", "ctx")),
            P(("dp", "expert", "ctx"), None),
            P(("dp", "expert", "ctx"), None),
            P(("dp", "expert", "ctx"), None),
            P(("dp", "expert", "ctx"), None),
            P(("dp", "expert", "ctx"), None),
            P(("dp", "expert", "ctx"), None),
            P(("dp", "expert", "ctx"), None),
            P(("dp", "expert", "ctx"), None),
            P(("dp", "expert", "ctx")),
            P(("dp", "expert", "ctx")),
            P(("dp", "expert", "ctx")),
            P(("dp", "expert", "ctx")),
            P(("dp", "expert", "ctx"), None),
            P(("dp", "expert", "ctx"), None),
            P(("dp", "expert", "ctx"), None),
            P(("dp", "expert", "ctx"), None),
            P("expert", ("dp", "ctx"), None),
            P("expert", ("dp", "ctx"), None),
            P("expert", ("dp", "ctx"), None),
            P("expert", ("dp", "ctx"), None),
            P("expert", ("dp", "ctx"), None),
            P("expert", ("dp", "ctx"), None),
            P("expert", ("dp", "ctx"), None),
            P("expert", ("dp", "ctx"), None),
        ),
        check_vma=False,
    )
```

```python
import functools

import jax
import jax.numpy as jnp
from jax import lax
from jax.experimental import pallas as pl
from jax.experimental.pallas import tpu as pltpu
from jax.sharding import PartitionSpec as P

D = 1536
H = 24
KV = 8
HD = 64
FFE = 512
EXPERTS = 40
TOP = 8
STEP = 8
CAP = 64


EPS_NORM = 1e-06
ATTN_SCALE = 0.015625
RESIDUAL_SCALE = 0.22
BETA_ONE = 0.9
BETA_TWO = 0.95
ADAM_EPS = 1e-08
DECAY_RATE = 0.1
ROPE_BASE = 10000.0


def normalize(rows):
    factor = lax.rsqrt(jnp.mean(rows * rows, axis=-1, keepdims=True) + EPS_NORM)
    return (rows * factor, factor)


def norm_back(grad_normed, normed, factor):
    return factor * (grad_normed - normed * jnp.mean(grad_normed * normed, axis=-1, keepdims=True))


def learn_rates():
    return (
        0.3,
        3.0 / (D // 16) ** 0.5,
        3.0 / (D // 12) ** 0.5,
        0.3,
        3.0 / (4 * D) ** 0.5,
        3.0 / D**0.5,
        3.0 / (FFE // 32) ** 0.5,
    )


def adam_step(weight, first, second, grad, decay, rate):
    new_first = BETA_ONE * first + (1.0 - BETA_ONE) * grad
    new_second = BETA_TWO * second + (1.0 - BETA_TWO) * grad * grad
    corrected = (new_first * (1.0 / (1.0 - BETA_ONE**STEP))) / (
        jnp.sqrt(new_second * (1.0 / (1.0 - BETA_TWO**STEP))) + ADAM_EPS
    )
    old = weight.astype(jnp.float32)
    return (grad, new_first, new_second, old - rate * (corrected + decay * old))


def lane_tables(table):
    half = HD // 2
    source = lax.broadcasted_iota(jnp.int32, (128, 128), 0)
    target = lax.broadcasted_iota(jnp.int32, (128, 128), 1)
    same = (source % half) == (target % half)
    group = source // half
    first = (target % HD) < half
    cosine = jnp.where(same & (group < 2), 1.0, 0.0).astype(jnp.bfloat16)
    ahead = jnp.where(same & (group >= 2) & first, -1.0, 0.0).astype(jnp.bfloat16)
    behind = jnp.where(same & (group >= 2) & jnp.logical_not(first), 1.0, 0.0).astype(jnp.bfloat16)
    return tuple(
        jnp.dot(table, item, preferred_element_type=jnp.float32)
        for item in (cosine, ahead, behind)
    )


def turn_lanes(block, tables, sign):
    cosine, ahead, behind = tables
    half = HD // 2
    turned = pltpu.roll(block, 128 - half, 1) * ahead + pltpu.roll(block, half, 1) * behind
    return block * cosine + sign * turned


def scores_of(keys, query, start, length):
    scores = (
        lax.dot_general(
            keys, query, (((1,), (1,)), ((), ())), preferred_element_type=jnp.float32
        )
        * ATTN_SCALE
    )
    rows = lax.broadcasted_iota(jnp.int32, scores.shape, 0)
    columns = lax.broadcasted_iota(jnp.int32, scores.shape, 1) + start
    return jnp.where(rows <= columns, scores, -1e30)


def project_rows(rows_ref, table_ref, weight, normed_ref, query_ref, keys_ref, values_ref, flipped):
    blocks, block = rows_ref.shape[:2]
    heads, groups = query_ref.shape[0], keys_ref.shape[0]
    wide = heads * HD
    for index in range(blocks):
        span = pl.ds(index * block, block)
        rows = rows_ref[index].astype(jnp.float32)
        factor = lax.rsqrt(jnp.mean(rows * rows, axis=-1, keepdims=True) + EPS_NORM)
        normed = (rows * factor).astype(jnp.bfloat16)
        normed_ref[span, :] = normed
        tables = lane_tables(table_ref[index])
        mixed = jnp.dot(normed, weight, preferred_element_type=jnp.float32)
        for column in range(0, wide + 2 * groups * HD, 128):
            part = mixed[:, column : column + 128]
            if column < wide + groups * HD:
                part = turn_lanes(part, tables, 1.0)
            else:
                flipped[column - wide - groups * HD : column - wide - groups * HD + 128, span] = (
                    part.T.astype(jnp.bfloat16)
                )
            part = part.astype(jnp.bfloat16)
            for half in range(2):
                head = column // HD + half
                piece = part[:, half * HD : (half + 1) * HD]
                if head < heads:
                    query_ref[head, span, :] = piece
                elif head < heads + groups:
                    keys_ref[head - heads, span, :] = piece
                else:
                    values_ref[head - heads - groups, span, :] = piece


def attend_rows(index, block, query_ref, keys_ref, out_ref, flipped):
    heads, groups = query_ref.shape[0], keys_ref.shape[0]
    length = (index + 1) * block
    span = pl.ds(index * block, block)
    outputs = []
    for head in range(heads):
        group = head // (heads // groups)
        scores = scores_of(
            keys_ref[group, :length, :], query_ref[head, span, :], index * block, length
        )
        peak = jnp.max(scores, axis=0, keepdims=True)
        raised = jnp.exp(scores - peak)
        total = jnp.sum(raised, axis=0, keepdims=True)
        probs = (raised * (1.0 / total)).astype(jnp.bfloat16)
        outputs.append(
            jnp.dot(
                flipped[group * HD : (group + 1) * HD, :length],
                probs,
                preferred_element_type=jnp.float32,
            )
        )
    out_ref[index] = jnp.concatenate(outputs, 0).T.astype(jnp.bfloat16)


def attend_kernel(rows_ref, table_ref, weight_ref, normed_ref, query_ref, keys_ref, values_ref, out_ref, flipped):
    project_rows(rows_ref, table_ref, weight_ref[...], normed_ref, query_ref, keys_ref, values_ref, flipped)
    for index in range(rows_ref.shape[0]):
        attend_rows(index, rows_ref.shape[1], query_ref, keys_ref, out_ref, flipped)


def attend_shapes(rows, heads, groups):
    blocks, block = rows[:2]
    length = blocks * block
    return (
        jax.ShapeDtypeStruct((length, D), jnp.bfloat16),
        jax.ShapeDtypeStruct((heads, length, HD), jnp.bfloat16),
        jax.ShapeDtypeStruct((groups, length, HD), jnp.bfloat16),
        jax.ShapeDtypeStruct((groups, length, HD), jnp.bfloat16),
        jax.ShapeDtypeStruct((blocks, block, heads * HD), jnp.bfloat16),
    )


def attend_back(rows_ref, query_ref, keys_ref, values_ref, grad_ref, out_ref, flipped, grad_keys, grad_values, between=None):
    block = 256
    blocks = rows_ref.shape[0] // block
    heads, groups = query_ref.shape[0], keys_ref.shape[0]
    repeat = heads // groups
    wide = heads * HD
    for group in range(groups):
        flipped[group * HD : (group + 1) * HD, :] = (
            keys_ref[group].astype(jnp.float32).T.astype(jnp.bfloat16)
        )
    grad_keys[...] = jnp.zeros_like(grad_keys)
    grad_values[...] = jnp.zeros_like(grad_values)
    for index in range(blocks):
        length = (index + 1) * block
        span = pl.ds(index * block, block)
        outputs = []
        for head in range(heads):
            group = head // repeat
            query = query_ref[head, span, :]
            grad = grad_ref[index, :, head * HD : (head + 1) * HD]
            scores = scores_of(keys_ref[group, :length, :], query, index * block, length)
            peak = jnp.max(scores, axis=0, keepdims=True)
            raised = jnp.exp(scores - peak)
            total = jnp.sum(raised, axis=0, keepdims=True)
            probs = raised * (1.0 / total)
            grad_probs = lax.dot_general(
                values_ref[group, :length, :],
                grad,
                (((1,), (1,)), ((), ())),
                preferred_element_type=jnp.float32,
            )
            middle = jnp.sum(probs * grad_probs, axis=0, keepdims=True)
            grad_scores = (probs * (grad_probs - middle)).astype(jnp.bfloat16)
            grad_keys[group, :length, :] += jnp.dot(
                grad_scores, query, preferred_element_type=jnp.float32
            )
            grad_values[group, :length, :] += jnp.dot(
                probs.astype(jnp.bfloat16), grad, preferred_element_type=jnp.float32
            )
            outputs.append(
                jnp.dot(
                    flipped[group * HD : (group + 1) * HD, :length],
                    grad_scores,
                    preferred_element_type=jnp.float32,
                )
            )
        tables = lane_tables(rows_ref[span, :])
        stacked = jnp.concatenate(outputs, 0).T * ATTN_SCALE
        for column in range(0, wide, 128):
            out_ref[span, column : column + 128] = turn_lanes(
                stacked[:, column : column + 128], tables, -1.0
            ).astype(jnp.bfloat16)
        if between is not None and index == 1:
            between()
    for index in range(blocks):
        span = pl.ds(index * block, block)
        tables = lane_tables(rows_ref[span, :])
        keys = jnp.concatenate([grad_keys[group, span, :] for group in range(groups)], 1)
        values = jnp.concatenate([grad_values[group, span, :] for group in range(groups)], 1)
        keys = turn_lanes(keys * ATTN_SCALE, tables, -1.0)
        out_ref[span, wide : wide + groups * HD] = keys.astype(jnp.bfloat16)
        out_ref[span, wide + groups * HD :] = values.astype(jnp.bfloat16)


def attend_forward(rows, table, weight, heads, groups):
    return pl.pallas_call(
        attend_kernel,
        out_shape=attend_shapes(rows.shape, heads, groups),
        scratch_shapes=[pltpu.VMEM((groups * HD, rows.shape[0] * rows.shape[1]), jnp.bfloat16)],
        compiler_params=pltpu.CompilerParams(vmem_limit_bytes=48 * 1024 * 1024),
        cost_estimate=pl.CostEstimate(flops=1, bytes_accessed=1, transcendentals=0),
    )(rows, table, weight)


def attend_backward(table, query, keys, values, grad):
    heads, length = query.shape[:2]
    groups = keys.shape[0]
    return pl.pallas_call(
        attend_back,
        out_shape=jax.ShapeDtypeStruct((length, (heads + 2 * groups) * HD), jnp.bfloat16),
        scratch_shapes=[
            pltpu.VMEM((groups * HD, length), jnp.bfloat16),
            pltpu.VMEM((groups, length, HD), jnp.float32),
            pltpu.VMEM((groups, length, HD), jnp.float32),
        ],
        compiler_params=pltpu.CompilerParams(vmem_limit_bytes=48 * 1024 * 1024),
        cost_estimate=pl.CostEstimate(flops=1, bytes_accessed=1, transcendentals=0),
    )(table, query, keys, values, grad)


def dispatch_kernel(first_ref, rows_ref, grads_ref, out_rows, out_grads, out_pick):
    count = out_rows.shape[0]
    tokens = rows_ref.shape[1]
    padded = -(-count // 16) * 16
    tail = rows_ref[0, :, D:]
    lane = lax.broadcasted_iota(jnp.int32, (padded, 128), 1)
    row = lax.broadcasted_iota(jnp.int32, (padded, 128), 0)
    wanted = (lane == 2 * EXPERTS + first_ref[0] + row) & (row < count)
    marks = lax.dot_general(
        wanted.astype(jnp.bfloat16),
        tail,
        (((1,), (1,)), ((), ())),
        preferred_element_type=jnp.float32,
    )
    earlier = lax.broadcasted_iota(jnp.int32, (tokens, tokens), 0) < lax.broadcasted_iota(
        jnp.int32, (tokens, tokens), 1
    )
    rank = jnp.dot(
        marks.astype(jnp.bfloat16),
        earlier.astype(jnp.bfloat16),
        preferred_element_type=jnp.float32,
    )
    slot = lax.broadcasted_iota(jnp.int32, (CAP, tokens), 0).astype(jnp.float32)
    pick = jnp.concatenate(
        [
            jnp.where(
                rank[item : item + 1, :] == slot, marks[item : item + 1, :], 0.0
            ).astype(jnp.bfloat16)
            for item in range(count)
        ],
        0,
    )
    out_pick[0] = pick
    moved = jnp.dot(pick, rows_ref[0], preferred_element_type=jnp.float32).astype(jnp.bfloat16)
    moved_grads = jnp.dot(pick, grads_ref[0], preferred_element_type=jnp.float32).astype(
        jnp.bfloat16
    )
    for item in range(count):
        out_rows[item] = moved[item * CAP : (item + 1) * CAP]
        out_grads[item] = moved_grads[item * CAP : (item + 1) * CAP]


def dispatch(first, rows, grads, count):
    sources, tokens, wide = rows.shape
    return pl.pallas_call(
        dispatch_kernel,
        grid_spec=pltpu.PrefetchScalarGridSpec(
            num_scalar_prefetch=1,
            grid=(sources,),
            in_specs=[
                pl.BlockSpec((1, tokens, wide), lambda s, f: (s, 0, 0)),
                pl.BlockSpec((1, tokens, D), lambda s, f: (s, 0, 0)),
            ],
            out_specs=(
                pl.BlockSpec((count, CAP, wide), lambda s, f: (0, s, 0)),
                pl.BlockSpec((count, CAP, D), lambda s, f: (0, s, 0)),
                pl.BlockSpec((1, count * CAP, tokens), lambda s, f: (s, 0, 0)),
            ),
        ),
        out_shape=(
            jax.ShapeDtypeStruct((count, sources * CAP, wide), jnp.bfloat16),
            jax.ShapeDtypeStruct((count, sources * CAP, D), jnp.bfloat16),
            jax.ShapeDtypeStruct((sources, count * CAP, tokens), jnp.bfloat16),
        ),
        compiler_params=pltpu.CompilerParams(vmem_limit_bytes=62 * 1024 * 1024),
        cost_estimate=pl.CostEstimate(flops=1, bytes_accessed=1, transcendentals=0),
    )(first, rows, grads)


def combine_kernel(pick_ref, *refs):
    half = len(refs) // 2
    for rows_ref, out_ref in zip(refs[:half], refs[half:]):
        rows = jnp.concatenate([rows_ref[item] for item in range(rows_ref.shape[0])], 0)
        out_ref[0] = lax.dot_general(
            pick_ref[0], rows, (((0,), (0,)), ((), ())), preferred_element_type=jnp.float32
        ).astype(jnp.bfloat16)


def combine(pick, arrays):
    sources, slots, tokens = pick.shape
    count = arrays[0].shape[0]
    return pl.pallas_call(
        combine_kernel,
        grid=(sources,),
        in_specs=[pl.BlockSpec((1, slots, tokens), lambda s: (s, 0, 0))]
        + [pl.BlockSpec((count, CAP, rows.shape[2]), lambda s: (0, s, 0)) for rows in arrays],
        out_specs=tuple(
            pl.BlockSpec((1, tokens, rows.shape[2]), lambda s: (s, 0, 0)) for rows in arrays
        ),
        out_shape=tuple(
            jax.ShapeDtypeStruct((sources, tokens, rows.shape[2]), jnp.bfloat16)
            for rows in arrays
        ),
        compiler_params=pltpu.CompilerParams(vmem_limit_bytes=62 * 1024 * 1024),
        cost_estimate=pl.CostEstimate(flops=1, bytes_accessed=1, transcendentals=0),
    )(pick, *arrays)


def expert_kernel(first_ref, order_ref, slots_ref, rows_ref, grads_ref, *refs):
    whole_in, whole_out, total_in, total_out = refs[-4:]
    pieces, (produced_ref, grad_rows_ref), outs = refs[:2], refs[2:4], refs[4:-4]
    expert = first_ref[0] + pl.program_id(0)
    chunk = pl.program_id(1)
    parted = len(pieces[0].shape) == 4

    @pl.when(chunk == 0)
    def assemble():
        if not parted:
            whole_in[...] = pieces[0][0]
            whole_out[...] = pieces[1][0]
            return
        for index in range(pieces[0].shape[0]):
            block = order_ref[index]
            for piece, whole in zip(pieces, (whole_in, whole_out)):
                deep = piece.shape[2]
                whole[pl.ds(pl.multiple_of(block * deep, deep), deep), :] = piece[index, 0]

    tail = rows_ref[0, :, D:].astype(jnp.float32)
    lane = lax.broadcasted_iota(jnp.int32, tail.shape, 1)
    own = (lane == expert) | (lane == EXPERTS + expert)
    gate = jnp.sum(jnp.where(own, tail, 0.0), axis=-1, keepdims=True)
    hidden = whole_out.shape[0]
    gate_up = jnp.dot(rows_ref[0, :, :D], whole_in[...], preferred_element_type=jnp.float32)
    gate_half = gate_up[:, :hidden]
    up_half = gate_up[:, hidden:]
    sigma = 1.0 / (1.0 + jnp.exp(-gate_half))
    activated = gate_half * sigma
    middle = activated * up_half
    gated = (gate * middle).astype(jnp.bfloat16)
    produced_ref[0] = jnp.dot(gated, whole_out[...], preferred_element_type=jnp.float32).astype(
        jnp.bfloat16
    )
    grad_middle = RESIDUAL_SCALE * lax.dot_general(
        grads_ref[0],
        whole_out[...],
        (((1,), (1,)), ((), ())),
        preferred_element_type=jnp.float32,
    )
    grad_gate = jnp.sum(middle * grad_middle, axis=-1, keepdims=True)
    grad_middle = gate * grad_middle
    slope = sigma * (1.0 + gate_half * (1.0 - sigma))
    grad_hidden = jnp.concatenate(
        [grad_middle * up_half * slope, grad_middle * activated], -1
    ).astype(jnp.bfloat16)
    grad_rows_ref[0, :, :D] = lax.dot_general(
        grad_hidden,
        whole_in[...],
        (((1,), (1,)), ((), ())),
        preferred_element_type=jnp.float32,
    ).astype(jnp.bfloat16)
    high = grad_gate.astype(jnp.bfloat16).astype(jnp.float32)
    spread = jnp.where(
        lane == expert, high, jnp.where(lane == EXPERTS + expert, grad_gate - high, 0.0)
    )
    grad_rows_ref[0, :, D:] = spread.astype(jnp.bfloat16)

    turned = (((0,), (0,)), ((), ()))
    part_in = lax.dot_general(
        rows_ref[0, :, :D], grad_hidden, turned, preferred_element_type=jnp.float32
    )
    part_out = RESIDUAL_SCALE * lax.dot_general(
        gated, grads_ref[0], turned, preferred_element_type=jnp.float32
    )

    @pl.when(chunk == 0)
    def store():
        total_in[...] = part_in
        total_out[...] = part_out

    @pl.when(chunk > 0)
    def add():
        total_in[...] += part_in
        total_out[...] += part_out

    @pl.when(chunk == pl.num_programs(1) - 1)
    def finish():
        if not parted:
            outs[0][0] = total_in[...].astype(jnp.bfloat16)
            outs[1][0] = total_out[...].astype(jnp.bfloat16)
            return
        wide = total_in.shape[1]
        turns = outs[0].shape[0]
        deep = outs[0].shape[2]
        folds = (outs[0].shape[3] - D) // wide
        for number, out in enumerate(outs):
            for turn in range(turns):
                block = slots_ref[number * turns + turn]
                for fold in range(folds):
                    start = pl.multiple_of((block * folds + fold) * deep, deep)
                    out[turn, 0, :, fold * wide : (fold + 1) * wide] = total_in[
                        pl.ds(start, deep), :
                    ].astype(jnp.bfloat16)
                start = pl.multiple_of(block * deep, deep)
                out[turn, 0, :, folds * wide :] = total_out[pl.ds(start, deep), :].astype(
                    jnp.bfloat16
                )


def run_experts(first, order, rows, grads, pieces, hidden, parted):
    count, slots, wide = rows.shape
    chunk = min(512, slots)
    by_chunk = lambda e, c, *_: (e, c, 0)
    by_expert = lambda e, c, *_: (e, 0, 0)
    by_turn = lambda e, c, *_: (0, e, 0, 0)
    if parted:
        _, _, shards, ctx = block_order()
        places = []
        for step in reversed(range(shards)):
            for bit in (1, 0):
                places += [step * ctx + turn for turn in range(bit, ctx, 2)]
        places = jnp.stack([order[place] for place in places])
        deep = pieces[1].shape[2]
        folds = pieces[0].shape[2] // deep
        shapes = [(ctx // 2, count, deep, folds * 2 * hidden + D)] * (2 * shards)
        block = lambda shape: pl.BlockSpec((shape[0], 1) + shape[2:], by_turn)
    else:
        places = order
        shapes = [(count, D, 2 * hidden), (count, hidden, D)]
        block = lambda shape: pl.BlockSpec((1,) + shape[1:], by_expert)
    outs = pl.pallas_call(
        expert_kernel,
        grid_spec=pltpu.PrefetchScalarGridSpec(
            num_scalar_prefetch=3,
            grid=(count, slots // chunk),
            in_specs=[
                pl.BlockSpec((1, chunk, wide), by_chunk),
                pl.BlockSpec((1, chunk, D), by_chunk),
            ]
            + [block(piece.shape) for piece in pieces],
            out_specs=(
                pl.BlockSpec((1, chunk, D), by_chunk),
                pl.BlockSpec((1, chunk, wide), by_chunk),
            )
            + tuple(block(shape) for shape in shapes),
            scratch_shapes=[
                pltpu.VMEM((D, 2 * hidden), jnp.bfloat16),
                pltpu.VMEM((hidden, D), jnp.bfloat16),
                pltpu.VMEM((D, 2 * hidden), jnp.float32),
                pltpu.VMEM((hidden, D), jnp.float32),
            ],
        ),
        out_shape=(
            jax.ShapeDtypeStruct((count, slots, D), jnp.bfloat16),
            jax.ShapeDtypeStruct((count, slots, wide), jnp.bfloat16),
        )
        + tuple(jax.ShapeDtypeStruct(shape, jnp.bfloat16) for shape in shapes),
        compiler_params=pltpu.CompilerParams(vmem_limit_bytes=62 * 1024 * 1024),
        cost_estimate=pl.CostEstimate(flops=1, bytes_accessed=1, transcendentals=0),
    )(first, order, places, rows, grads, *pieces)
    return outs[0], outs[1], outs[2:]


def swap(rows, axis, flip):
    size = lax.axis_size(axis)
    return lax.ppermute(rows, axis, [(i, i ^ flip) for i in range(size)])


def near(place, axis, flip):
    if lax.axis_size(axis) == 2:
        return 1 - place
    if flip == 1:
        return place + 1 - 2 * lax.rem(place, 2)
    if flip == 2:
        return lax.rem(place + 2, 4)
    return 3 - place


def greet(partners):
    barrier = pltpu.get_barrier_semaphore()
    for axis, flip in partners:
        pl.semaphore_signal(
            barrier,
            inc=1,
            device_id={axis: near(lax.axis_index(axis), axis, flip)},
            device_id_type=pl.DeviceIdType.MESH,
        )
    pl.semaphore_wait(barrier, len(partners))


class Link:
    def __init__(self, sends, receives):
        self.sends, self.receives, self.used, self.started = sends, receives, 0, []

    def push(self, source, target, axis, flip):
        copy = pltpu.make_async_remote_copy(
            src_ref=source,
            dst_ref=target,
            send_sem=self.sends.at[self.used],
            recv_sem=self.receives.at[self.used],
            device_id={axis: near(lax.axis_index(axis), axis, flip)},
            device_id_type=pl.DeviceIdType.MESH,
        )
        copy.start()
        self.used += 1
        self.started.append(copy)
        return copy

    def finish(self):
        for copy in self.started:
            copy.wait_send()


class Line:
    def __init__(self, rows_ref, out_ref, sends, receives):
        z, y = lax.axis_index("dp"), lax.axis_index("expert")
        self.inner = z * (3 - z) > 0
        self.outer = z * (3 - z) < 1

        def slot(flip):
            return 2 * (near(z, "dp", flip) if flip else z) + y

        def hand(sent, received, source, target, flip, axis="dp"):
            return pltpu.make_async_remote_copy(
                src_ref=source,
                dst_ref=target,
                send_sem=sends.at[sent],
                recv_sem=receives.at[received],
                device_id={axis: near(lax.axis_index(axis), axis, flip)},
                device_id_type=pl.DeviceIdType.MESH,
            )

        def block(flip):
            return out_ref.at[slot(flip)]

        self.to_first = hand(0, 1, rows_ref, block(0), 1)
        self.across_own = hand(1, 3, rows_ref, block(0), 3)
        self.across_first = hand(2, 2, block(1), block(1), 3)
        self.pass_third = hand(3, 2, block(3), block(3), 1)
        self.pass_second = hand(8, 3, block(2), block(2), 1)
        self.over = [
            hand(4 + flip, 4 + flip, block(flip) if flip else rows_ref, block(flip), 1, "expert")
            for flip in range(4)
        ]
        self.got = [None] + [hand(0, flip, block(flip), block(flip), 1) for flip in range(1, 4)]
        self.got_over = [
            hand(0, 4 + flip, block(flip), out_ref.at[slot(flip) + 1 - 2 * y], 1, "expert")
            for flip in range(4)
        ]

    def start(self):
        self.to_first.start()

        @pl.when(self.inner)
        def inner():
            self.across_own.start()

        self.over[0].start()

    def first(self):
        self.got[1].wait_recv()

        @pl.when(self.inner)
        def inner():
            self.across_first.start()

        self.over[1].start()

    def second(self):
        @pl.when(self.inner)
        def inner():
            self.got[3].wait_recv()
            self.pass_third.start()
            self.over[3].start()

        @pl.when(self.outer)
        def outer():
            self.got[2].wait_recv()
            self.over[2].start()

    def third(self):
        @pl.when(self.inner)
        def inner():
            self.got[2].wait_recv()
            self.pass_second.start()
            self.over[2].start()

        @pl.when(self.outer)
        def outer():
            self.got[3].wait_recv()
            self.over[3].start()

    def finish(self):
        self.to_first.wait_send()

        @pl.when(self.inner)
        def inner():
            for copy in (self.across_own, self.across_first, self.pass_third, self.pass_second):
                copy.wait_send()

        for copy in self.over:
            copy.wait_send()
        for copy in self.got_over:
            copy.wait_recv()


class Fold:
    def __init__(self, blocks_ref, out_ref, over, sums, parts, sends, receives, local=None):
        z, y = lax.axis_index("dp"), lax.axis_index("expert")
        self.inner = z * (3 - z) > 0
        self.outer = z * (3 - z) < 1
        self.blocks, self.out, self.over, self.sums, self.parts = blocks_ref, out_ref, over, sums, parts
        self.y = y

        def slot(flip, plane):
            return 2 * (near(z, "dp", flip) if flip else z) + plane

        def hand(number, source, target, flip, axis="dp"):
            return pltpu.make_async_remote_copy(
                src_ref=source,
                dst_ref=target,
                send_sem=sends.at[number],
                recv_sem=receives.at[number],
                device_id={axis: near(lax.axis_index(axis), axis, flip)},
                device_id_type=pl.DeviceIdType.MESH,
            )

        self.slot = slot
        self.staged = [
            pltpu.make_async_copy(blocks_ref.at[slot(flip, y)], sums.at[flip], local.at[flip])
            for flip in range(4 if local is not None else 0)
        ]
        self.across = [
            hand(flip, blocks_ref.at[slot(flip, 1 - y)], over.at[flip], 1, "expert")
            for flip in range(4)
        ]
        self.to_line = [hand(4 + k, sums.at[3 - k], parts.at[k], 1) for k in range(3)]
        self.to_middle = [hand(7 + k, sums.at[2 + k], parts.at[3 + k], 3) for k in range(2)]
        self.to_end = hand(9, sums.at[1], parts.at[5], 1)

    def own(self, flip):
        self.across[flip].wait_recv()
        if self.staged:
            self.staged[flip].wait()
            held = self.sums[flip]
        else:
            held = self.blocks[self.slot(flip, self.y)]
        return held.astype(jnp.float32) + self.over[flip].astype(jnp.float32)

    def part(self, number):
        return self.parts[number].astype(jnp.float32)

    def start(self):
        @pl.when(self.inner)
        def inner():
            for flip in (2, 3, 1, 0):
                self.across[flip].start()

        @pl.when(self.outer)
        def outer():
            for flip in (3, 2, 1, 0):
                self.across[flip].start()

        for copy in self.staged:
            copy.start()

    def early(self, k, ends=True, middle=True):
        if middle:

            @pl.when(self.inner)
            def inner():
                total = self.own(2 + k)
                self.to_line[k].wait_recv()
                self.sums[2 + k] = (total + self.part(k)).astype(jnp.bfloat16)
                self.to_middle[k].start()

        if ends:

            @pl.when(self.outer)
            def outer():
                self.sums[3 - k] = self.own(3 - k).astype(jnp.bfloat16)
                self.to_line[k].start()

    def late(self):
        @pl.when(self.inner)
        def inner():
            total = self.own(1)
            self.to_middle[0].wait_recv()
            self.sums[1] = (total + self.part(3)).astype(jnp.bfloat16)
            self.to_end.start()

        @pl.when(self.outer)
        def outer():
            self.sums[1] = self.own(1).astype(jnp.bfloat16)
            self.to_line[2].start()

    def last(self):
        @pl.when(self.inner)
        def inner():
            total = self.own(0)
            self.to_line[2].wait_recv()
            self.to_middle[1].wait_recv()
            self.out[...] = (total + self.part(2) + self.part(4)).astype(self.out.dtype)

        @pl.when(self.outer)
        def outer():
            total = self.own(0)
            self.to_end.wait_recv()
            self.out[...] = (total + self.part(5)).astype(self.out.dtype)

    def finish(self):
        @pl.when(self.inner)
        def inner():
            for copy in self.to_middle + [self.to_end]:
                copy.wait_send()

        @pl.when(self.outer)
        def outer():
            for copy in self.to_line:
                copy.wait_send()

        for copy in self.across:
            copy.wait_send()


def fold_scratch(shape):
    return [
        pltpu.VMEM((4,) + shape, jnp.bfloat16),
        pltpu.VMEM((4,) + shape, jnp.bfloat16),
        pltpu.VMEM((6,) + shape, jnp.bfloat16),
        pltpu.SemaphoreType.DMA((10,)),
        pltpu.SemaphoreType.DMA((10,)),
    ]


def add_into(target, sources):
    def body(item, carry):
        total = sources[0][item].astype(jnp.float32)
        for source in sources[1:]:
            total = total + source[item].astype(jnp.float32)
        target[item] = total.astype(jnp.bfloat16)
        return carry

    lax.fori_loop(0, target.shape[0], body, 0)


def fetch(pairs, local):
    copies = [
        pltpu.make_async_copy(source, target, local.at[number])
        for number, (source, target) in enumerate(pairs)
    ]
    for copy in copies:
        copy.start()
    for copy in copies:
        copy.wait()


EVERYONE = [("dp", 1), ("dp", 2), ("dp", 3), ("expert", 1), ("ctx", 1), ("ctx", 2), ("ctx", 3)]


def returning_kernel(
    blocks_ref, moe_blocks, give3, keep3, give2, keep2, give1, keep1, give0,
    after_ref, input_ref, gates_ref, grad_ref, gain_ref, pack_ref, attended_ref,
    grad_after_ref, seq_grad_ref, grad_pack_ref, output_ref, arrived, done3, ready2, ready1,
    routed, over, sums, parts, fold_sends, fold_receives, fold_local,
    moe_over, moe_sums, moe_parts, moe_sends, moe_receives, moe_local,
    sent, crossed, stage, outgoing, sends, receives, local,
):
    z, c = lax.axis_index("dp"), lax.axis_index("ctx")
    greet(EVERYONE)
    link = Link(sends, receives)
    fold = Fold(blocks_ref, routed, over, sums, parts, fold_sends, fold_receives, fold_local)
    moe_fold = Fold(
        moe_blocks, routed.at[:, :D], moe_over, moe_sums, moe_parts, moe_sends, moe_receives, moe_local
    )
    gives = {3: give3, 2: give2, 1: give1, 0: give0}
    keeps = {3: keep3, 2: keep2, 1: keep1}
    core = {step: link.push(gives[step], arrived.at[step], "ctx", 1) for step in (3, 2, 1, 0)}
    fold.start()
    pair = {}
    count = stage.shape[1]

    def cross(step, cut):
        core[step].wait_recv()
        fetch([(keeps[step].at[1], stage.at[0]), (arrived.at[step, 1], stage.at[1])], local)
        add_into(sent.at[step - 1], [stage.at[0], stage.at[1]])
        source, target = sent.at[step - 1], crossed.at[step - 1]
        if cut:
            pair[step] = [
                link.push(source.at[item], target.at[item], "ctx", 2) for item in range(count)
            ]
        else:
            pair[step] = [link.push(source, target, "ctx", 2)]

    def close(step):
        fetch([(keeps[step].at[0], stage.at[2]), (arrived.at[step, 0], stage.at[3])], local)
        for copy in pair[step]:
            copy.wait_recv()
            copy.wait_send()
        add_into(sent.at[step - 1], [stage.at[2], stage.at[3], crossed.at[step - 1]])

    line = []

    def close_one(item):
        pair[3][item].wait_recv()
        pair[3][item].wait_send()
        sent[2, item] = (
            stage[2, item].astype(jnp.float32)
            + stage[3, item].astype(jnp.float32)
            + crossed[2, item].astype(jnp.float32)
        ).astype(jnp.bfloat16)
        line.append(link.push(sent.at[2, item], done3.at[item], "dp", 3))

    cross(3, True)
    fetch([(keep3.at[0], stage.at[2]), (arrived.at[3, 0], stage.at[3])], local)
    close_one(0)
    fold.early(0)
    close_one(1)
    cross(2, False)
    close_one(2)
    fold.early(1)
    for item in range(3, count):
        close_one(item)
    cross(1, False)
    fold.late()
    moe_fold.start()
    fold.last()
    moe_fold.early(0, middle=False)

    gates = gates_ref[...]
    high = routed[:, D:]
    lane = lax.broadcasted_iota(jnp.int32, high.shape, 1)
    grad_gates = jnp.where(lane < EXPERTS, high + pltpu.roll(high, 128 - EXPERTS, 1), 0.0)
    grad_picked = gates * (grad_gates - jnp.sum(gates * grad_gates, axis=-1, keepdims=True))
    grad_logits = grad_picked.astype(jnp.bfloat16)
    grad_input = routed[:, :D] + lax.dot_general(
        grad_logits,
        pack_ref[:, D:],
        (((1,), (1,)), ((), ())),
        preferred_element_type=jnp.float32,
    )
    normed, factor = normalize(after_ref[...])
    grad_after = grad_ref[...].astype(jnp.float32) + norm_back(
        grad_input * gain_ref[...], normed, factor
    )
    grad_after_ref[...] = grad_after
    grad_branch = (RESIDUAL_SCALE * grad_after).astype(jnp.bfloat16)
    wide = outgoing.shape[2]
    for index in range(outgoing.shape[0]):
        outgoing[index] = lax.dot_general(
            grad_branch,
            pack_ref[index * wide : (index + 1) * wide, :D],
            (((1,), (1,)), ((), ())),
            preferred_element_type=jnp.float32,
        ).astype(jnp.bfloat16)
    seq_grad_ref[c] = outgoing[c]
    spread = [
        link.push(outgoing.at[near(c, "ctx", flip)], seq_grad_ref.at[c], "ctx", flip)
        for flip in (1, 2, 3)
    ]
    moe_fold.early(0, ends=False)
    moe_fold.early(1, middle=False)
    close(2)
    keep_ready = [pltpu.make_async_copy(sent.at[1], ready2, local.at[0])]
    keep_ready[0].start()
    turned = (((0,), (0,)), ((), ()))
    column = (lane == EXPERTS).astype(jnp.bfloat16)
    small = lax.dot_general(
        input_ref[:, :D], grad_logits, turned, preferred_element_type=jnp.float32
    ) + lax.dot_general(
        (grad_input * normed).astype(jnp.bfloat16),
        column,
        turned,
        preferred_element_type=jnp.float32,
    )
    small = small.astype(jnp.bfloat16).reshape(grad_pack_ref.shape[:3] + (128,))
    grad_pack_ref[..., D:] = small
    moe_fold.early(1, ends=False)
    some = grad_pack_ref.shape[0] // outgoing.shape[0]
    for index in range(outgoing.shape[0]):
        part = lax.dot_general(
            attended_ref[index], grad_branch, turned, preferred_element_type=jnp.float32
        ).astype(jnp.bfloat16)
        grad_pack_ref[index * some : (index + 1) * some, :, :, :D] = part.reshape(
            (some,) + grad_pack_ref.shape[1:3] + (D,)
        )
    keep_ready[0].wait()
    moe_fold.late()
    close(1)
    fetch([(sent.at[0], ready1)], local)
    moe_fold.last()
    output_ref[...] = (after_ref[...] + RESIDUAL_SCALE * routed[:, :D]).astype(jnp.bfloat16)
    moe_fold.finish()
    for copy in spread + line + [core[0]]:
        copy.wait_recv()
    fold.finish()
    for copy in list(core.values()) + spread + line:
        copy.wait_send()


def returning(blocks, moe_blocks, parts, after, expert_input, gates, grads, gain, pack, attended, number):
    kind = jnp.bfloat16
    far = pl.BlockSpec(memory_space=pl.ANY)
    held = pl.BlockSpec(memory_space=pltpu.VMEM)
    give3, keep3, give2, keep2, give1, keep1, give0, _ = parts
    piece = give3.shape[1:]
    ctx, tokens, wide = attended.shape
    shape = blocks.shape[1:]
    return pl.pallas_call(
        returning_kernel,
        out_shape=(
            jax.ShapeDtypeStruct((tokens, D), jnp.float32),
            jax.ShapeDtypeStruct(attended.shape, kind),
            jax.ShapeDtypeStruct((8, ctx, D // (8 * ctx), shape[1]), kind),
            jax.ShapeDtypeStruct((tokens, D), kind),
            jax.ShapeDtypeStruct((4,) + give3.shape, kind),
            jax.ShapeDtypeStruct(piece, kind),
            jax.ShapeDtypeStruct(piece, kind),
            jax.ShapeDtypeStruct(piece, kind),
        ),
        in_specs=[far] * 9 + [held] * 7,
        out_specs=(held, held, held, held, far, far, far, far),
        scratch_shapes=[pltpu.VMEM(shape, jnp.float32)]
        + fold_scratch(shape)
        + [pltpu.SemaphoreType.DMA((4,))]
        + fold_scratch((tokens, D))
        + [
            pltpu.SemaphoreType.DMA((4,)),
            pltpu.VMEM((3,) + piece, kind),
            pltpu.VMEM((3,) + piece, kind),
            pltpu.VMEM((4,) + piece, kind),
            pltpu.VMEM(attended.shape, kind),
            pltpu.SemaphoreType.DMA((9 + 2 * piece[0],)),
            pltpu.SemaphoreType.DMA((9 + 2 * piece[0],)),
            pltpu.SemaphoreType.DMA((2,)),
        ],
        compiler_params=pltpu.CompilerParams(
            collective_id=number, has_side_effects=True, vmem_limit_bytes=63 * 1024 * 1024
        ),
    )(
        blocks, moe_blocks, give3, keep3, give2, keep2, give1, keep1, give0,
        after, expert_input, gates, grads, gain, pack, attended,
    )


def closing_kernel(
    ready2, ready1, keep0, arrived, table_ref, query_ref, keys_ref, values_ref, seq_grad_ref,
    normed_ref, columns_ref, grad_pack_ref, rows_ref, grad_after_ref,
    done2, done1, done0, input_grad_ref, shard_columns_ref, shard_pack_ref,
    sent, crossed, stage, mixed, flipped, grad_keys, grad_values,
    pack_core, pack_pair, pack_sent, pack_blocks, pack_over, pack_sums, pack_parts, pack_sends, pack_receives,
    scaled, scaled_core, scaled_pair, scaled_sent,
    part_blocks, part_out, part_over, part_sums, part_parts, part_sends, part_receives,
    sends, receives, local,
):
    z, c = lax.axis_index("dp"), lax.axis_index("ctx")
    greet(EVERYONE)
    link = Link(sends, receives)

    def c_at(flip):
        return near(c, "ctx", flip) if flip else c

    to_core = [
        link.push(grad_pack_ref.at[:, c_at(flip)], pack_core.at[number], "ctx", 1)
        for number, flip in enumerate((3, 1))
    ]
    line = [link.push(ready2, done2, "dp", 2), link.push(ready1, done1, "dp", 1)]
    zones = grad_pack_ref.shape[0]
    held = []

    def pack_step():
        to_core[0].wait_recv()
        for zone in range(zones):
            pack_sent[zone] = (
                grad_pack_ref[zone, c_at(2)].astype(jnp.float32)
                + pack_core[0, zone].astype(jnp.float32)
            ).astype(jnp.bfloat16)
        held.append(link.push(pack_sent, pack_pair, "ctx", 2))

    fetch([(keep0.at[1], stage.at[0]), (arrived.at[0, 1], stage.at[1])], local)
    add_into(sent, [stage.at[0], stage.at[1]])
    pair = link.push(sent, crossed, "ctx", 2)
    attend_back(
        table_ref,
        query_ref,
        keys_ref,
        values_ref,
        seq_grad_ref,
        mixed,
        flipped,
        grad_keys,
        grad_values,
        pack_step,
    )
    blocks, block = scaled.shape[:2]
    for index in range(blocks):
        scaled[index] = lax.dot_general(
            mixed[index * block : (index + 1) * block, :],
            columns_ref[...],
            (((1,), (1,)), ((), ())),
            preferred_element_type=jnp.float32,
        ).astype(jnp.bfloat16)
    scaled_to_core = [
        link.push(scaled.at[c_at(flip)], scaled_core.at[number], "ctx", 1)
        for number, flip in enumerate((3, 1))
    ]
    wide = normed_ref.shape[1] // blocks
    some = zones // blocks
    for index in range(blocks):
        part = lax.dot_general(
            normed_ref[:, index * wide : (index + 1) * wide],
            mixed[...],
            (((0,), (0,)), ((), ())),
            preferred_element_type=jnp.float32,
        ).astype(jnp.bfloat16)
        part_blocks[index * some : (index + 1) * some] = part.reshape(
            (some,) + part_blocks.shape[1:]
        )
    part_fold = Fold(
        part_blocks, part_out, part_over, part_sums, part_parts, part_sends, part_receives
    )
    part_fold.start()
    scaled_to_core[0].wait_recv()
    scaled_sent[...] = (
        scaled[c_at(2)].astype(jnp.float32) + scaled_core[0].astype(jnp.float32)
    ).astype(jnp.bfloat16)
    scaled_over_pair = link.push(scaled_sent, scaled_pair, "ctx", 2)
    to_core[1].wait_recv()
    held[0].wait_recv()
    for zone in range(zones):
        pack_blocks[zone] = (
            grad_pack_ref[zone, c].astype(jnp.float32)
            + pack_core[1, zone].astype(jnp.float32)
            + pack_pair[zone].astype(jnp.float32)
        ).astype(jnp.bfloat16)
    pack_fold = Fold(
        pack_blocks, shard_pack_ref, pack_over, pack_sums, pack_parts, pack_sends, pack_receives
    )
    pack_fold.start()
    part_fold.early(0)
    part_fold.early(1)
    pack_fold.early(0)
    pack_fold.early(1)
    part_fold.late()
    part_fold.last()
    apart = [
        link.push(part_out.at[c_at(flip)], shard_columns_ref.at[c], "ctx", flip)
        for flip in (1, 2, 3)
    ]
    shard_columns_ref[c] = part_out[c]
    scaled_to_core[1].wait_recv()
    scaled_over_pair.wait_recv()
    grad_normed = (
        scaled[c].astype(jnp.float32)
        + scaled_core[1].astype(jnp.float32)
        + scaled_pair[...].astype(jnp.float32)
    )
    normed, factor = normalize(rows_ref[...].astype(jnp.float32))
    input_grad_ref[...] = grad_after_ref[...] + norm_back(grad_normed, normed, factor)
    pack_fold.late()
    pack_fold.last()
    fetch([(keep0.at[0], stage.at[0]), (arrived.at[0, 0], stage.at[1])], local)
    pair.wait_recv()
    pair.wait_send()
    add_into(sent, [stage.at[0], stage.at[1], crossed])
    fetch([(sent, done0)], local)
    for copy in apart + line:
        copy.wait_recv()
    part_fold.finish()
    pack_fold.finish()
    for copy in link.started:
        if copy is not pair:
            copy.wait_send()


def closing(
    ready2, ready1, keep0, arrived, table, query, keys, values, seq_grad, normed, columns,
    grad_pack, rows, grad_after, number,
):
    kind = jnp.bfloat16
    far = pl.BlockSpec(memory_space=pl.ANY)
    held = pl.BlockSpec(memory_space=pltpu.VMEM)
    piece = ready2.shape
    heads, length = query.shape[:2]
    groups = keys.shape[0]
    zones, ctx, share, wide = grad_pack.shape
    width = columns.shape[1]
    pack = (zones, share, wide)
    block = (length // ctx, D)
    part = (ctx, share, width)
    return pl.pallas_call(
        closing_kernel,
        out_shape=(
            jax.ShapeDtypeStruct(piece, kind),
            jax.ShapeDtypeStruct(piece, kind),
            jax.ShapeDtypeStruct(piece, kind),
            jax.ShapeDtypeStruct(rows.shape, jnp.float32),
            jax.ShapeDtypeStruct(part, kind),
            jax.ShapeDtypeStruct((share, wide), jnp.float32),
        ),
        in_specs=[far] * 4 + [held] * 10,
        out_specs=(far, far, far, held, held, held),
        scratch_shapes=[
            pltpu.VMEM(piece, kind),
            pltpu.VMEM(piece, kind),
            pltpu.VMEM((2,) + piece, kind),
            pltpu.VMEM((length, width), kind),
            pltpu.VMEM((groups * HD, length), kind),
            pltpu.VMEM((groups, length, HD), jnp.float32),
            pltpu.VMEM((groups, length, HD), jnp.float32),
            pltpu.VMEM((2,) + pack, kind),
            pltpu.VMEM(pack, kind),
            pltpu.VMEM(pack, kind),
            pltpu.VMEM(pack, kind),
        ]
        + fold_scratch(pack[1:])
        + [
            pltpu.VMEM((ctx,) + block, kind),
            pltpu.VMEM((2,) + block, kind),
            pltpu.VMEM(block, kind),
            pltpu.VMEM(block, kind),
            pltpu.VMEM((zones,) + part, kind),
            pltpu.VMEM(part, kind),
        ]
        + fold_scratch(part)
        + [
            pltpu.SemaphoreType.DMA((12,)),
            pltpu.SemaphoreType.DMA((12,)),
            pltpu.SemaphoreType.DMA((2,)),
        ],
        compiler_params=pltpu.CompilerParams(
            collective_id=number, has_side_effects=True, vmem_limit_bytes=62 * 1024 * 1024
        ),
    )(
        ready2, ready1, keep0, arrived, table, query, keys, values, seq_grad, normed, columns,
        grad_pack, rows, grad_after,
    )


def route_rows(rows, pack_ref, attended_ref, routes_ref, after_ref, gates_ref, gain_ref, packed):
    quarters = attended_ref.shape[0]
    wide = pack_ref.shape[-1]
    branch = jnp.zeros((rows.shape[0], D), jnp.float32)
    tails = []
    for index in range(quarters):
        pack = pack_ref[index].reshape(-1, wide)
        branch += jnp.dot(attended_ref[index], pack[:, :D], preferred_element_type=jnp.float32)
        tails.append(pack[:, D:])
    tail = jnp.concatenate(tails, 0)
    after = rows.astype(jnp.float32) + RESIDUAL_SCALE * branch
    after_ref[...] = after
    normed, _ = normalize(after)
    single = lax.broadcasted_iota(jnp.int32, (8, 128), 1) == EXPERTS
    gain = lax.dot_general(
        single.astype(jnp.bfloat16),
        tail,
        (((1,), (1,)), ((), ())),
        preferred_element_type=jnp.float32,
    )[:1]
    gain_ref[...] = gain
    expert_input = (normed * gain).astype(jnp.bfloat16)
    logits = jnp.dot(expert_input, tail, preferred_element_type=jnp.float32)
    lane = lax.broadcasted_iota(jnp.int32, logits.shape, 1)
    marks = jnp.zeros(logits.shape, jnp.float32)
    for index in range(TOP):
        marks = jnp.where(lane == routes_ref[:, index : index + 1], 1.0, marks)
    chosen = marks > 0.0
    peak = jnp.max(jnp.where(chosen, logits, -3e38), axis=-1, keepdims=True)
    raised = jnp.where(chosen, jnp.exp(jnp.where(chosen, logits - peak, 0.0)), 0.0)
    gates = raised / jnp.sum(raised, axis=-1, keepdims=True)
    gates_ref[...] = gates
    high = gates.astype(jnp.bfloat16).astype(jnp.float32)
    packed[:, :D] = expert_input
    packed[:, D:] = (
        high + pltpu.roll(gates - high, EXPERTS, 1) + pltpu.roll(marks, 2 * EXPERTS, 1)
    ).astype(jnp.bfloat16)


def opening_kernel(
    rows_ref, table_ref, columns_ref, pack_ref, weights_in, weights_out, grads_ref, routes_ref,
    all_rows, all_table, all_columns, all_pack, pieces_in, pieces_out, all_grads, all_packed,
    after_ref, gates_ref, gain_ref, packed,
    normed_ref, query_ref, keys_ref, values_ref, attended_ref,
    outgoing, flipped, sends, receives, line_sends, line_receives, token_sends, token_receives, locals_,
):
    z, y, c = lax.axis_index("dp"), lax.axis_index("expert"), lax.axis_index("ctx")
    greet(EVERYONE)
    link = Link(sends, receives)
    line = Line(grads_ref, all_grads, line_sends, line_receives)
    token_line = Line(packed, all_packed, token_sends, token_receives)
    own = 2 * z + y
    count = weights_in.shape[1]

    def z_at(flip):
        return near(z, "dp", flip) if flip else z

    def c_at(flip):
        return near(c, "ctx", flip) if flip else c

    def keep(number, source, target):
        copy = pltpu.make_async_copy(source, target, locals_.at[number])
        copy.start()
        return copy

    def both(target, source, axis, flip):
        return [link.push(source(ref), target(ref), axis, flip) for ref in (pieces_in, pieces_out)]

    def share(*place):
        step, rest = place[0], place[1:]
        source = lambda ref: ref.at[(step, 0) + rest]
        over = both(lambda ref: ref.at[(step, 2) + rest], source, "ctx", 2)
        core = both(lambda ref: ref.at[(step, 1) + rest], source, "ctx", 1)
        return over, core

    def hand_on(*place):
        step, rest = place[0], place[1:]
        return both(
            lambda ref: ref.at[(step, 3) + rest], lambda ref: ref.at[(step, 2) + rest], "ctx", 1
        )

    def move(step, *rest):
        return [
            link.push(weights.at[(z_at(step),) + rest], ref.at[(step, 0) + rest], "dp", step)
            for weights, ref in ((weights_in, pieces_in), (weights_out, pieces_out))
        ]

    def arrive(copies):
        for copy in copies:
            copy.wait_recv()

    kept = [
        keep(0, columns_ref.at[c], all_columns.at[own, c]),
        keep(1, weights_in.at[z], pieces_in.at[0, 0]),
        keep(2, weights_out.at[z], pieces_out.at[0, 0]),
        keep(3, rows_ref, all_rows.at[c]),
        keep(4, pack_ref, all_pack.at[z, y, c]),
        keep(5, grads_ref, all_grads.at[own]),
        keep(7, table_ref, all_table.at[c]),
    ]
    cut = [
        link.push(columns_ref.at[c_at(flip)], all_columns.at[own, c], "ctx", flip)
        for flip in (1, 2, 3)
    ]
    table_all = [link.push(table_ref, all_table.at[c], "ctx", flip) for flip in (1, 2, 3)]
    rows_over = link.push(rows_ref, all_rows.at[c], "ctx", 2)
    rows_core = link.push(rows_ref, all_rows.at[c], "ctx", 1)
    pack_line = [link.push(pack_ref, all_pack.at[z, y, c], "dp", flip) for flip in (1, 2, 3)]
    kept[0].wait()
    arrive(cut)
    column_line = [
        link.push(all_columns.at[own], all_columns.at[own], "dp", flip) for flip in (1, 2, 3)
    ]
    column_over = [link.push(all_columns.at[own], all_columns.at[own], "expert", 1)]
    kept[1].wait()
    kept[2].wait()
    rows_over.wait_recv()
    rows_pass = link.push(all_rows.at[c_at(2)], all_rows.at[c_at(2)], "ctx", 1)
    shared = [share(0)]
    arrive(pack_line)
    kept[4].wait()
    pack_over = link.push(all_pack.at[:, y, c], all_pack.at[:, y, c], "expert", 1)
    for flip in (1, 2, 3):
        column_line[flip - 1].wait_recv()
        block = all_columns.at[2 * z_at(flip) + y]
        column_over.append(link.push(block, block, "expert", 1))
    moved = {2: move(2), 1: move(1)}
    line.start()
    arrive([pack_over])
    pack_pair = link.push(all_pack.at[:, :, c], all_pack.at[:, :, c], "ctx", 2)
    pack_core = link.push(all_pack.at[:, :, c], all_pack.at[:, :, c], "ctx", 1)
    arrive([rows_core, rows_pass] + column_over + table_all)
    kept[3].wait()
    kept[6].wait()
    project_rows(
        all_rows,
        all_table,
        all_columns[...].reshape(D, all_columns.shape[-1]),
        normed_ref,
        query_ref,
        keys_ref,
        values_ref,
        flipped,
    )
    for index in range(all_rows.shape[0]):
        attend_rows(index, all_rows.shape[1], query_ref, keys_ref, outgoing, flipped)
    attended = [
        link.push(outgoing.at[c_at(flip)], attended_ref.at[c], "ctx", flip) for flip in (1, 2, 3)
    ]
    attended_ref[c] = outgoing[c]
    arrive([pack_pair])
    pack_last = link.push(all_pack.at[:, :, c_at(2)], all_pack.at[:, :, c_at(2)], "ctx", 1)
    arrive([pack_core, pack_last] + attended)
    route_rows(
        all_rows[c], all_pack, attended_ref, routes_ref, after_ref, gates_ref, gain_ref, packed
    )
    token_line.start()
    kept.append(keep(6, packed, all_packed.at[own]))
    line.first()
    arrive(shared[0][0])
    passed = hand_on(0)
    arrive(moved[1])
    shared.append(share(1))
    line.second()
    token_line.first()
    line.third()
    token_line.second()
    arrive(moved[2])
    shared.append(share(2))
    last = [move(3, 0), move(3, 1)]
    token_line.third()
    arrive(shared[1][0])
    passed += hand_on(1)

    def next_piece(item):
        arrive(last[item])
        if item + 2 < count:
            last.append(move(3, item + 2))
        shared.append(share(3, item))

    for item in range(count):
        next_piece(item)
    arrive(shared[2][0])
    passed += hand_on(2)
    for item in range(count):
        arrive(shared[3 + item][0])
        passed += hand_on(3, item)
    kept[5].wait()
    kept[7].wait()
    arrive(passed)
    for over, core in shared:
        arrive(core)
    line.finish()
    token_line.finish()
    link.finish()


def opening(rows, table, columns, pack, weights_in, weights_out, grads, routes, heads, groups, number):
    ctx = columns.shape[0]
    shards, count = weights_in.shape[:2]
    tokens = rows.shape[0]
    kind = jnp.bfloat16
    copies = 27 + 2 * (2 + 3 * 3 + 5 * count)
    far = pl.BlockSpec(memory_space=pl.ANY)
    held = pl.BlockSpec(memory_space=pltpu.VMEM)
    all_rows = (ctx,) + rows.shape
    return pl.pallas_call(
        opening_kernel,
        out_shape=(
            jax.ShapeDtypeStruct(all_rows, kind),
            jax.ShapeDtypeStruct((ctx,) + table.shape, kind),
            jax.ShapeDtypeStruct((8,) + columns.shape, kind),
            jax.ShapeDtypeStruct((shards, 2, ctx) + pack.shape, kind),
            jax.ShapeDtypeStruct((shards, ctx) + weights_in.shape[1:], kind),
            jax.ShapeDtypeStruct((shards, ctx) + weights_out.shape[1:], kind),
            jax.ShapeDtypeStruct((8,) + grads.shape, kind),
            jax.ShapeDtypeStruct((8, tokens, D + 128), kind),
            jax.ShapeDtypeStruct((tokens, D), jnp.float32),
            jax.ShapeDtypeStruct((tokens, 128), jnp.float32),
            jax.ShapeDtypeStruct((1, D), jnp.float32),
            jax.ShapeDtypeStruct((tokens, D + 128), kind),
        )
        + attend_shapes(all_rows, heads, groups),
        in_specs=[far] * 7 + [held],
        out_specs=(held, held, held, held, far, far, far, far) + (held,) * 9,
        scratch_shapes=[
            pltpu.VMEM((ctx, rows.shape[0], heads * HD), kind),
            pltpu.VMEM((groups * HD, ctx * rows.shape[0]), kind),
            pltpu.SemaphoreType.DMA((copies,)),
            pltpu.SemaphoreType.DMA((copies,)),
            pltpu.SemaphoreType.DMA((9,)),
            pltpu.SemaphoreType.DMA((8,)),
            pltpu.SemaphoreType.DMA((9,)),
            pltpu.SemaphoreType.DMA((8,)),
            pltpu.SemaphoreType.DMA((8,)),
        ],
        compiler_params=pltpu.CompilerParams(
            collective_id=number, has_side_effects=True, vmem_limit_bytes=56 * 1024 * 1024
        ),
    )(rows, table, columns, pack, weights_in, weights_out, grads, routes)


def split_high_low(values):
    high = values.astype(jnp.bfloat16)
    return high, (values - high.astype(jnp.float32)).astype(jnp.bfloat16)


def pad_columns(like, columns):
    return jnp.zeros((like.shape[0], columns), like.dtype)


def gather_ctx(rows):
    ctx = lax.axis_size("ctx")
    column = lax.axis_index("ctx")
    pieces = {0: rows}
    flip = ctx // 2
    while flip:
        pieces.update({turn ^ flip: swap(item, "ctx", flip) for turn, item in pieces.items()})
        flip //= 2
    out = jnp.zeros((ctx,) + rows.shape, rows.dtype)
    for turn in range(ctx):
        out = lax.dynamic_update_index_in_dim(out, pieces[turn], column ^ turn, 0)
    return out


def exchange_ctx(blocks):
    column = lax.axis_index("ctx")
    out = jnp.zeros(blocks.shape, blocks.dtype)
    for turn in range(blocks.shape[0]):
        item = lax.dynamic_index_in_dim(blocks, column ^ turn, 0, keepdims=False)
        if turn:
            item = swap(item, "ctx", turn)
        out = lax.dynamic_update_index_in_dim(out, item, column ^ turn, 0)
    return out


def scatter_ctx(blocks):
    column = lax.axis_index("ctx")
    flip = 1
    held = blocks
    while flip < lax.axis_size("ctx"):
        pairs = held.reshape((held.shape[0] // 2, 2) + held.shape[1:])
        bit = (column // flip) % 2
        keep = lax.dynamic_index_in_dim(pairs, bit, 1, keepdims=False)
        give = lax.dynamic_index_in_dim(pairs, 1 - bit, 1, keepdims=False)
        held = keep.astype(jnp.float32) + swap(give, "ctx", flip).astype(jnp.float32)
        flip *= 2
        if flip < lax.axis_size("ctx"):
            held = held.astype(jnp.bfloat16)
    return held[0]


def group_columns(rows, ctx):
    depth = rows.shape[0]
    cuts = (rows[:, : H * HD], rows[:, H * HD : (H + KV) * HD], rows[:, (H + KV) * HD :])
    return jnp.concatenate([cut.reshape(depth, ctx, -1) for cut in cuts], -1).transpose(1, 0, 2)


def ungroup_columns(groups):
    ctx, depth, _ = groups.shape
    query, key = H * HD // ctx, KV * HD // ctx
    cuts = (groups[..., :query], groups[..., query : query + key], groups[..., query + key :])
    return jnp.concatenate([cut.transpose(1, 0, 2).reshape(depth, -1) for cut in cuts], 1)


def block_order():
    shards, ctx = lax.axis_size("dp"), lax.axis_size("ctx")
    place, column = lax.axis_index("dp"), lax.axis_index("ctx")
    return place, column, shards, ctx


def fold_weights(expert_in, expert_out):
    deep = expert_out.shape[1]
    folds = expert_in.shape[1] // deep
    cuts = [expert_in[:, fold * deep : (fold + 1) * deep] for fold in range(folds)]
    return jnp.concatenate(cuts + [expert_out], -1)


def piece_order():
    place, column, shards, ctx = block_order()
    blocks = [
        (place ^ step) * ctx + (column ^ turn) for step in range(shards) for turn in range(ctx)
    ]
    return jnp.stack(blocks).astype(jnp.int32)


def spread_weights(expert_in, expert_out):
    shards = lax.axis_size("dp")
    count, depth = expert_in.shape[:2]
    part = FFE // shards
    cut = expert_in.reshape(count, depth, 2, shards, part).transpose(3, 0, 1, 2, 4)
    moved_in = lax.all_to_all(cut, "dp", split_axis=0, concat_axis=0, tiled=True)
    all_in = lax.all_gather(moved_in.transpose(1, 0, 2, 3, 4), "ctx", axis=2, tiled=True)
    all_out = lax.all_gather(expert_out, "ctx", axis=1, tiled=True)
    return [all_in.reshape(count, -1, 2 * part), all_out]


def collect_weights(grad_in, grad_out):
    shards = lax.axis_size("dp")
    count = grad_in.shape[0]
    part = FFE // shards
    part_in = lax.psum_scatter(
        grad_in.reshape(count, shards, -1, 2, part), "ctx", scatter_dimension=2, tiled=True
    )
    own_in = lax.all_to_all(
        part_in.transpose(1, 0, 2, 3, 4), "dp", split_axis=0, concat_axis=0, tiled=True
    )
    own_in = own_in.transpose(1, 2, 3, 0, 4).reshape(count, -1, 2 * FFE)
    own_out = lax.psum_scatter(grad_out, "ctx", scatter_dimension=1, tiled=True)
    return [(0, fold_weights(own_in, own_out))]


def expert_step_kernel(places_ref, *refs):
    states, outs = refs[-14:-8], refs[-8:]
    grads = refs[:-14]
    number = pl.program_id(0)
    wide = states[0].shape[2]
    deep = states[3].shape[1]
    folds = states[0].shape[1] // deep
    rates = learn_rates()

    def update(grad_ref):
        for fold in range(folds):
            span = pl.ds(fold * deep, deep)
            grad = grad_ref[0, :, fold * wide : (fold + 1) * wide].astype(jnp.float32)
            news = adam_step(
                states[0][0, span, :],
                states[1][0, span, :],
                states[2][0, span, :],
                grad,
                DECAY_RATE,
                rates[5],
            )
            for out, new in zip(outs[:4], news):
                out[0, span, :] = new
        grad = grad_ref[0, :, folds * wide :].astype(jnp.float32)
        news = adam_step(states[3][0], states[4][0], states[5][0], grad, DECAY_RATE, rates[6])
        for out, new in zip(outs[4:], news):
            out[0] = new

    count = pl.num_programs(0) // len(grads)
    for index, grad_ref in enumerate(grads):
        pl.when(number // count == index)(functools.partial(update, grad_ref))


def expert_step(places, grads, states):
    count = grads[0].shape[0]
    shapes = [states[1].shape] * 4 + [states[4].shape] * 4
    moved = lambda e, p: (p[e // count] * count + e % count, 0, 0)
    block = lambda shape: pl.BlockSpec((1,) + shape[1:], moved)

    def grad_spec(index):
        return pl.BlockSpec(
            (1,) + grads[0].shape[1:], lambda e, p: (jnp.clip(e - index * count, 0, count - 1), 0, 0)
        )

    return pl.pallas_call(
        expert_step_kernel,
        grid_spec=pltpu.PrefetchScalarGridSpec(
            num_scalar_prefetch=1,
            grid=(count * len(grads),),
            in_specs=[grad_spec(index) for index in range(len(grads))]
            + [block(state.shape) for state in states],
            out_specs=tuple(block(shape) for shape in shapes),
        ),
        out_shape=tuple(jax.ShapeDtypeStruct(shape, jnp.float32) for shape in shapes),
        compiler_params=pltpu.CompilerParams(vmem_limit_bytes=62 * 1024 * 1024),
        cost_estimate=pl.CostEstimate(flops=1, bytes_accessed=1, transcendentals=0),
    )(places, *grads, *states)


def local(
    tokens,
    cotangent,
    routes,
    positions,
    gain_attend,
    gain_attend_mean,
    gain_attend_square,
    project_in,
    project_in_mean,
    project_in_square,
    project_out,
    project_out_mean,
    project_out_square,
    gain_expert,
    gain_expert_mean,
    gain_expert_square,
    router_weight,
    router_weight_mean,
    router_weight_square,
    expert_in,
    expert_in_mean,
    expert_in_square,
    expert_out,
    expert_out_mean,
    expert_out_square,
):
    everywhere = ("dp", "expert", "ctx")
    owners = ("dp", "expert")
    shards = lax.axis_size("dp")
    planes = lax.axis_size("expert")
    ctx = lax.axis_size("ctx")
    rows_local = tokens.shape[0]
    local_count = expert_in.shape[0]
    close = (shards, planes, ctx) == (4, 2, 4) and local_count % shards == 0
    heads, groups = H // ctx, KV // ctx
    hidden_in = tokens.astype(jnp.float32)

    half = HD // 2
    freqs = ROPE_BASE ** (-jnp.arange(half, dtype=jnp.float32) * 2.0 / HD)
    angles = positions.astype(jnp.float32)[:, None] * freqs[None, :]
    table = jnp.concatenate(split_high_low(jnp.cos(angles)) + split_high_low(jnp.sin(angles)), 1)
    gain_attend_wide = gain_attend.astype(jnp.float32)[:, None]
    scaled_in = (gain_attend_wide * project_in.astype(jnp.float32)).astype(jnp.bfloat16)
    columns = group_columns(scaled_in, ctx)
    pack_out = jnp.concatenate(
        [project_out, router_weight, gain_expert[:, None], pad_columns(project_out, 87)], 1
    )
    order = piece_order()
    if close:
        parted = lambda array: array.reshape((shards, -1) + array.shape[1:])
        (
            _, seq_table, own_in, full_pack_out, all_in, all_out, all_grads, all_packed,
            after, gates_wide, gain_two, packed,
            seq_normed, query, keys, values, attended_heads,
        ) = opening(
            tokens, table, columns, pack_out, parted(expert_in), parted(expert_out), cotangent, routes,
            heads, groups, 1,
        )
        pieces = [array.reshape((-1,) + array.shape[2:]) for array in (all_in, all_out)]
    else:
        seq_rows, seq_table = gather_ctx(tokens), gather_ctx(table)
        own_in = lax.all_gather(exchange_ctx(columns), owners, axis=0, tiled=False)
        full_pack_out = lax.all_gather(pack_out, everywhere, axis=0, tiled=True)
        all_grads = lax.all_gather(cotangent, owners, axis=0, tiled=False)
        pieces = spread_weights(expert_in, expert_out)
        seq_normed, query, keys, values, seq_attended = attend_forward(
            seq_rows, seq_table, own_in.reshape(D, -1), heads, groups
        )
        attended_heads = exchange_ctx(seq_attended)
    seq_table = seq_table.reshape(-1, 128)
    own_in = own_in.reshape(D, -1)
    full_pack_out = full_pack_out.reshape(H * HD, -1)
    if not close:
        full_out = full_pack_out[:, :D]
        full_router = full_pack_out[:, D : D + EXPERTS]
        gain_two = full_pack_out[:, D + EXPERTS].astype(jnp.float32)[None]
        attended = attended_heads.transpose(1, 0, 2).reshape(rows_local, H * HD)
        branch = jnp.dot(attended, full_out, preferred_element_type=jnp.float32)
        after = hidden_in + RESIDUAL_SCALE * branch
        normed_two, factor_two = normalize(after)
        expert_input = (normed_two * gain_two).astype(jnp.bfloat16)
        logits = jnp.dot(expert_input, full_router, preferred_element_type=jnp.float32)
        chosen = jnp.any(routes[:, :, None] == jnp.arange(EXPERTS, dtype=jnp.int32), axis=1)
        peak = jnp.max(jnp.where(chosen, logits, -3e38), axis=-1, keepdims=True)
        raised = jnp.where(chosen, jnp.exp(jnp.where(chosen, logits - peak, 0.0)), 0.0)
        gates = raised / jnp.sum(raised, axis=-1, keepdims=True)
        packed = jnp.concatenate(
            (expert_input,)
            + split_high_low(gates)
            + (chosen.astype(jnp.bfloat16), pad_columns(expert_input, 128 - 3 * EXPERTS)),
            1,
        )
        all_packed = lax.all_gather(packed, owners, axis=0, tiled=False)

    first = lax.axis_index("expert") * local_count
    count = local_count
    hidden = FFE // shards
    if close:
        count = local_count // shards
        hidden = FFE
        first = first + lax.axis_index("dp") * count
    first = first.astype(jnp.int32).reshape(1)
    slot_rows, slot_grads, pick = dispatch(first, all_packed, all_grads, count)
    produced, grad_rows, parts = run_experts(
        first, order, slot_rows, slot_grads, pieces, hidden, close
    )
    shared_grads, shared = combine(pick, (grad_rows, produced))
    if close:
        place = lax.axis_index("dp")
        (
            grad_after, seq_grad, grad_pack_out, block_output, arrived, done3, ready2, ready1,
        ) = returning(
            shared_grads,
            shared,
            parts,
            after,
            packed,
            gates_wide,
            cotangent,
            gain_two,
            full_pack_out,
            attended_heads,
            3,
        )
        done2, done1, done0, input_grad, shard_columns, shard_pack_out = closing(
            ready2,
            ready1,
            parts[7],
            arrived,
            seq_table,
            query,
            keys,
            values,
            seq_grad,
            seq_normed,
            own_in,
            grad_pack_out,
            tokens,
            grad_after,
            4,
        )
        expert_grads = [
            (near(place, "dp", 3), done3),
            (near(place, "dp", 2), done2),
            (near(place, "dp", 1), done1),
            (place, done0),
        ]
    else:
        grad_routed = lax.psum_scatter(
            shared_grads, owners, scatter_dimension=0, tiled=False
        ).astype(jnp.float32)
        moe = lax.psum_scatter(shared, owners, scatter_dimension=0, tiled=False)
        block_output = (after + RESIDUAL_SCALE * moe.astype(jnp.float32)).astype(jnp.bfloat16)
        expert_grads = collect_weights(*parts)
        grad_final = cotangent.astype(jnp.float32)
        grad_gates = grad_routed[:, D : D + EXPERTS] + grad_routed[:, D + EXPERTS : D + 2 * EXPERTS]
        grad_picked = gates * (grad_gates - jnp.sum(gates * grad_gates, axis=-1, keepdims=True))
        grad_logits = grad_picked.astype(jnp.bfloat16)
        grad_from_router = jnp.einsum(
            "te,de->td", grad_logits, full_router, preferred_element_type=jnp.float32
        )
        grad_input = grad_from_router + grad_routed[:, :D]
        grad_after = grad_final + norm_back(grad_input * gain_two, normed_two, factor_two)
        grad_branch = (RESIDUAL_SCALE * grad_after).astype(jnp.bfloat16)
        grad_attended = jnp.einsum(
            "td,cd->tc", grad_branch, full_out, preferred_element_type=jnp.float32
        ).astype(jnp.bfloat16)
        seq_grad = exchange_ctx(
            grad_attended.reshape(rows_local, ctx, heads * HD).transpose(1, 0, 2)
        )
        grad_mixed = attend_backward(seq_table, query, keys, values, seq_grad)
        grad_in_part = jnp.einsum(
            "td,tc->dc", seq_normed, grad_mixed, preferred_element_type=jnp.float32
        ).astype(jnp.bfloat16)
        grad_in_part = grad_in_part.reshape(shards * planes, -1, grad_in_part.shape[1])
        shard_columns = lax.psum_scatter(grad_in_part, owners, scatter_dimension=0, tiled=False)
        shard_columns = exchange_ctx(shard_columns.reshape(ctx, -1, shard_columns.shape[-1]))
        grad_scaled = jnp.einsum(
            "tc,dc->td", grad_mixed, own_in, preferred_element_type=jnp.float32
        ).astype(jnp.bfloat16)
        grad_normed = scatter_ctx(grad_scaled.reshape(ctx, rows_local, D))
        normed_one, factor_one = normalize(hidden_in)
        input_grad = grad_after + norm_back(grad_normed, normed_one, factor_one)
        grad_project_out = jnp.einsum(
            "tc,td->cd", attended, grad_branch, preferred_element_type=jnp.float32
        ).astype(jnp.bfloat16)
        ones = jnp.where(jnp.arange(128) == EXPERTS, 1.0, 0.0).astype(jnp.bfloat16)
        grad_small = jnp.einsum(
            "td,te->de",
            jnp.concatenate([expert_input, (grad_input * normed_two).astype(jnp.bfloat16)], 0),
            jnp.concatenate(
                [
                    jnp.pad(grad_logits, ((0, 0), (0, 128 - EXPERTS))),
                    jnp.broadcast_to(ones, (rows_local, 128)),
                ],
                0,
            ),
            preferred_element_type=jnp.float32,
        ).astype(jnp.bfloat16)
        grad_pack_out = jnp.concatenate([grad_project_out, grad_small], 1)
        shard_pack_out = lax.psum_scatter(
            grad_pack_out, everywhere, scatter_dimension=0, tiled=True
        ).astype(jnp.float32)
    shard_scaled = ungroup_columns(shard_columns).astype(jnp.float32)
    shard_in = gain_attend_wide * shard_scaled
    shard_attend = jnp.sum(shard_scaled * project_in.astype(jnp.float32), axis=1)
    shard_out = shard_pack_out[:, :D]
    shard_router = shard_pack_out[:, D : D + EXPERTS]
    shard_expert = shard_pack_out[:, D + EXPERTS]
    rates = learn_rates()
    results = [block_output, input_grad]
    results.extend(
        adam_step(gain_attend, gain_attend_mean, gain_attend_square, shard_attend, 0.0, rates[0])
    )
    results.extend(
        adam_step(project_in, project_in_mean, project_in_square, shard_in, DECAY_RATE, rates[1])
    )
    results.extend(
        adam_step(
            project_out, project_out_mean, project_out_square, shard_out, DECAY_RATE, rates[2]
        )
    )
    results.extend(
        adam_step(gain_expert, gain_expert_mean, gain_expert_square, shard_expert, 0.0, rates[3])
    )
    results.extend(
        adam_step(
            router_weight,
            router_weight_mean,
            router_weight_square,
            shard_router,
            DECAY_RATE,
            rates[4],
        )
    )
    states = (expert_in, expert_in_mean, expert_in_square, expert_out, expert_out_mean, expert_out_square)
    places = jnp.stack([jnp.asarray(place, jnp.int32) for place, _ in expert_grads])
    expert_outs = expert_step(places, [folded for _, folded in expert_grads], states)
    results.extend(expert_outs)
    return tuple(results)


def solution(mesh):
    placed = (
        P(("dp", "expert", "ctx"), None),
        P(("dp", "expert", "ctx"), None),
        P(("dp", "expert", "ctx"), None),
        P(("dp", "expert", "ctx")),
        P(("dp", "expert", "ctx")),
        P(("dp", "expert", "ctx")),
        P(("dp", "expert", "ctx")),
        P(("dp", "expert", "ctx"), None),
        P(("dp", "expert", "ctx"), None),
        P(("dp", "expert", "ctx"), None),
        P(("dp", "expert", "ctx"), None),
        P(("dp", "expert", "ctx"), None),
        P(("dp", "expert", "ctx"), None),
        P(("dp", "expert", "ctx")),
        P(("dp", "expert", "ctx")),
        P(("dp", "expert", "ctx")),
        P(("dp", "expert", "ctx"), None),
        P(("dp", "expert", "ctx"), None),
        P(("dp", "expert", "ctx"), None),
        P("expert", ("dp", "ctx"), None),
        P("expert", ("dp", "ctx"), None),
        P("expert", ("dp", "ctx"), None),
        P("expert", ("dp", "ctx"), None),
        P("expert", ("dp", "ctx"), None),
        P("expert", ("dp", "ctx"), None),
    )
    return jax.shard_map(
        local,
        mesh=mesh,
        in_specs=placed,
        out_specs=(
            P(("dp", "expert", "ctx"), None),
            P(("dp", "expert", "ctx"), None),
            P(("dp", "expert", "ctx")),
            P(("dp", "expert", "ctx")),
            P(("dp", "expert", "ctx")),
            P(("dp", "expert", "ctx")),
            P(("dp", "expert", "ctx"), None),
            P(("dp", "expert", "ctx"), None),
            P(("dp", "expert", "ctx"), None),
            P(("dp", "expert", "ctx"), None),
            P(("dp", "expert", "ctx"), None),
            P(("dp", "expert", "ctx"), None),
            P(("dp", "expert", "ctx"), None),
            P(("dp", "expert", "ctx"), None),
            P(("dp", "expert", "ctx")),
            P(("dp", "expert", "ctx")),
            P(("dp", "expert", "ctx")),
            P(("dp", "expert", "ctx")),
            P(("dp", "expert", "ctx"), None),
            P(("dp", "expert", "ctx"), None),
            P(("dp", "expert", "ctx"), None),
            P(("dp", "expert", "ctx"), None),
            P("expert", ("dp", "ctx"), None),
            P("expert", ("dp", "ctx"), None),
            P("expert", ("dp", "ctx"), None),
            P("expert", ("dp", "ctx"), None),
            P("expert", ("dp", "ctx"), None),
            P("expert", ("dp", "ctx"), None),
            P("expert", ("dp", "ctx"), None),
            P("expert", ("dp", "ctx"), None),
        ),
        check_vma=False,
    )
```

```python
import functools

import jax
import jax.numpy as jnp
from jax import lax
from jax.experimental import pallas as pl
from jax.experimental.pallas import tpu as pltpu
from jax.sharding import PartitionSpec as P

D = 1536
H = 24
KV = 8
HD = 64
FFE = 512
EXPERTS = 40
TOP = 8
STEP = 8
CAP = 64


EPS_NORM = 1e-06
ATTN_SCALE = 0.015625
RESIDUAL_SCALE = 0.22
BETA_ONE = 0.9
BETA_TWO = 0.95
ADAM_EPS = 1e-08
DECAY_RATE = 0.1
ROPE_BASE = 10000.0


def normalize(rows):
    factor = lax.rsqrt(jnp.mean(rows * rows, axis=-1, keepdims=True) + EPS_NORM)
    return (rows * factor, factor)


def norm_back(grad_normed, normed, factor):
    return factor * (grad_normed - normed * jnp.mean(grad_normed * normed, axis=-1, keepdims=True))


def learn_rates():
    return (
        0.3,
        3.0 / (D // 16) ** 0.5,
        3.0 / (D // 12) ** 0.5,
        0.3,
        3.0 / (4 * D) ** 0.5,
        3.0 / D**0.5,
        3.0 / (FFE // 32) ** 0.5,
    )


def adam_step(weight, first, second, grad, decay, rate):
    new_first = BETA_ONE * first + (1.0 - BETA_ONE) * grad
    new_second = BETA_TWO * second + (1.0 - BETA_TWO) * grad * grad
    corrected = (new_first * (1.0 / (1.0 - BETA_ONE**STEP))) / (
        jnp.sqrt(new_second * (1.0 / (1.0 - BETA_TWO**STEP))) + ADAM_EPS
    )
    old = weight.astype(jnp.float32)
    return (grad, new_first, new_second, old - rate * (corrected + decay * old))


def lane_tables(table):
    half = HD // 2
    source = lax.broadcasted_iota(jnp.int32, (128, 128), 0)
    target = lax.broadcasted_iota(jnp.int32, (128, 128), 1)
    same = (source % half) == (target % half)
    group = source // half
    first = (target % HD) < half
    cosine = jnp.where(same & (group < 2), 1.0, 0.0).astype(jnp.bfloat16)
    ahead = jnp.where(same & (group >= 2) & first, -1.0, 0.0).astype(jnp.bfloat16)
    behind = jnp.where(same & (group >= 2) & jnp.logical_not(first), 1.0, 0.0).astype(jnp.bfloat16)
    return tuple(
        jnp.dot(table, item, preferred_element_type=jnp.float32)
        for item in (cosine, ahead, behind)
    )


def turn_lanes(block, tables, sign):
    cosine, ahead, behind = tables
    half = HD // 2
    turned = pltpu.roll(block, 128 - half, 1) * ahead + pltpu.roll(block, half, 1) * behind
    return block * cosine + sign * turned


def scores_of(keys, query, start, length):
    scores = (
        lax.dot_general(
            keys, query, (((1,), (1,)), ((), ())), preferred_element_type=jnp.float32
        )
        * ATTN_SCALE
    )
    rows = lax.broadcasted_iota(jnp.int32, scores.shape, 0)
    columns = lax.broadcasted_iota(jnp.int32, scores.shape, 1) + start
    return jnp.where(rows <= columns, scores, -1e30)


def project_rows(rows_ref, table_ref, weight, normed_ref, query_ref, keys_ref, values_ref, flipped):
    blocks, block = rows_ref.shape[:2]
    heads, groups = query_ref.shape[0], keys_ref.shape[0]
    wide = heads * HD
    for index in range(blocks):
        span = pl.ds(index * block, block)
        rows = rows_ref[index].astype(jnp.float32)
        factor = lax.rsqrt(jnp.mean(rows * rows, axis=-1, keepdims=True) + EPS_NORM)
        normed = (rows * factor).astype(jnp.bfloat16)
        normed_ref[span, :] = normed
        tables = lane_tables(table_ref[index])
        mixed = jnp.dot(normed, weight, preferred_element_type=jnp.float32)
        for column in range(0, wide + 2 * groups * HD, 128):
            part = mixed[:, column : column + 128]
            if column < wide + groups * HD:
                part = turn_lanes(part, tables, 1.0)
            else:
                flipped[column - wide - groups * HD : column - wide - groups * HD + 128, span] = (
                    part.T.astype(jnp.bfloat16)
                )
            part = part.astype(jnp.bfloat16)
            for half in range(2):
                head = column // HD + half
                piece = part[:, half * HD : (half + 1) * HD]
                if head < heads:
                    query_ref[head, span, :] = piece
                elif head < heads + groups:
                    keys_ref[head - heads, span, :] = piece
                else:
                    values_ref[head - heads - groups, span, :] = piece


def attend_rows(index, block, query_ref, keys_ref, out_ref, flipped):
    heads, groups = query_ref.shape[0], keys_ref.shape[0]
    length = (index + 1) * block
    span = pl.ds(index * block, block)
    outputs = []
    for head in range(heads):
        group = head // (heads // groups)
        scores = scores_of(
            keys_ref[group, :length, :], query_ref[head, span, :], index * block, length
        )
        peak = jnp.max(scores, axis=0, keepdims=True)
        raised = jnp.exp(scores - peak)
        total = jnp.sum(raised, axis=0, keepdims=True)
        probs = (raised * (1.0 / total)).astype(jnp.bfloat16)
        outputs.append(
            jnp.dot(
                flipped[group * HD : (group + 1) * HD, :length],
                probs,
                preferred_element_type=jnp.float32,
            )
        )
    out_ref[index] = jnp.concatenate(outputs, 0).T.astype(jnp.bfloat16)


def attend_kernel(rows_ref, table_ref, weight_ref, normed_ref, query_ref, keys_ref, values_ref, out_ref, flipped):
    project_rows(rows_ref, table_ref, weight_ref[...], normed_ref, query_ref, keys_ref, values_ref, flipped)
    for index in range(rows_ref.shape[0]):
        attend_rows(index, rows_ref.shape[1], query_ref, keys_ref, out_ref, flipped)


def attend_shapes(rows, heads, groups):
    blocks, block = rows[:2]
    length = blocks * block
    return (
        jax.ShapeDtypeStruct((length, D), jnp.bfloat16),
        jax.ShapeDtypeStruct((heads, length, HD), jnp.bfloat16),
        jax.ShapeDtypeStruct((groups, length, HD), jnp.bfloat16),
        jax.ShapeDtypeStruct((groups, length, HD), jnp.bfloat16),
        jax.ShapeDtypeStruct((blocks, block, heads * HD), jnp.bfloat16),
    )


def attend_back(rows_ref, query_ref, keys_ref, values_ref, grad_ref, out_ref, flipped, grad_keys, grad_values, between=None):
    block = 256
    blocks = rows_ref.shape[0] // block
    heads, groups = query_ref.shape[0], keys_ref.shape[0]
    repeat = heads // groups
    wide = heads * HD
    for group in range(groups):
        flipped[group * HD : (group + 1) * HD, :] = (
            keys_ref[group].astype(jnp.float32).T.astype(jnp.bfloat16)
        )
    grad_keys[...] = jnp.zeros_like(grad_keys)
    grad_values[...] = jnp.zeros_like(grad_values)
    for index in range(blocks):
        length = (index + 1) * block
        span = pl.ds(index * block, block)
        outputs = []
        for head in range(heads):
            group = head // repeat
            query = query_ref[head, span, :]
            grad = grad_ref[index, :, head * HD : (head + 1) * HD]
            scores = scores_of(keys_ref[group, :length, :], query, index * block, length)
            peak = jnp.max(scores, axis=0, keepdims=True)
            raised = jnp.exp(scores - peak)
            total = jnp.sum(raised, axis=0, keepdims=True)
            probs = raised * (1.0 / total)
            grad_probs = lax.dot_general(
                values_ref[group, :length, :],
                grad,
                (((1,), (1,)), ((), ())),
                preferred_element_type=jnp.float32,
            )
            middle = jnp.sum(probs * grad_probs, axis=0, keepdims=True)
            grad_scores = (probs * (grad_probs - middle)).astype(jnp.bfloat16)
            grad_keys[group, :length, :] += jnp.dot(
                grad_scores, query, preferred_element_type=jnp.float32
            )
            grad_values[group, :length, :] += jnp.dot(
                probs.astype(jnp.bfloat16), grad, preferred_element_type=jnp.float32
            )
            outputs.append(
                jnp.dot(
                    flipped[group * HD : (group + 1) * HD, :length],
                    grad_scores,
                    preferred_element_type=jnp.float32,
                )
            )
        tables = lane_tables(rows_ref[span, :])
        stacked = jnp.concatenate(outputs, 0).T * ATTN_SCALE
        for column in range(0, wide, 128):
            out_ref[span, column : column + 128] = turn_lanes(
                stacked[:, column : column + 128], tables, -1.0
            ).astype(jnp.bfloat16)
        if between is not None and index == 1:
            between()
    for index in range(blocks):
        span = pl.ds(index * block, block)
        tables = lane_tables(rows_ref[span, :])
        keys = jnp.concatenate([grad_keys[group, span, :] for group in range(groups)], 1)
        values = jnp.concatenate([grad_values[group, span, :] for group in range(groups)], 1)
        keys = turn_lanes(keys * ATTN_SCALE, tables, -1.0)
        out_ref[span, wide : wide + groups * HD] = keys.astype(jnp.bfloat16)
        out_ref[span, wide + groups * HD :] = values.astype(jnp.bfloat16)


def attend_forward(rows, table, weight, heads, groups):
    return pl.pallas_call(
        attend_kernel,
        out_shape=attend_shapes(rows.shape, heads, groups),
        scratch_shapes=[pltpu.VMEM((groups * HD, rows.shape[0] * rows.shape[1]), jnp.bfloat16)],
        compiler_params=pltpu.CompilerParams(vmem_limit_bytes=48 * 1024 * 1024),
        cost_estimate=pl.CostEstimate(flops=1, bytes_accessed=1, transcendentals=0),
    )(rows, table, weight)


def attend_backward(table, query, keys, values, grad):
    heads, length = query.shape[:2]
    groups = keys.shape[0]
    return pl.pallas_call(
        attend_back,
        out_shape=jax.ShapeDtypeStruct((length, (heads + 2 * groups) * HD), jnp.bfloat16),
        scratch_shapes=[
            pltpu.VMEM((groups * HD, length), jnp.bfloat16),
            pltpu.VMEM((groups, length, HD), jnp.float32),
            pltpu.VMEM((groups, length, HD), jnp.float32),
        ],
        compiler_params=pltpu.CompilerParams(vmem_limit_bytes=48 * 1024 * 1024),
        cost_estimate=pl.CostEstimate(flops=1, bytes_accessed=1, transcendentals=0),
    )(table, query, keys, values, grad)


def dispatch_kernel(first_ref, rows_ref, grads_ref, out_rows, out_grads, out_pick):
    count = out_rows.shape[0]
    tokens = rows_ref.shape[1]
    padded = -(-count // 16) * 16
    tail = rows_ref[0, :, D:]
    lane = lax.broadcasted_iota(jnp.int32, (padded, 128), 1)
    row = lax.broadcasted_iota(jnp.int32, (padded, 128), 0)
    wanted = (lane == 2 * EXPERTS + first_ref[0] + row) & (row < count)
    marks = lax.dot_general(
        wanted.astype(jnp.bfloat16),
        tail,
        (((1,), (1,)), ((), ())),
        preferred_element_type=jnp.float32,
    )
    earlier = lax.broadcasted_iota(jnp.int32, (tokens, tokens), 0) < lax.broadcasted_iota(
        jnp.int32, (tokens, tokens), 1
    )
    rank = jnp.dot(
        marks.astype(jnp.bfloat16),
        earlier.astype(jnp.bfloat16),
        preferred_element_type=jnp.float32,
    )
    slot = lax.broadcasted_iota(jnp.int32, (CAP, tokens), 0).astype(jnp.float32)
    pick = jnp.concatenate(
        [
            jnp.where(
                rank[item : item + 1, :] == slot, marks[item : item + 1, :], 0.0
            ).astype(jnp.bfloat16)
            for item in range(count)
        ],
        0,
    )
    out_pick[0] = pick
    moved = jnp.dot(pick, rows_ref[0], preferred_element_type=jnp.float32).astype(jnp.bfloat16)
    moved_grads = jnp.dot(pick, grads_ref[0], preferred_element_type=jnp.float32).astype(
        jnp.bfloat16
    )
    for item in range(count):
        out_rows[item] = moved[item * CAP : (item + 1) * CAP]
        out_grads[item] = moved_grads[item * CAP : (item + 1) * CAP]


def dispatch(first, rows, grads, count):
    sources, tokens, wide = rows.shape
    return pl.pallas_call(
        dispatch_kernel,
        grid_spec=pltpu.PrefetchScalarGridSpec(
            num_scalar_prefetch=1,
            grid=(sources,),
            in_specs=[
                pl.BlockSpec((1, tokens, wide), lambda s, f: (s, 0, 0)),
                pl.BlockSpec((1, tokens, D), lambda s, f: (s, 0, 0)),
            ],
            out_specs=(
                pl.BlockSpec((count, CAP, wide), lambda s, f: (0, s, 0)),
                pl.BlockSpec((count, CAP, D), lambda s, f: (0, s, 0)),
                pl.BlockSpec((1, count * CAP, tokens), lambda s, f: (s, 0, 0)),
            ),
        ),
        out_shape=(
            jax.ShapeDtypeStruct((count, sources * CAP, wide), jnp.bfloat16),
            jax.ShapeDtypeStruct((count, sources * CAP, D), jnp.bfloat16),
            jax.ShapeDtypeStruct((sources, count * CAP, tokens), jnp.bfloat16),
        ),
        compiler_params=pltpu.CompilerParams(vmem_limit_bytes=62 * 1024 * 1024),
        cost_estimate=pl.CostEstimate(flops=1, bytes_accessed=1, transcendentals=0),
    )(first, rows, grads)


def combine_kernel(pick_ref, *refs):
    half = len(refs) // 2
    for rows_ref, out_ref in zip(refs[:half], refs[half:]):
        rows = jnp.concatenate([rows_ref[item] for item in range(rows_ref.shape[0])], 0)
        out_ref[0] = lax.dot_general(
            pick_ref[0], rows, (((0,), (0,)), ((), ())), preferred_element_type=jnp.float32
        ).astype(jnp.bfloat16)


def combine(pick, arrays):
    sources, slots, tokens = pick.shape
    count = arrays[0].shape[0]
    return pl.pallas_call(
        combine_kernel,
        grid=(sources,),
        in_specs=[pl.BlockSpec((1, slots, tokens), lambda s: (s, 0, 0))]
        + [pl.BlockSpec((count, CAP, rows.shape[2]), lambda s: (0, s, 0)) for rows in arrays],
        out_specs=tuple(
            pl.BlockSpec((1, tokens, rows.shape[2]), lambda s: (s, 0, 0)) for rows in arrays
        ),
        out_shape=tuple(
            jax.ShapeDtypeStruct((sources, tokens, rows.shape[2]), jnp.bfloat16)
            for rows in arrays
        ),
        compiler_params=pltpu.CompilerParams(vmem_limit_bytes=62 * 1024 * 1024),
        cost_estimate=pl.CostEstimate(flops=1, bytes_accessed=1, transcendentals=0),
    )(pick, *arrays)


def expert_kernel(first_ref, order_ref, slots_ref, rows_ref, grads_ref, *refs):
    whole_in, whole_out, total_in, total_out = refs[-4:]
    pieces, (produced_ref, grad_rows_ref), outs = refs[:2], refs[2:4], refs[4:-4]
    expert = first_ref[0] + pl.program_id(0)
    chunk = pl.program_id(1)
    parted = len(pieces[0].shape) == 4

    @pl.when(chunk == 0)
    def assemble():
        if not parted:
            whole_in[...] = pieces[0][0]
            whole_out[...] = pieces[1][0]
            return
        for index in range(pieces[0].shape[0]):
            block = order_ref[index]
            for piece, whole in zip(pieces, (whole_in, whole_out)):
                deep = piece.shape[2]
                whole[pl.ds(pl.multiple_of(block * deep, deep), deep), :] = piece[index, 0]

    tail = rows_ref[0, :, D:].astype(jnp.float32)
    lane = lax.broadcasted_iota(jnp.int32, tail.shape, 1)
    own = (lane == expert) | (lane == EXPERTS + expert)
    gate = jnp.sum(jnp.where(own, tail, 0.0), axis=-1, keepdims=True)
    hidden = whole_out.shape[0]
    gate_up = jnp.dot(rows_ref[0, :, :D], whole_in[...], preferred_element_type=jnp.float32)
    gate_half = gate_up[:, :hidden]
    up_half = gate_up[:, hidden:]
    sigma = 1.0 / (1.0 + jnp.exp(-gate_half))
    activated = gate_half * sigma
    middle = activated * up_half
    gated = (gate * middle).astype(jnp.bfloat16)
    produced_ref[0] = jnp.dot(gated, whole_out[...], preferred_element_type=jnp.float32).astype(
        jnp.bfloat16
    )
    grad_middle = RESIDUAL_SCALE * lax.dot_general(
        grads_ref[0],
        whole_out[...],
        (((1,), (1,)), ((), ())),
        preferred_element_type=jnp.float32,
    )
    grad_gate = jnp.sum(middle * grad_middle, axis=-1, keepdims=True)
    grad_middle = gate * grad_middle
    slope = sigma * (1.0 + gate_half * (1.0 - sigma))
    grad_hidden = jnp.concatenate(
        [grad_middle * up_half * slope, grad_middle * activated], -1
    ).astype(jnp.bfloat16)
    grad_rows_ref[0, :, :D] = lax.dot_general(
        grad_hidden,
        whole_in[...],
        (((1,), (1,)), ((), ())),
        preferred_element_type=jnp.float32,
    ).astype(jnp.bfloat16)
    high = grad_gate.astype(jnp.bfloat16).astype(jnp.float32)
    spread = jnp.where(
        lane == expert, high, jnp.where(lane == EXPERTS + expert, grad_gate - high, 0.0)
    )
    grad_rows_ref[0, :, D:] = spread.astype(jnp.bfloat16)

    turned = (((0,), (0,)), ((), ()))
    part_in = lax.dot_general(
        rows_ref[0, :, :D], grad_hidden, turned, preferred_element_type=jnp.float32
    )
    part_out = RESIDUAL_SCALE * lax.dot_general(
        gated, grads_ref[0], turned, preferred_element_type=jnp.float32
    )

    @pl.when(chunk == 0)
    def store():
        total_in[...] = part_in
        total_out[...] = part_out

    @pl.when(chunk > 0)
    def add():
        total_in[...] += part_in
        total_out[...] += part_out

    @pl.when(chunk == pl.num_programs(1) - 1)
    def finish():
        if not parted:
            outs[0][0] = total_in[...].astype(jnp.bfloat16)
            outs[1][0] = total_out[...].astype(jnp.bfloat16)
            return
        wide = total_in.shape[1]
        turns = outs[0].shape[0]
        deep = outs[0].shape[2]
        folds = (outs[0].shape[3] - D) // wide
        for number, out in enumerate(outs):
            for turn in range(turns):
                block = slots_ref[number * turns + turn]
                for fold in range(folds):
                    start = pl.multiple_of((block * folds + fold) * deep, deep)
                    out[turn, 0, :, fold * wide : (fold + 1) * wide] = total_in[
                        pl.ds(start, deep), :
                    ].astype(jnp.bfloat16)
                start = pl.multiple_of(block * deep, deep)
                out[turn, 0, :, folds * wide :] = total_out[pl.ds(start, deep), :].astype(
                    jnp.bfloat16
                )


def run_experts(first, order, rows, grads, pieces, hidden, parted):
    count, slots, wide = rows.shape
    chunk = min(512, slots)
    by_chunk = lambda e, c, *_: (e, c, 0)
    by_expert = lambda e, c, *_: (e, 0, 0)
    by_turn = lambda e, c, *_: (0, e, 0, 0)
    if parted:
        _, _, shards, ctx = block_order()
        places = []
        for step in reversed(range(shards)):
            for bit in (1, 0):
                places += [step * ctx + turn for turn in range(bit, ctx, 2)]
        places = jnp.stack([order[place] for place in places])
        deep = pieces[1].shape[2]
        folds = pieces[0].shape[2] // deep
        shapes = [(ctx // 2, count, deep, folds * 2 * hidden + D)] * (2 * shards)
        block = lambda shape: pl.BlockSpec((shape[0], 1) + shape[2:], by_turn)
    else:
        places = order
        shapes = [(count, D, 2 * hidden), (count, hidden, D)]
        block = lambda shape: pl.BlockSpec((1,) + shape[1:], by_expert)
    outs = pl.pallas_call(
        expert_kernel,
        grid_spec=pltpu.PrefetchScalarGridSpec(
            num_scalar_prefetch=3,
            grid=(count, slots // chunk),
            in_specs=[
                pl.BlockSpec((1, chunk, wide), by_chunk),
                pl.BlockSpec((1, chunk, D), by_chunk),
            ]
            + [block(piece.shape) for piece in pieces],
            out_specs=(
                pl.BlockSpec((1, chunk, D), by_chunk),
                pl.BlockSpec((1, chunk, wide), by_chunk),
            )
            + tuple(block(shape) for shape in shapes),
            scratch_shapes=[
                pltpu.VMEM((D, 2 * hidden), jnp.bfloat16),
                pltpu.VMEM((hidden, D), jnp.bfloat16),
                pltpu.VMEM((D, 2 * hidden), jnp.float32),
                pltpu.VMEM((hidden, D), jnp.float32),
            ],
        ),
        out_shape=(
            jax.ShapeDtypeStruct((count, slots, D), jnp.bfloat16),
            jax.ShapeDtypeStruct((count, slots, wide), jnp.bfloat16),
        )
        + tuple(jax.ShapeDtypeStruct(shape, jnp.bfloat16) for shape in shapes),
        compiler_params=pltpu.CompilerParams(vmem_limit_bytes=62 * 1024 * 1024),
        cost_estimate=pl.CostEstimate(flops=1, bytes_accessed=1, transcendentals=0),
    )(first, order, places, rows, grads, *pieces)
    return outs[0], outs[1], outs[2:]


def swap(rows, axis, flip):
    size = lax.axis_size(axis)
    return lax.ppermute(rows, axis, [(i, i ^ flip) for i in range(size)])


def near(place, axis, flip):
    if lax.axis_size(axis) == 2:
        return 1 - place
    if flip == 1:
        return place + 1 - 2 * lax.rem(place, 2)
    if flip == 2:
        return lax.rem(place + 2, 4)
    return 3 - place


def greet(partners):
    barrier = pltpu.get_barrier_semaphore()
    for axis, flip in partners:
        pl.semaphore_signal(
            barrier,
            inc=1,
            device_id={axis: near(lax.axis_index(axis), axis, flip)},
            device_id_type=pl.DeviceIdType.MESH,
        )
    pl.semaphore_wait(barrier, len(partners))


class Link:
    def __init__(self, sends, receives):
        self.sends, self.receives, self.used, self.started = sends, receives, 0, []

    def push(self, source, target, axis, flip):
        copy = pltpu.make_async_remote_copy(
            src_ref=source,
            dst_ref=target,
            send_sem=self.sends.at[self.used],
            recv_sem=self.receives.at[self.used],
            device_id={axis: near(lax.axis_index(axis), axis, flip)},
            device_id_type=pl.DeviceIdType.MESH,
        )
        copy.start()
        self.used += 1
        self.started.append(copy)
        return copy

    def finish(self):
        for copy in self.started:
            copy.wait_send()


class Line:
    def __init__(self, rows_ref, out_ref, sends, receives):
        z, y = lax.axis_index("dp"), lax.axis_index("expert")
        self.inner = z * (3 - z) > 0
        self.outer = z * (3 - z) < 1

        def slot(flip):
            return 2 * (near(z, "dp", flip) if flip else z) + y

        def hand(sent, received, source, target, flip, axis="dp"):
            return pltpu.make_async_remote_copy(
                src_ref=source,
                dst_ref=target,
                send_sem=sends.at[sent],
                recv_sem=receives.at[received],
                device_id={axis: near(lax.axis_index(axis), axis, flip)},
                device_id_type=pl.DeviceIdType.MESH,
            )

        def block(flip):
            return out_ref.at[slot(flip)]

        self.to_first = hand(0, 1, rows_ref, block(0), 1)
        self.across_own = hand(1, 3, rows_ref, block(0), 3)
        self.across_first = hand(2, 2, block(1), block(1), 3)
        self.pass_third = hand(3, 2, block(3), block(3), 1)
        self.pass_second = hand(8, 3, block(2), block(2), 1)
        self.over = [
            hand(4 + flip, 4 + flip, block(flip) if flip else rows_ref, block(flip), 1, "expert")
            for flip in range(4)
        ]
        self.got = [None] + [hand(0, flip, block(flip), block(flip), 1) for flip in range(1, 4)]
        self.got_over = [
            hand(0, 4 + flip, block(flip), out_ref.at[slot(flip) + 1 - 2 * y], 1, "expert")
            for flip in range(4)
        ]

    def start(self):
        self.to_first.start()

        @pl.when(self.inner)
        def inner():
            self.across_own.start()

        self.over[0].start()

    def first(self):
        self.got[1].wait_recv()

        @pl.when(self.inner)
        def inner():
            self.across_first.start()

        self.over[1].start()

    def second(self):
        @pl.when(self.inner)
        def inner():
            self.got[3].wait_recv()
            self.pass_third.start()
            self.over[3].start()

        @pl.when(self.outer)
        def outer():
            self.got[2].wait_recv()
            self.over[2].start()

    def third(self):
        @pl.when(self.inner)
        def inner():
            self.got[2].wait_recv()
            self.pass_second.start()
            self.over[2].start()

        @pl.when(self.outer)
        def outer():
            self.got[3].wait_recv()
            self.over[3].start()

    def finish(self):
        self.to_first.wait_send()

        @pl.when(self.inner)
        def inner():
            for copy in (self.across_own, self.across_first, self.pass_third, self.pass_second):
                copy.wait_send()

        for copy in self.over:
            copy.wait_send()
        for copy in self.got_over:
            copy.wait_recv()


class Fold:
    def __init__(self, blocks_ref, out_ref, over, sums, parts, sends, receives, local=None):
        z, y = lax.axis_index("dp"), lax.axis_index("expert")
        self.inner = z * (3 - z) > 0
        self.outer = z * (3 - z) < 1
        self.blocks, self.out, self.over, self.sums, self.parts = blocks_ref, out_ref, over, sums, parts
        self.y = y

        def slot(flip, plane):
            return 2 * (near(z, "dp", flip) if flip else z) + plane

        def hand(number, source, target, flip, axis="dp"):
            return pltpu.make_async_remote_copy(
                src_ref=source,
                dst_ref=target,
                send_sem=sends.at[number],
                recv_sem=receives.at[number],
                device_id={axis: near(lax.axis_index(axis), axis, flip)},
                device_id_type=pl.DeviceIdType.MESH,
            )

        self.slot = slot
        self.staged = [
            pltpu.make_async_copy(blocks_ref.at[slot(flip, y)], sums.at[flip], local.at[flip])
            for flip in range(4 if local is not None else 0)
        ]
        self.across = [
            hand(flip, blocks_ref.at[slot(flip, 1 - y)], over.at[flip], 1, "expert")
            for flip in range(4)
        ]
        self.to_line = [hand(4 + k, sums.at[3 - k], parts.at[k], 1) for k in range(3)]
        self.to_middle = [hand(7 + k, sums.at[2 + k], parts.at[3 + k], 3) for k in range(2)]
        self.to_end = hand(9, sums.at[1], parts.at[5], 1)

    def own(self, flip):
        self.across[flip].wait_recv()
        if self.staged:
            self.staged[flip].wait()
            held = self.sums[flip]
        else:
            held = self.blocks[self.slot(flip, self.y)]
        return held.astype(jnp.float32) + self.over[flip].astype(jnp.float32)

    def part(self, number):
        return self.parts[number].astype(jnp.float32)

    def start(self):
        @pl.when(self.inner)
        def inner():
            for flip in (2, 3, 1, 0):
                self.across[flip].start()

        @pl.when(self.outer)
        def outer():
            for flip in (3, 2, 1, 0):
                self.across[flip].start()

        for copy in self.staged:
            copy.start()

    def early(self, k, ends=True, middle=True):
        if middle:

            @pl.when(self.inner)
            def inner():
                total = self.own(2 + k)
                self.to_line[k].wait_recv()
                self.sums[2 + k] = (total + self.part(k)).astype(jnp.bfloat16)
                self.to_middle[k].start()

        if ends:

            @pl.when(self.outer)
            def outer():
                self.sums[3 - k] = self.own(3 - k).astype(jnp.bfloat16)
                self.to_line[k].start()

    def late(self):
        @pl.when(self.inner)
        def inner():
            total = self.own(1)
            self.to_middle[0].wait_recv()
            self.sums[1] = (total + self.part(3)).astype(jnp.bfloat16)
            self.to_end.start()

        @pl.when(self.outer)
        def outer():
            self.sums[1] = self.own(1).astype(jnp.bfloat16)
            self.to_line[2].start()

    def last(self):
        @pl.when(self.inner)
        def inner():
            total = self.own(0)
            self.to_line[2].wait_recv()
            self.to_middle[1].wait_recv()
            self.out[...] = (total + self.part(2) + self.part(4)).astype(self.out.dtype)

        @pl.when(self.outer)
        def outer():
            total = self.own(0)
            self.to_end.wait_recv()
            self.out[...] = (total + self.part(5)).astype(self.out.dtype)

    def finish(self):
        @pl.when(self.inner)
        def inner():
            for copy in self.to_middle + [self.to_end]:
                copy.wait_send()

        @pl.when(self.outer)
        def outer():
            for copy in self.to_line:
                copy.wait_send()

        for copy in self.across:
            copy.wait_send()


def fold_scratch(shape):
    return [
        pltpu.VMEM((4,) + shape, jnp.bfloat16),
        pltpu.VMEM((4,) + shape, jnp.bfloat16),
        pltpu.VMEM((6,) + shape, jnp.bfloat16),
        pltpu.SemaphoreType.DMA((10,)),
        pltpu.SemaphoreType.DMA((10,)),
    ]


def add_into(target, sources):
    def body(item, carry):
        total = sources[0][item].astype(jnp.float32)
        for source in sources[1:]:
            total = total + source[item].astype(jnp.float32)
        target[item] = total.astype(jnp.bfloat16)
        return carry

    lax.fori_loop(0, target.shape[0], body, 0)


def fetch(pairs, local):
    copies = [
        pltpu.make_async_copy(source, target, local.at[number])
        for number, (source, target) in enumerate(pairs)
    ]
    for copy in copies:
        copy.start()
    for copy in copies:
        copy.wait()


EVERYONE = [("dp", 1), ("dp", 2), ("dp", 3), ("expert", 1), ("ctx", 1), ("ctx", 2), ("ctx", 3)]


def returning_kernel(
    blocks_ref, moe_blocks, give3, keep3, give2, keep2, give1, keep1, give0,
    after_ref, input_ref, gates_ref, grad_ref, gain_ref, pack_ref, attended_ref,
    grad_after_ref, seq_grad_ref, grad_pack_ref, output_ref, arrived, done3, ready2, ready1,
    routed, over, sums, parts, fold_sends, fold_receives, fold_local,
    moe_over, moe_sums, moe_parts, moe_sends, moe_receives, moe_local,
    sent, crossed, stage, outgoing, sends, receives, local,
):
    z, c = lax.axis_index("dp"), lax.axis_index("ctx")
    greet(EVERYONE)
    link = Link(sends, receives)
    fold = Fold(blocks_ref, routed, over, sums, parts, fold_sends, fold_receives, fold_local)
    moe_fold = Fold(
        moe_blocks, routed.at[:, :D], moe_over, moe_sums, moe_parts, moe_sends, moe_receives, moe_local
    )
    gives = {3: give3, 2: give2, 1: give1, 0: give0}
    keeps = {3: keep3, 2: keep2, 1: keep1}
    core = {step: link.push(gives[step], arrived.at[step], "ctx", 1) for step in (3, 2, 1, 0)}
    fold.start()
    pair = {}
    count = stage.shape[1]

    def cross(step, cut):
        core[step].wait_recv()
        fetch([(keeps[step].at[1], stage.at[0]), (arrived.at[step, 1], stage.at[1])], local)
        add_into(sent.at[step - 1], [stage.at[0], stage.at[1]])
        source, target = sent.at[step - 1], crossed.at[step - 1]
        if cut:
            pair[step] = [
                link.push(source.at[item], target.at[item], "ctx", 2) for item in range(count)
            ]
        else:
            pair[step] = [link.push(source, target, "ctx", 2)]

    def close(step):
        fetch([(keeps[step].at[0], stage.at[2]), (arrived.at[step, 0], stage.at[3])], local)
        for copy in pair[step]:
            copy.wait_recv()
            copy.wait_send()
        add_into(sent.at[step - 1], [stage.at[2], stage.at[3], crossed.at[step - 1]])

    line = []

    def close_one(item):
        pair[3][item].wait_recv()
        pair[3][item].wait_send()
        sent[2, item] = (
            stage[2, item].astype(jnp.float32)
            + stage[3, item].astype(jnp.float32)
            + crossed[2, item].astype(jnp.float32)
        ).astype(jnp.bfloat16)
        line.append(link.push(sent.at[2, item], done3.at[item], "dp", 3))

    cross(3, True)
    fetch([(keep3.at[0], stage.at[2]), (arrived.at[3, 0], stage.at[3])], local)
    close_one(0)
    fold.early(0)
    close_one(1)
    cross(2, False)
    close_one(2)
    fold.early(1)
    for item in range(3, count):
        close_one(item)
    cross(1, False)
    fold.late()
    moe_fold.start()
    fold.last()
    moe_fold.early(0, middle=False)

    gates = gates_ref[...]
    high = routed[:, D:]
    lane = lax.broadcasted_iota(jnp.int32, high.shape, 1)
    grad_gates = jnp.where(lane < EXPERTS, high + pltpu.roll(high, 128 - EXPERTS, 1), 0.0)
    grad_picked = gates * (grad_gates - jnp.sum(gates * grad_gates, axis=-1, keepdims=True))
    grad_logits = grad_picked.astype(jnp.bfloat16)
    grad_input = routed[:, :D] + lax.dot_general(
        grad_logits,
        pack_ref[:, D:],
        (((1,), (1,)), ((), ())),
        preferred_element_type=jnp.float32,
    )
    normed, factor = normalize(after_ref[...])
    grad_after = grad_ref[...].astype(jnp.float32) + norm_back(
        grad_input * gain_ref[...], normed, factor
    )
    grad_after_ref[...] = grad_after
    grad_branch = (RESIDUAL_SCALE * grad_after).astype(jnp.bfloat16)
    wide = outgoing.shape[2]
    for index in range(outgoing.shape[0]):
        outgoing[index] = lax.dot_general(
            grad_branch,
            pack_ref[index * wide : (index + 1) * wide, :D],
            (((1,), (1,)), ((), ())),
            preferred_element_type=jnp.float32,
        ).astype(jnp.bfloat16)
    seq_grad_ref[c] = outgoing[c]
    spread = [
        link.push(outgoing.at[near(c, "ctx", flip)], seq_grad_ref.at[c], "ctx", flip)
        for flip in (1, 2, 3)
    ]
    moe_fold.early(0, ends=False)
    moe_fold.early(1, middle=False)
    close(2)
    keep_ready = [pltpu.make_async_copy(sent.at[1], ready2, local.at[0])]
    keep_ready[0].start()
    turned = (((0,), (0,)), ((), ()))
    column = (lane == EXPERTS).astype(jnp.bfloat16)
    small = lax.dot_general(
        input_ref[:, :D], grad_logits, turned, preferred_element_type=jnp.float32
    ) + lax.dot_general(
        (grad_input * normed).astype(jnp.bfloat16),
        column,
        turned,
        preferred_element_type=jnp.float32,
    )
    small = small.astype(jnp.bfloat16).reshape(grad_pack_ref.shape[:3] + (128,))
    grad_pack_ref[..., D:] = small
    moe_fold.early(1, ends=False)
    some = grad_pack_ref.shape[0] // outgoing.shape[0]
    for index in range(outgoing.shape[0]):
        part = lax.dot_general(
            attended_ref[index], grad_branch, turned, preferred_element_type=jnp.float32
        ).astype(jnp.bfloat16)
        grad_pack_ref[index * some : (index + 1) * some, :, :, :D] = part.reshape(
            (some,) + grad_pack_ref.shape[1:3] + (D,)
        )
    keep_ready[0].wait()
    moe_fold.late()
    close(1)
    fetch([(sent.at[0], ready1)], local)
    moe_fold.last()
    output_ref[...] = (after_ref[...] + RESIDUAL_SCALE * routed[:, :D]).astype(jnp.bfloat16)
    moe_fold.finish()
    for copy in spread + line + [core[0]]:
        copy.wait_recv()
    fold.finish()
    for copy in list(core.values()) + spread + line:
        copy.wait_send()


def returning(blocks, moe_blocks, parts, after, expert_input, gates, grads, gain, pack, attended, number):
    kind = jnp.bfloat16
    far = pl.BlockSpec(memory_space=pl.ANY)
    held = pl.BlockSpec(memory_space=pltpu.VMEM)
    give3, keep3, give2, keep2, give1, keep1, give0, _ = parts
    piece = give3.shape[1:]
    ctx, tokens, wide = attended.shape
    shape = blocks.shape[1:]
    return pl.pallas_call(
        returning_kernel,
        out_shape=(
            jax.ShapeDtypeStruct((tokens, D), jnp.float32),
            jax.ShapeDtypeStruct(attended.shape, kind),
            jax.ShapeDtypeStruct((8, ctx, D // (8 * ctx), shape[1]), kind),
            jax.ShapeDtypeStruct((tokens, D), kind),
            jax.ShapeDtypeStruct((4,) + give3.shape, kind),
            jax.ShapeDtypeStruct(piece, kind),
            jax.ShapeDtypeStruct(piece, kind),
            jax.ShapeDtypeStruct(piece, kind),
        ),
        in_specs=[far] * 9 + [held] * 7,
        out_specs=(held, held, held, held, far, far, far, far),
        scratch_shapes=[pltpu.VMEM(shape, jnp.float32)]
        + fold_scratch(shape)
        + [pltpu.SemaphoreType.DMA((4,))]
        + fold_scratch((tokens, D))
        + [
            pltpu.SemaphoreType.DMA((4,)),
            pltpu.VMEM((3,) + piece, kind),
            pltpu.VMEM((3,) + piece, kind),
            pltpu.VMEM((4,) + piece, kind),
            pltpu.VMEM(attended.shape, kind),
            pltpu.SemaphoreType.DMA((9 + 2 * piece[0],)),
            pltpu.SemaphoreType.DMA((9 + 2 * piece[0],)),
            pltpu.SemaphoreType.DMA((2,)),
        ],
        compiler_params=pltpu.CompilerParams(
            collective_id=number, has_side_effects=True, vmem_limit_bytes=63 * 1024 * 1024
        ),
    )(
        blocks, moe_blocks, give3, keep3, give2, keep2, give1, keep1, give0,
        after, expert_input, gates, grads, gain, pack, attended,
    )


def closing_kernel(
    ready2, ready1, keep0, arrived, table_ref, query_ref, keys_ref, values_ref, seq_grad_ref,
    normed_ref, columns_ref, grad_pack_ref, rows_ref, grad_after_ref,
    done2, done1, done0, input_grad_ref, shard_columns_ref, shard_pack_ref,
    sent, crossed, stage, mixed, flipped, grad_keys, grad_values,
    pack_core, pack_pair, pack_sent, pack_blocks, pack_over, pack_sums, pack_parts, pack_sends, pack_receives,
    scaled, scaled_core, scaled_pair, scaled_sent,
    part_blocks, part_out, part_over, part_sums, part_parts, part_sends, part_receives,
    sends, receives, local,
):
    z, c = lax.axis_index("dp"), lax.axis_index("ctx")
    greet(EVERYONE)
    link = Link(sends, receives)

    def c_at(flip):
        return near(c, "ctx", flip) if flip else c

    to_core = [
        link.push(grad_pack_ref.at[:, c_at(flip)], pack_core.at[number], "ctx", 1)
        for number, flip in enumerate((3, 1))
    ]
    line = [link.push(ready2, done2, "dp", 2), link.push(ready1, done1, "dp", 1)]
    zones = grad_pack_ref.shape[0]
    held = []

    def pack_step():
        to_core[0].wait_recv()
        for zone in range(zones):
            pack_sent[zone] = (
                grad_pack_ref[zone, c_at(2)].astype(jnp.float32)
                + pack_core[0, zone].astype(jnp.float32)
            ).astype(jnp.bfloat16)
        held.append(link.push(pack_sent, pack_pair, "ctx", 2))

    fetch([(keep0.at[1], stage.at[0]), (arrived.at[0, 1], stage.at[1])], local)
    add_into(sent, [stage.at[0], stage.at[1]])
    pair = link.push(sent, crossed, "ctx", 2)
    attend_back(
        table_ref,
        query_ref,
        keys_ref,
        values_ref,
        seq_grad_ref,
        mixed,
        flipped,
        grad_keys,
        grad_values,
        pack_step,
    )
    blocks, block = scaled.shape[:2]
    wide = normed_ref.shape[1] // blocks
    some = zones // blocks
    for index in range(blocks):
        part = lax.dot_general(
            normed_ref[:, index * wide : (index + 1) * wide],
            mixed[...],
            (((0,), (0,)), ((), ())),
            preferred_element_type=jnp.float32,
        ).astype(jnp.bfloat16)
        part_blocks[index * some : (index + 1) * some] = part.reshape(
            (some,) + part_blocks.shape[1:]
        )
    part_fold = Fold(
        part_blocks, part_out, part_over, part_sums, part_parts, part_sends, part_receives
    )
    part_fold.start()
    for index in range(blocks):
        scaled[index] = lax.dot_general(
            mixed[index * block : (index + 1) * block, :],
            columns_ref[...],
            (((1,), (1,)), ((), ())),
            preferred_element_type=jnp.float32,
        ).astype(jnp.bfloat16)
    scaled_to_core = [
        link.push(scaled.at[c_at(flip)], scaled_core.at[number], "ctx", 1)
        for number, flip in enumerate((3, 1))
    ]
    scaled_to_core[0].wait_recv()
    scaled_sent[...] = (
        scaled[c_at(2)].astype(jnp.float32) + scaled_core[0].astype(jnp.float32)
    ).astype(jnp.bfloat16)
    scaled_over_pair = link.push(scaled_sent, scaled_pair, "ctx", 2)
    part_fold.early(0)
    to_core[1].wait_recv()
    held[0].wait_recv()
    for zone in range(zones):
        pack_blocks[zone] = (
            grad_pack_ref[zone, c].astype(jnp.float32)
            + pack_core[1, zone].astype(jnp.float32)
            + pack_pair[zone].astype(jnp.float32)
        ).astype(jnp.bfloat16)
    pack_fold = Fold(
        pack_blocks, shard_pack_ref, pack_over, pack_sums, pack_parts, pack_sends, pack_receives
    )
    pack_fold.start()
    part_fold.early(1)
    pack_fold.early(0)
    pack_fold.early(1)
    part_fold.late()
    part_fold.last()
    apart = [
        link.push(part_out.at[c_at(flip)], shard_columns_ref.at[c], "ctx", flip)
        for flip in (1, 2, 3)
    ]
    shard_columns_ref[c] = part_out[c]
    scaled_to_core[1].wait_recv()
    scaled_over_pair.wait_recv()
    grad_normed = (
        scaled[c].astype(jnp.float32)
        + scaled_core[1].astype(jnp.float32)
        + scaled_pair[...].astype(jnp.float32)
    )
    normed, factor = normalize(rows_ref[...].astype(jnp.float32))
    input_grad_ref[...] = grad_after_ref[...] + norm_back(grad_normed, normed, factor)
    pack_fold.late()
    pack_fold.last()
    fetch([(keep0.at[0], stage.at[0]), (arrived.at[0, 0], stage.at[1])], local)
    pair.wait_recv()
    pair.wait_send()
    add_into(sent, [stage.at[0], stage.at[1], crossed])
    fetch([(sent, done0)], local)
    for copy in apart + line:
        copy.wait_recv()
    part_fold.finish()
    pack_fold.finish()
    for copy in link.started:
        if copy is not pair:
            copy.wait_send()


def closing(
    ready2, ready1, keep0, arrived, table, query, keys, values, seq_grad, normed, columns,
    grad_pack, rows, grad_after, number,
):
    kind = jnp.bfloat16
    far = pl.BlockSpec(memory_space=pl.ANY)
    held = pl.BlockSpec(memory_space=pltpu.VMEM)
    piece = ready2.shape
    heads, length = query.shape[:2]
    groups = keys.shape[0]
    zones, ctx, share, wide = grad_pack.shape
    width = columns.shape[1]
    pack = (zones, share, wide)
    block = (length // ctx, D)
    part = (ctx, share, width)
    return pl.pallas_call(
        closing_kernel,
        out_shape=(
            jax.ShapeDtypeStruct(piece, kind),
            jax.ShapeDtypeStruct(piece, kind),
            jax.ShapeDtypeStruct(piece, kind),
            jax.ShapeDtypeStruct(rows.shape, jnp.float32),
            jax.ShapeDtypeStruct(part, kind),
            jax.ShapeDtypeStruct((share, wide), jnp.float32),
        ),
        in_specs=[far] * 4 + [held] * 10,
        out_specs=(far, far, far, held, held, held),
        scratch_shapes=[
            pltpu.VMEM(piece, kind),
            pltpu.VMEM(piece, kind),
            pltpu.VMEM((2,) + piece, kind),
            pltpu.VMEM((length, width), kind),
            pltpu.VMEM((groups * HD, length), kind),
            pltpu.VMEM((groups, length, HD), jnp.float32),
            pltpu.VMEM((groups, length, HD), jnp.float32),
            pltpu.VMEM((2,) + pack, kind),
            pltpu.VMEM(pack, kind),
            pltpu.VMEM(pack, kind),
            pltpu.VMEM(pack, kind),
        ]
        + fold_scratch(pack[1:])
        + [
            pltpu.VMEM((ctx,) + block, kind),
            pltpu.VMEM((2,) + block, kind),
            pltpu.VMEM(block, kind),
            pltpu.VMEM(block, kind),
            pltpu.VMEM((zones,) + part, kind),
            pltpu.VMEM(part, kind),
        ]
        + fold_scratch(part)
        + [
            pltpu.SemaphoreType.DMA((12,)),
            pltpu.SemaphoreType.DMA((12,)),
            pltpu.SemaphoreType.DMA((2,)),
        ],
        compiler_params=pltpu.CompilerParams(
            collective_id=number, has_side_effects=True, vmem_limit_bytes=62 * 1024 * 1024
        ),
    )(
        ready2, ready1, keep0, arrived, table, query, keys, values, seq_grad, normed, columns,
        grad_pack, rows, grad_after,
    )


def route_rows(rows, pack_ref, attended_ref, routes_ref, after_ref, gates_ref, gain_ref, packed):
    quarters = attended_ref.shape[0]
    wide = pack_ref.shape[-1]
    branch = jnp.zeros((rows.shape[0], D), jnp.float32)
    tails = []
    for index in range(quarters):
        pack = pack_ref[index].reshape(-1, wide)
        branch += jnp.dot(attended_ref[index], pack[:, :D], preferred_element_type=jnp.float32)
        tails.append(pack[:, D:])
    tail = jnp.concatenate(tails, 0)
    after = rows.astype(jnp.float32) + RESIDUAL_SCALE * branch
    after_ref[...] = after
    normed, _ = normalize(after)
    single = lax.broadcasted_iota(jnp.int32, (8, 128), 1) == EXPERTS
    gain = lax.dot_general(
        single.astype(jnp.bfloat16),
        tail,
        (((1,), (1,)), ((), ())),
        preferred_element_type=jnp.float32,
    )[:1]
    gain_ref[...] = gain
    expert_input = (normed * gain).astype(jnp.bfloat16)
    logits = jnp.dot(expert_input, tail, preferred_element_type=jnp.float32)
    lane = lax.broadcasted_iota(jnp.int32, logits.shape, 1)
    marks = jnp.zeros(logits.shape, jnp.float32)
    for index in range(TOP):
        marks = jnp.where(lane == routes_ref[:, index : index + 1], 1.0, marks)
    chosen = marks > 0.0
    peak = jnp.max(jnp.where(chosen, logits, -3e38), axis=-1, keepdims=True)
    raised = jnp.where(chosen, jnp.exp(jnp.where(chosen, logits - peak, 0.0)), 0.0)
    gates = raised / jnp.sum(raised, axis=-1, keepdims=True)
    gates_ref[...] = gates
    high = gates.astype(jnp.bfloat16).astype(jnp.float32)
    packed[:, :D] = expert_input
    packed[:, D:] = (
        high + pltpu.roll(gates - high, EXPERTS, 1) + pltpu.roll(marks, 2 * EXPERTS, 1)
    ).astype(jnp.bfloat16)


def opening_kernel(
    rows_ref, table_ref, columns_ref, pack_ref, weights_in, weights_out, grads_ref, routes_ref,
    all_rows, all_table, all_columns, all_pack, pieces_in, pieces_out, all_grads, all_packed,
    after_ref, gates_ref, gain_ref, packed,
    normed_ref, query_ref, keys_ref, values_ref, attended_ref,
    outgoing, flipped, sends, receives, line_sends, line_receives, token_sends, token_receives, locals_,
):
    z, y, c = lax.axis_index("dp"), lax.axis_index("expert"), lax.axis_index("ctx")
    greet(EVERYONE)
    link = Link(sends, receives)
    line = Line(grads_ref, all_grads, line_sends, line_receives)
    token_line = Line(packed, all_packed, token_sends, token_receives)
    own = 2 * z + y
    count = weights_in.shape[1]

    def z_at(flip):
        return near(z, "dp", flip) if flip else z

    def c_at(flip):
        return near(c, "ctx", flip) if flip else c

    def keep(number, source, target):
        copy = pltpu.make_async_copy(source, target, locals_.at[number])
        copy.start()
        return copy

    def both(target, source, axis, flip):
        return [link.push(source(ref), target(ref), axis, flip) for ref in (pieces_in, pieces_out)]

    def share(*place):
        step, rest = place[0], place[1:]
        source = lambda ref: ref.at[(step, 0) + rest]
        over = both(lambda ref: ref.at[(step, 2) + rest], source, "ctx", 2)
        core = both(lambda ref: ref.at[(step, 1) + rest], source, "ctx", 1)
        return over, core

    def hand_on(*place):
        step, rest = place[0], place[1:]
        return both(
            lambda ref: ref.at[(step, 3) + rest], lambda ref: ref.at[(step, 2) + rest], "ctx", 1
        )

    def move(step, *rest):
        return [
            link.push(weights.at[(z_at(step),) + rest], ref.at[(step, 0) + rest], "dp", step)
            for weights, ref in ((weights_in, pieces_in), (weights_out, pieces_out))
        ]

    def arrive(copies):
        for copy in copies:
            copy.wait_recv()

    kept = [
        keep(0, columns_ref.at[c], all_columns.at[own, c]),
        keep(1, weights_in.at[z], pieces_in.at[0, 0]),
        keep(2, weights_out.at[z], pieces_out.at[0, 0]),
        keep(3, rows_ref, all_rows.at[c]),
        keep(4, pack_ref, all_pack.at[z, y, c]),
        keep(5, grads_ref, all_grads.at[own]),
        keep(7, table_ref, all_table.at[c]),
    ]
    cut = [
        link.push(columns_ref.at[c_at(flip)], all_columns.at[own, c], "ctx", flip)
        for flip in (1, 2, 3)
    ]
    table_all = [link.push(table_ref, all_table.at[c], "ctx", flip) for flip in (1, 2, 3)]
    rows_over = link.push(rows_ref, all_rows.at[c], "ctx", 2)
    rows_core = link.push(rows_ref, all_rows.at[c], "ctx", 1)
    pack_line = [link.push(pack_ref, all_pack.at[z, y, c], "dp", flip) for flip in (1, 2, 3)]
    kept[0].wait()
    arrive(cut)
    column_line = [
        link.push(all_columns.at[own], all_columns.at[own], "dp", flip) for flip in (1, 2, 3)
    ]
    column_over = [link.push(all_columns.at[own], all_columns.at[own], "expert", 1)]
    kept[1].wait()
    kept[2].wait()
    rows_over.wait_recv()
    rows_pass = link.push(all_rows.at[c_at(2)], all_rows.at[c_at(2)], "ctx", 1)
    shared = [share(0)]
    arrive(pack_line)
    kept[4].wait()
    pack_over = link.push(all_pack.at[:, y, c], all_pack.at[:, y, c], "expert", 1)
    for flip in (1, 2, 3):
        column_line[flip - 1].wait_recv()
        block = all_columns.at[2 * z_at(flip) + y]
        column_over.append(link.push(block, block, "expert", 1))
    moved = {2: move(2), 1: move(1)}
    line.start()
    arrive([pack_over])
    pack_pair = link.push(all_pack.at[:, :, c], all_pack.at[:, :, c], "ctx", 2)
    pack_core = link.push(all_pack.at[:, :, c], all_pack.at[:, :, c], "ctx", 1)
    arrive([rows_core, rows_pass] + column_over + table_all)
    kept[3].wait()
    kept[6].wait()
    project_rows(
        all_rows,
        all_table,
        all_columns[...].reshape(D, all_columns.shape[-1]),
        normed_ref,
        query_ref,
        keys_ref,
        values_ref,
        flipped,
    )
    for index in range(all_rows.shape[0]):
        attend_rows(index, all_rows.shape[1], query_ref, keys_ref, outgoing, flipped)
    attended = [
        link.push(outgoing.at[c_at(flip)], attended_ref.at[c], "ctx", flip) for flip in (1, 2, 3)
    ]
    attended_ref[c] = outgoing[c]
    arrive([pack_pair])
    pack_last = link.push(all_pack.at[:, :, c_at(2)], all_pack.at[:, :, c_at(2)], "ctx", 1)
    arrive([pack_core, pack_last] + attended)
    route_rows(
        all_rows[c], all_pack, attended_ref, routes_ref, after_ref, gates_ref, gain_ref, packed
    )
    token_line.start()
    kept.append(keep(6, packed, all_packed.at[own]))
    line.first()
    arrive(shared[0][0])
    passed = hand_on(0)
    arrive(moved[1])
    shared.append(share(1))
    line.second()
    token_line.first()
    line.third()
    token_line.second()
    arrive(moved[2])
    shared.append(share(2))
    last = [move(3, 0), move(3, 1)]
    token_line.third()
    arrive(shared[1][0])
    passed += hand_on(1)

    def next_piece(item):
        arrive(last[item])
        if item + 2 < count:
            last.append(move(3, item + 2))
        shared.append(share(3, item))

    for item in range(count):
        next_piece(item)
    arrive(shared[2][0])
    passed += hand_on(2)
    for item in range(count):
        arrive(shared[3 + item][0])
        passed += hand_on(3, item)
    kept[5].wait()
    kept[7].wait()
    arrive(passed)
    for over, core in shared:
        arrive(core)
    line.finish()
    token_line.finish()
    link.finish()


def opening(rows, table, columns, pack, weights_in, weights_out, grads, routes, heads, groups, number):
    ctx = columns.shape[0]
    shards, count = weights_in.shape[:2]
    tokens = rows.shape[0]
    kind = jnp.bfloat16
    copies = 27 + 2 * (2 + 3 * 3 + 5 * count)
    far = pl.BlockSpec(memory_space=pl.ANY)
    held = pl.BlockSpec(memory_space=pltpu.VMEM)
    all_rows = (ctx,) + rows.shape
    return pl.pallas_call(
        opening_kernel,
        out_shape=(
            jax.ShapeDtypeStruct(all_rows, kind),
            jax.ShapeDtypeStruct((ctx,) + table.shape, kind),
            jax.ShapeDtypeStruct((8,) + columns.shape, kind),
            jax.ShapeDtypeStruct((shards, 2, ctx) + pack.shape, kind),
            jax.ShapeDtypeStruct((shards, ctx) + weights_in.shape[1:], kind),
            jax.ShapeDtypeStruct((shards, ctx) + weights_out.shape[1:], kind),
            jax.ShapeDtypeStruct((8,) + grads.shape, kind),
            jax.ShapeDtypeStruct((8, tokens, D + 128), kind),
            jax.ShapeDtypeStruct((tokens, D), jnp.float32),
            jax.ShapeDtypeStruct((tokens, 128), jnp.float32),
            jax.ShapeDtypeStruct((1, D), jnp.float32),
            jax.ShapeDtypeStruct((tokens, D + 128), kind),
        )
        + attend_shapes(all_rows, heads, groups),
        in_specs=[far] * 7 + [held],
        out_specs=(held, held, held, held, far, far, far, far) + (held,) * 9,
        scratch_shapes=[
            pltpu.VMEM((ctx, rows.shape[0], heads * HD), kind),
            pltpu.VMEM((groups * HD, ctx * rows.shape[0]), kind),
            pltpu.SemaphoreType.DMA((copies,)),
            pltpu.SemaphoreType.DMA((copies,)),
            pltpu.SemaphoreType.DMA((9,)),
            pltpu.SemaphoreType.DMA((8,)),
            pltpu.SemaphoreType.DMA((9,)),
            pltpu.SemaphoreType.DMA((8,)),
            pltpu.SemaphoreType.DMA((8,)),
        ],
        compiler_params=pltpu.CompilerParams(
            collective_id=number, has_side_effects=True, vmem_limit_bytes=56 * 1024 * 1024
        ),
    )(rows, table, columns, pack, weights_in, weights_out, grads, routes)


def split_high_low(values):
    high = values.astype(jnp.bfloat16)
    return high, (values - high.astype(jnp.float32)).astype(jnp.bfloat16)


def pad_columns(like, columns):
    return jnp.zeros((like.shape[0], columns), like.dtype)


def gather_ctx(rows):
    ctx = lax.axis_size("ctx")
    column = lax.axis_index("ctx")
    pieces = {0: rows}
    flip = ctx // 2
    while flip:
        pieces.update({turn ^ flip: swap(item, "ctx", flip) for turn, item in pieces.items()})
        flip //= 2
    out = jnp.zeros((ctx,) + rows.shape, rows.dtype)
    for turn in range(ctx):
        out = lax.dynamic_update_index_in_dim(out, pieces[turn], column ^ turn, 0)
    return out


def exchange_ctx(blocks):
    column = lax.axis_index("ctx")
    out = jnp.zeros(blocks.shape, blocks.dtype)
    for turn in range(blocks.shape[0]):
        item = lax.dynamic_index_in_dim(blocks, column ^ turn, 0, keepdims=False)
        if turn:
            item = swap(item, "ctx", turn)
        out = lax.dynamic_update_index_in_dim(out, item, column ^ turn, 0)
    return out


def scatter_ctx(blocks):
    column = lax.axis_index("ctx")
    flip = 1
    held = blocks
    while flip < lax.axis_size("ctx"):
        pairs = held.reshape((held.shape[0] // 2, 2) + held.shape[1:])
        bit = (column // flip) % 2
        keep = lax.dynamic_index_in_dim(pairs, bit, 1, keepdims=False)
        give = lax.dynamic_index_in_dim(pairs, 1 - bit, 1, keepdims=False)
        held = keep.astype(jnp.float32) + swap(give, "ctx", flip).astype(jnp.float32)
        flip *= 2
        if flip < lax.axis_size("ctx"):
            held = held.astype(jnp.bfloat16)
    return held[0]


def group_columns(rows, ctx):
    depth = rows.shape[0]
    cuts = (rows[:, : H * HD], rows[:, H * HD : (H + KV) * HD], rows[:, (H + KV) * HD :])
    return jnp.concatenate([cut.reshape(depth, ctx, -1) for cut in cuts], -1).transpose(1, 0, 2)


def ungroup_columns(groups):
    ctx, depth, _ = groups.shape
    query, key = H * HD // ctx, KV * HD // ctx
    cuts = (groups[..., :query], groups[..., query : query + key], groups[..., query + key :])
    return jnp.concatenate([cut.transpose(1, 0, 2).reshape(depth, -1) for cut in cuts], 1)


def block_order():
    shards, ctx = lax.axis_size("dp"), lax.axis_size("ctx")
    place, column = lax.axis_index("dp"), lax.axis_index("ctx")
    return place, column, shards, ctx


def fold_weights(expert_in, expert_out):
    deep = expert_out.shape[1]
    folds = expert_in.shape[1] // deep
    cuts = [expert_in[:, fold * deep : (fold + 1) * deep] for fold in range(folds)]
    return jnp.concatenate(cuts + [expert_out], -1)


def piece_order():
    place, column, shards, ctx = block_order()
    blocks = [
        (place ^ step) * ctx + (column ^ turn) for step in range(shards) for turn in range(ctx)
    ]
    return jnp.stack(blocks).astype(jnp.int32)


def spread_weights(expert_in, expert_out):
    shards = lax.axis_size("dp")
    count, depth = expert_in.shape[:2]
    part = FFE // shards
    cut = expert_in.reshape(count, depth, 2, shards, part).transpose(3, 0, 1, 2, 4)
    moved_in = lax.all_to_all(cut, "dp", split_axis=0, concat_axis=0, tiled=True)
    all_in = lax.all_gather(moved_in.transpose(1, 0, 2, 3, 4), "ctx", axis=2, tiled=True)
    all_out = lax.all_gather(expert_out, "ctx", axis=1, tiled=True)
    return [all_in.reshape(count, -1, 2 * part), all_out]


def collect_weights(grad_in, grad_out):
    shards = lax.axis_size("dp")
    count = grad_in.shape[0]
    part = FFE // shards
    part_in = lax.psum_scatter(
        grad_in.reshape(count, shards, -1, 2, part), "ctx", scatter_dimension=2, tiled=True
    )
    own_in = lax.all_to_all(
        part_in.transpose(1, 0, 2, 3, 4), "dp", split_axis=0, concat_axis=0, tiled=True
    )
    own_in = own_in.transpose(1, 2, 3, 0, 4).reshape(count, -1, 2 * FFE)
    own_out = lax.psum_scatter(grad_out, "ctx", scatter_dimension=1, tiled=True)
    return [(0, fold_weights(own_in, own_out))]


def expert_step_kernel(places_ref, *refs):
    states, outs = refs[-14:-8], refs[-8:]
    grads = refs[:-14]
    number = pl.program_id(0)
    wide = states[0].shape[2]
    deep = states[3].shape[1]
    folds = states[0].shape[1] // deep
    rates = learn_rates()

    def update(grad_ref):
        for fold in range(folds):
            span = pl.ds(fold * deep, deep)
            grad = grad_ref[0, :, fold * wide : (fold + 1) * wide].astype(jnp.float32)
            news = adam_step(
                states[0][0, span, :],
                states[1][0, span, :],
                states[2][0, span, :],
                grad,
                DECAY_RATE,
                rates[5],
            )
            for out, new in zip(outs[:4], news):
                out[0, span, :] = new
        grad = grad_ref[0, :, folds * wide :].astype(jnp.float32)
        news = adam_step(states[3][0], states[4][0], states[5][0], grad, DECAY_RATE, rates[6])
        for out, new in zip(outs[4:], news):
            out[0] = new

    count = pl.num_programs(0) // len(grads)
    for index, grad_ref in enumerate(grads):
        pl.when(number // count == index)(functools.partial(update, grad_ref))


def expert_step(places, grads, states):
    count = grads[0].shape[0]
    shapes = [states[1].shape] * 4 + [states[4].shape] * 4
    moved = lambda e, p: (p[e // count] * count + e % count, 0, 0)
    block = lambda shape: pl.BlockSpec((1,) + shape[1:], moved)

    def grad_spec(index):
        return pl.BlockSpec(
            (1,) + grads[0].shape[1:], lambda e, p: (jnp.clip(e - index * count, 0, count - 1), 0, 0)
        )

    return pl.pallas_call(
        expert_step_kernel,
        grid_spec=pltpu.PrefetchScalarGridSpec(
            num_scalar_prefetch=1,
            grid=(count * len(grads),),
            in_specs=[grad_spec(index) for index in range(len(grads))]
            + [block(state.shape) for state in states],
            out_specs=tuple(block(shape) for shape in shapes),
        ),
        out_shape=tuple(jax.ShapeDtypeStruct(shape, jnp.float32) for shape in shapes),
        compiler_params=pltpu.CompilerParams(vmem_limit_bytes=62 * 1024 * 1024),
        cost_estimate=pl.CostEstimate(flops=1, bytes_accessed=1, transcendentals=0),
    )(places, *grads, *states)


def local(
    tokens,
    cotangent,
    routes,
    positions,
    gain_attend,
    gain_attend_mean,
    gain_attend_square,
    project_in,
    project_in_mean,
    project_in_square,
    project_out,
    project_out_mean,
    project_out_square,
    gain_expert,
    gain_expert_mean,
    gain_expert_square,
    router_weight,
    router_weight_mean,
    router_weight_square,
    expert_in,
    expert_in_mean,
    expert_in_square,
    expert_out,
    expert_out_mean,
    expert_out_square,
):
    everywhere = ("dp", "expert", "ctx")
    owners = ("dp", "expert")
    shards = lax.axis_size("dp")
    planes = lax.axis_size("expert")
    ctx = lax.axis_size("ctx")
    rows_local = tokens.shape[0]
    local_count = expert_in.shape[0]
    close = (shards, planes, ctx) == (4, 2, 4) and local_count % shards == 0
    heads, groups = H // ctx, KV // ctx
    hidden_in = tokens.astype(jnp.float32)

    half = HD // 2
    freqs = ROPE_BASE ** (-jnp.arange(half, dtype=jnp.float32) * 2.0 / HD)
    angles = positions.astype(jnp.float32)[:, None] * freqs[None, :]
    table = jnp.concatenate(split_high_low(jnp.cos(angles)) + split_high_low(jnp.sin(angles)), 1)
    gain_attend_wide = gain_attend.astype(jnp.float32)[:, None]
    scaled_in = (gain_attend_wide * project_in.astype(jnp.float32)).astype(jnp.bfloat16)
    columns = group_columns(scaled_in, ctx)
    pack_out = jnp.concatenate(
        [project_out, router_weight, gain_expert[:, None], pad_columns(project_out, 87)], 1
    )
    order = piece_order()
    if close:
        parted = lambda array: array.reshape((shards, -1) + array.shape[1:])
        (
            _, seq_table, own_in, full_pack_out, all_in, all_out, all_grads, all_packed,
            after, gates_wide, gain_two, packed,
            seq_normed, query, keys, values, attended_heads,
        ) = opening(
            tokens, table, columns, pack_out, parted(expert_in), parted(expert_out), cotangent, routes,
            heads, groups, 1,
        )
        pieces = [array.reshape((-1,) + array.shape[2:]) for array in (all_in, all_out)]
    else:
        seq_rows, seq_table = gather_ctx(tokens), gather_ctx(table)
        own_in = lax.all_gather(exchange_ctx(columns), owners, axis=0, tiled=False)
        full_pack_out = lax.all_gather(pack_out, everywhere, axis=0, tiled=True)
        all_grads = lax.all_gather(cotangent, owners, axis=0, tiled=False)
        pieces = spread_weights(expert_in, expert_out)
        seq_normed, query, keys, values, seq_attended = attend_forward(
            seq_rows, seq_table, own_in.reshape(D, -1), heads, groups
        )
        attended_heads = exchange_ctx(seq_attended)
    seq_table = seq_table.reshape(-1, 128)
    own_in = own_in.reshape(D, -1)
    full_pack_out = full_pack_out.reshape(H * HD, -1)
    if not close:
        full_out = full_pack_out[:, :D]
        full_router = full_pack_out[:, D : D + EXPERTS]
        gain_two = full_pack_out[:, D + EXPERTS].astype(jnp.float32)[None]
        attended = attended_heads.transpose(1, 0, 2).reshape(rows_local, H * HD)
        branch = jnp.dot(attended, full_out, preferred_element_type=jnp.float32)
        after = hidden_in + RESIDUAL_SCALE * branch
        normed_two, factor_two = normalize(after)
        expert_input = (normed_two * gain_two).astype(jnp.bfloat16)
        logits = jnp.dot(expert_input, full_router, preferred_element_type=jnp.float32)
        chosen = jnp.any(routes[:, :, None] == jnp.arange(EXPERTS, dtype=jnp.int32), axis=1)
        peak = jnp.max(jnp.where(chosen, logits, -3e38), axis=-1, keepdims=True)
        raised = jnp.where(chosen, jnp.exp(jnp.where(chosen, logits - peak, 0.0)), 0.0)
        gates = raised / jnp.sum(raised, axis=-1, keepdims=True)
        packed = jnp.concatenate(
            (expert_input,)
            + split_high_low(gates)
            + (chosen.astype(jnp.bfloat16), pad_columns(expert_input, 128 - 3 * EXPERTS)),
            1,
        )
        all_packed = lax.all_gather(packed, owners, axis=0, tiled=False)

    first = lax.axis_index("expert") * local_count
    count = local_count
    hidden = FFE // shards
    if close:
        count = local_count // shards
        hidden = FFE
        first = first + lax.axis_index("dp") * count
    first = first.astype(jnp.int32).reshape(1)
    slot_rows, slot_grads, pick = dispatch(first, all_packed, all_grads, count)
    produced, grad_rows, parts = run_experts(
        first, order, slot_rows, slot_grads, pieces, hidden, close
    )
    shared_grads, shared = combine(pick, (grad_rows, produced))
    if close:
        place = lax.axis_index("dp")
        (
            grad_after, seq_grad, grad_pack_out, block_output, arrived, done3, ready2, ready1,
        ) = returning(
            shared_grads,
            shared,
            parts,
            after,
            packed,
            gates_wide,
            cotangent,
            gain_two,
            full_pack_out,
            attended_heads,
            3,
        )
        done2, done1, done0, input_grad, shard_columns, shard_pack_out = closing(
            ready2,
            ready1,
            parts[7],
            arrived,
            seq_table,
            query,
            keys,
            values,
            seq_grad,
            seq_normed,
            own_in,
            grad_pack_out,
            tokens,
            grad_after,
            4,
        )
        expert_grads = [
            (near(place, "dp", 3), done3),
            (near(place, "dp", 2), done2),
            (near(place, "dp", 1), done1),
            (place, done0),
        ]
    else:
        grad_routed = lax.psum_scatter(
            shared_grads, owners, scatter_dimension=0, tiled=False
        ).astype(jnp.float32)
        moe = lax.psum_scatter(shared, owners, scatter_dimension=0, tiled=False)
        block_output = (after + RESIDUAL_SCALE * moe.astype(jnp.float32)).astype(jnp.bfloat16)
        expert_grads = collect_weights(*parts)
        grad_final = cotangent.astype(jnp.float32)
        grad_gates = grad_routed[:, D : D + EXPERTS] + grad_routed[:, D + EXPERTS : D + 2 * EXPERTS]
        grad_picked = gates * (grad_gates - jnp.sum(gates * grad_gates, axis=-1, keepdims=True))
        grad_logits = grad_picked.astype(jnp.bfloat16)
        grad_from_router = jnp.einsum(
            "te,de->td", grad_logits, full_router, preferred_element_type=jnp.float32
        )
        grad_input = grad_from_router + grad_routed[:, :D]
        grad_after = grad_final + norm_back(grad_input * gain_two, normed_two, factor_two)
        grad_branch = (RESIDUAL_SCALE * grad_after).astype(jnp.bfloat16)
        grad_attended = jnp.einsum(
            "td,cd->tc", grad_branch, full_out, preferred_element_type=jnp.float32
        ).astype(jnp.bfloat16)
        seq_grad = exchange_ctx(
            grad_attended.reshape(rows_local, ctx, heads * HD).transpose(1, 0, 2)
        )
        grad_mixed = attend_backward(seq_table, query, keys, values, seq_grad)
        grad_in_part = jnp.einsum(
            "td,tc->dc", seq_normed, grad_mixed, preferred_element_type=jnp.float32
        ).astype(jnp.bfloat16)
        grad_in_part = grad_in_part.reshape(shards * planes, -1, grad_in_part.shape[1])
        shard_columns = lax.psum_scatter(grad_in_part, owners, scatter_dimension=0, tiled=False)
        shard_columns = exchange_ctx(shard_columns.reshape(ctx, -1, shard_columns.shape[-1]))
        grad_scaled = jnp.einsum(
            "tc,dc->td", grad_mixed, own_in, preferred_element_type=jnp.float32
        ).astype(jnp.bfloat16)
        grad_normed = scatter_ctx(grad_scaled.reshape(ctx, rows_local, D))
        normed_one, factor_one = normalize(hidden_in)
        input_grad = grad_after + norm_back(grad_normed, normed_one, factor_one)
        grad_project_out = jnp.einsum(
            "tc,td->cd", attended, grad_branch, preferred_element_type=jnp.float32
        ).astype(jnp.bfloat16)
        ones = jnp.where(jnp.arange(128) == EXPERTS, 1.0, 0.0).astype(jnp.bfloat16)
        grad_small = jnp.einsum(
            "td,te->de",
            jnp.concatenate([expert_input, (grad_input * normed_two).astype(jnp.bfloat16)], 0),
            jnp.concatenate(
                [
                    jnp.pad(grad_logits, ((0, 0), (0, 128 - EXPERTS))),
                    jnp.broadcast_to(ones, (rows_local, 128)),
                ],
                0,
            ),
            preferred_element_type=jnp.float32,
        ).astype(jnp.bfloat16)
        grad_pack_out = jnp.concatenate([grad_project_out, grad_small], 1)
        shard_pack_out = lax.psum_scatter(
            grad_pack_out, everywhere, scatter_dimension=0, tiled=True
        ).astype(jnp.float32)
    shard_scaled = ungroup_columns(shard_columns).astype(jnp.float32)
    shard_in = gain_attend_wide * shard_scaled
    shard_attend = jnp.sum(shard_scaled * project_in.astype(jnp.float32), axis=1)
    shard_out = shard_pack_out[:, :D]
    shard_router = shard_pack_out[:, D : D + EXPERTS]
    shard_expert = shard_pack_out[:, D + EXPERTS]
    rates = learn_rates()
    results = [block_output, input_grad]
    results.extend(
        adam_step(gain_attend, gain_attend_mean, gain_attend_square, shard_attend, 0.0, rates[0])
    )
    results.extend(
        adam_step(project_in, project_in_mean, project_in_square, shard_in, DECAY_RATE, rates[1])
    )
    results.extend(
        adam_step(
            project_out, project_out_mean, project_out_square, shard_out, DECAY_RATE, rates[2]
        )
    )
    results.extend(
        adam_step(gain_expert, gain_expert_mean, gain_expert_square, shard_expert, 0.0, rates[3])
    )
    results.extend(
        adam_step(
            router_weight,
            router_weight_mean,
            router_weight_square,
            shard_router,
            DECAY_RATE,
            rates[4],
        )
    )
    states = (expert_in, expert_in_mean, expert_in_square, expert_out, expert_out_mean, expert_out_square)
    places = jnp.stack([jnp.asarray(place, jnp.int32) for place, _ in expert_grads])
    expert_outs = expert_step(places, [folded for _, folded in expert_grads], states)
    results.extend(expert_outs)
    return tuple(results)


def solution(mesh):
    placed = (
        P(("dp", "expert", "ctx"), None),
        P(("dp", "expert", "ctx"), None),
        P(("dp", "expert", "ctx"), None),
        P(("dp", "expert", "ctx")),
        P(("dp", "expert", "ctx")),
        P(("dp", "expert", "ctx")),
        P(("dp", "expert", "ctx")),
        P(("dp", "expert", "ctx"), None),
        P(("dp", "expert", "ctx"), None),
        P(("dp", "expert", "ctx"), None),
        P(("dp", "expert", "ctx"), None),
        P(("dp", "expert", "ctx"), None),
        P(("dp", "expert", "ctx"), None),
        P(("dp", "expert", "ctx")),
        P(("dp", "expert", "ctx")),
        P(("dp", "expert", "ctx")),
        P(("dp", "expert", "ctx"), None),
        P(("dp", "expert", "ctx"), None),
        P(("dp", "expert", "ctx"), None),
        P("expert", ("dp", "ctx"), None),
        P("expert", ("dp", "ctx"), None),
        P("expert", ("dp", "ctx"), None),
        P("expert", ("dp", "ctx"), None),
        P("expert", ("dp", "ctx"), None),
        P("expert", ("dp", "ctx"), None),
    )
    return jax.shard_map(
        local,
        mesh=mesh,
        in_specs=placed,
        out_specs=(
            P(("dp", "expert", "ctx"), None),
            P(("dp", "expert", "ctx"), None),
            P(("dp", "expert", "ctx")),
            P(("dp", "expert", "ctx")),
            P(("dp", "expert", "ctx")),
            P(("dp", "expert", "ctx")),
            P(("dp", "expert", "ctx"), None),
            P(("dp", "expert", "ctx"), None),
            P(("dp", "expert", "ctx"), None),
            P(("dp", "expert", "ctx"), None),
            P(("dp", "expert", "ctx"), None),
            P(("dp", "expert", "ctx"), None),
            P(("dp", "expert", "ctx"), None),
            P(("dp", "expert", "ctx"), None),
            P(("dp", "expert", "ctx")),
            P(("dp", "expert", "ctx")),
            P(("dp", "expert", "ctx")),
            P(("dp", "expert", "ctx")),
            P(("dp", "expert", "ctx"), None),
            P(("dp", "expert", "ctx"), None),
            P(("dp", "expert", "ctx"), None),
            P(("dp", "expert", "ctx"), None),
            P("expert", ("dp", "ctx"), None),
            P("expert", ("dp", "ctx"), None),
            P("expert", ("dp", "ctx"), None),
            P("expert", ("dp", "ctx"), None),
            P("expert", ("dp", "ctx"), None),
            P("expert", ("dp", "ctx"), None),
            P("expert", ("dp", "ctx"), None),
            P("expert", ("dp", "ctx"), None),
        ),
        check_vma=False,
    )
```
